32 devices in a mesh: shock: 8 (over y, x, core), trans: 4 (over z).
Axes of the slice: x: 2, y: 2, z: 4, core: 2. Of those that a mesh axis runs over, the one named last changes fastest.
Arguments:
- positions: float32 [16, 4, 3, 128], P('shock', 'trans'), may hold values from 0.35 to 12.8, as said below
- velocities: float32 [16, 4, 3, 128], P('shock', 'trans'), may hold values from -3 to 3
- features: bfloat16 [16, 4, 576, 128], P('shock', 'trans'), may hold values from -6 to 6
- neighbours: int32 [16, 4, 24, 128], P('shock', 'trans'), may hold values from 0 to 3455, as said below
- counts: int32 [16, 4, 128], P('shock', 'trans'), may hold values from 12 to 24, as said below
- w_first: float32 [64, 8], replicated, may hold values from -2 to 2
- w_second: float32 [192, 64], replicated, may hold values from -0.75 to 0.75
- w_read: float32 [128, 192], replicated, may hold values from -0.4375 to 0.4375
- w_out: float32 [128], replicated, may hold values from -0.5 to 0.5
- fresh_positions: float32 [4, 3, 128], P('trans'), may hold values from 0.35 to 12.8, as said below
- fresh_velocities: float32 [4, 3, 128], P('trans'), may hold values from -3 to 3
Outputs:
- energies: float32 [16, 4, 128], P('shock', 'trans')
- new_positions: float32 [16, 4, 3, 128], P('shock', 'trans')
- new_velocities: float32 [16, 4, 3, 128], P('shock', 'trans')
The draws below stay inside these ranges and needn't reach their ends.
Inputs may be any that keep to these rules, and one draw needn't show every extreme that they name: `positions`: Block-local coordinates of each block's 128 atoms lie near the sites of a body-centred cubic arrangement of 4 x 4 x 4 cells of side 3.3 inside a cube of side 13.2. `fresh_positions`: as for positions. `neighbours`: each code is ((dz + 1) * 9 + (ds + 1) * 3 + (dt + 1)) * 128 + j with ds, dt, dz in -1 .. 1, naming a lattice neighbour of the atom other than itself at a distance between 1.2 and 8.8; codes of an atom are distinct. `counts`: slots at or beyond an atom's count are padding. Every atom of the block rows below 8 has all 24 slots live.
All inputs are finite; a program needn't handle non-finite values.
Results may differ from the reference program's by a relative error of at most 0.0006.
Values may be sent and summed in bfloat16 or wider, within the bound.
No kernel may reach another device: no remote copies, remote signals or barrier semaphores. Data moves between devices by JAX's collectives and lax.ppermute only.
A program may use at most 128 MiB of HBM per device.

```python
import math
import jax
import jax.numpy as jnp
import numpy as np
from jax import lax

CH = 64
COMP = 9
NB = 8
RH = 64
EH = 128
NBR = 24
NSB = 16
NTB = 4


def lattice_sites():
    atom_ids = jnp.arange(128, dtype=jnp.int32)
    basis_bit = atom_ids % 2
    cell_id = atom_ids // 2
    return jnp.stack([2 * (cell_id // 16) + basis_bit, 2 * (cell_id // 4 % 4) + basis_bit, 2 * (cell_id % 4) + basis_bit])


def jittered(key, leading):
    centre = lattice_sites().astype(jnp.float32) * 1.65 + 0.8
    shape = leading + (3, 128)
    jitter = jax.random.uniform(key, shape, jnp.float32, -0.45, 0.45)
    return centre + jitter


def draw_positions(key, part):
    return jittered(jax.random.fold_in(key, 3), (NSB, NTB))


def draw_fresh_positions(key, part):
    return jittered(jax.random.fold_in(key, 5), (NTB,))


def candidate_table():
    found = []
    for step_x in range(-4, 5):
        for step_y in range(-4, 5):
            for step_z in range(-4, 5):
                same = step_x % 2 == step_y % 2 and step_y % 2 == step_z % 2
                square = step_x * step_x + step_y * step_y + step_z * step_z
                if same and 0 < square <= 19:
                    found.append([step_x, step_y, step_z])
    return np.array(found, dtype=np.int32)


def draw_neighbours(key, part):
    table = jnp.asarray(candidate_table())
    total = table.shape[0]
    scores = jax.random.randint(jax.random.fold_in(key, 11), (NSB, NTB, 128, total), 0, 1 << 20) * 128
    scores = scores + jnp.arange(total, dtype=jnp.int32)
    chosen = jnp.argsort(scores, axis=-1, stable=True)[..., :NBR]
    moves = table[chosen]
    sites = lattice_sites().T[None, None, :, None, :]
    target = sites + moves
    block_shift = jnp.floor_divide(target, 8)
    local = target - 8 * block_shift
    parity = local[..., 0] % 2
    cells = (local - parity[..., None]) // 2
    atom_ids = ((cells[..., 0] * 4 + cells[..., 1]) * 4 + cells[..., 2]) * 2 + parity
    codes = ((block_shift[..., 2] + 1) * 9 + (block_shift[..., 0] + 1) * 3 + (block_shift[..., 1] + 1)) * 128 + atom_ids
    return jnp.moveaxis(codes, 3, 2).astype(jnp.int32)


def draw_counts(key, part):
    block_rows = lax.broadcasted_iota(jnp.int32, (NSB, NTB, 128), 0)
    spread = jax.random.randint(jax.random.fold_in(key, 13), (NSB, NTB, 128), NBR // 2, NBR * 3 // 4 + 1)
    return jnp.where(block_rows < NSB // 2, NBR, spread).astype(jnp.int32)


def level_of(rng, extent, cuts, low, largest):
    factor_of = 1.0
    for dim, blocks in cuts:
        steps = jax.random.uniform(jax.random.fold_in(jax.random.fold_in(rng, 6), dim), (blocks,), jnp.float32, low / len(cuts), largest / len(cuts))
        factor_of = factor_of * jnp.repeat(jnp.exp(steps), extent[dim] // blocks).reshape((-1,) + (1,) * (len(extent) - 1 - dim))
    return factor_of


def normal_values(stream_key, shape, scale, most, split=(), held_as=jnp.bfloat16):
    values = jax.random.normal(stream_key, shape, jnp.float32) * scale
    if len(split) > 0:
        values = level_of(stream_key, shape, split, -0.22, 0.18) * values
    return jnp.clip(values, min=-most, max=most).astype(held_as)


def setup_inputs(seed: int = 0) -> dict:
    streams_of = jax.random.split(jax.random.key(seed), 12)
    return {
        "positions": draw_positions(jax.random.fold_in(streams_of[11], 71), 0),
        "velocities": normal_values(streams_of[1], (NSB, NTB, 3, 128), 0.5, 3.0, ((0, 8), (1, 4)), jnp.float32),
        "features": normal_values(streams_of[2], (NSB, NTB, COMP * CH, 128), 1.0, 6.0, ((0, 8), (1, 4))),
        "neighbours": draw_neighbours(jax.random.fold_in(streams_of[11], 71), 0),
        "counts": draw_counts(jax.random.fold_in(streams_of[11], 71), 0),
        "w_first": normal_values(streams_of[5], (RH, NB), NB ** -0.5, 2.0, (), jnp.float32),
        "w_second": normal_values(streams_of[6], (3 * CH, RH), RH ** -0.5, 0.75, (), jnp.float32),
        "w_read": normal_values(streams_of[7], (EH, 3 * CH), (3 * CH) ** -0.5, 0.4375, (), jnp.float32),
        "w_out": normal_values(streams_of[8], (EH,), EH ** -0.5, 0.5, (), jnp.float32),
        "fresh_positions": draw_fresh_positions(jax.random.fold_in(streams_of[11], 71), 0),
        "fresh_velocities": normal_values(streams_of[10], (NTB, 3, 128), 0.5, 3.0, ((0, 4),), jnp.float32),
    }


CUTOFF_RADIUS = 9.5
BLOCK_LENGTH = 13.2
KICK_FACTOR = 4.0
MOVE_FACTOR = 0.5
HIGHEST_MODE = lax.Precision.HIGHEST

def block_energy(window_pos, window_feat, slot_codes, live_count, w_first, w_second, w_read, w_out):
    channels = w_second.shape[0] // 3
    basis_count = w_first.shape[1]
    neighbors = slot_codes.shape[0]
    window_slot = slot_codes % 1152
    image_z = (slot_codes // 1152 - 1).astype(jnp.float32)
    near_block = window_slot // 128
    shock_shift = (near_block // 3 - 1).astype(jnp.float32)
    trans_shift = (near_block % 3 - 1).astype(jnp.float32)
    offsets = jnp.stack([shock_shift, trans_shift, image_z]) * BLOCK_LENGTH
    centre = window_pos[:, 512:640]
    others = jnp.take(window_pos, window_slot, axis=1)
    displace = others + offsets - centre[:, None, :]
    distance = jnp.sqrt(lax.optimization_barrier(jnp.sum(displace * displace, axis=0)))
    heading = displace / distance[None]
    ratio = distance / CUTOFF_RADIUS
    envelope = 1.0 - 28.0 * ratio ** 6 + 48.0 * ratio ** 7 - 21.0 * ratio ** 8
    freqs = math.pi / CUTOFF_RADIUS * jnp.arange(1, basis_count + 1).astype(jnp.float32)
    basis = math.sqrt(2.0 / CUTOFF_RADIUS) * jnp.sin(freqs[:, None, None] * distance[None]) / distance[None]
    slot_rank = lax.broadcasted_iota(jnp.int32, slot_codes.shape, 0)
    live = (slot_rank < live_count[None, :]).astype(jnp.float32)
    hidden = jax.nn.silu(jnp.dot(w_first, basis.reshape(basis_count, -1), precision=HIGHEST_MODE))
    radial = jnp.dot(w_second, hidden, precision=HIGHEST_MODE).reshape(3, channels, neighbors, 128)
    radial = radial * (envelope * live)[None, None]
    unit_x, unit_y, unit_z = (heading[0], heading[1], heading[2])
    root_three = math.sqrt(3.0)
    root_fifteen = math.sqrt(15.0)
    root_five = math.sqrt(5.0)
    harmonics = jnp.stack([jnp.ones_like(unit_x), root_three * unit_x, root_three * unit_y, root_three * unit_z, root_fifteen * unit_x * unit_y, root_fifteen * unit_y * unit_z, 0.5 * root_five * (3.0 * unit_z * unit_z - 1.0), root_fifteen * unit_x * unit_z, 0.5 * root_fifteen * (unit_x * unit_x - unit_y * unit_y)])
    gathered = jnp.take(window_feat, window_slot, axis=1).reshape(9, channels, neighbors, 128).astype(jnp.float32)
    along = jnp.einsum('cna,mna->mca', radial[0] * gathered[0], harmonics, precision=HIGHEST_MODE)
    direct = lax.optimization_barrier(jnp.sum(radial[1][None] * gathered, axis=2))
    vector_dot = lax.optimization_barrier(jnp.sum(gathered[1:4] * harmonics[1:4][:, None], axis=0))
    coupled = lax.optimization_barrier(jnp.sum(radial[2] * vector_dot, axis=1))
    tensor_sum = (along + direct).at[0].add(coupled) / neighbors
    squares = tensor_sum * tensor_sum
    invariants = jnp.concatenate([squares[0], lax.optimization_barrier(jnp.sum(squares[1:4], axis=0)), lax.optimization_barrier(jnp.sum(squares[4:9], axis=0))], axis=0)
    readout = jax.nn.silu(jnp.dot(w_read, invariants, precision=HIGHEST_MODE))
    return jnp.dot(w_out, readout, precision=HIGHEST_MODE)

def take_window(extended, row, col):
    zero = jnp.zeros((), jnp.int32)
    piece = lax.dynamic_slice(extended, (row, col, zero, zero), (3, 3, extended.shape[2], 128))
    return jnp.moveaxis(piece, 2, 0).reshape(extended.shape[2], 1152)

def sweep(pos_ext, feat_ext, neighbours, counts, w_first, w_second, w_read, w_out):
    nrows, ncols = (neighbours.shape[0], neighbours.shape[1])
    zero = jnp.zeros((), jnp.int32)

    def visit(block_id, carry):
        forces, energies = carry
        row = (block_id // ncols).astype(jnp.int32)
        col = (block_id % ncols).astype(jnp.int32)
        window_pos = take_window(pos_ext, row, col)
        window_feat = take_window(feat_ext, row, col)
        slot_codes = lax.dynamic_slice(neighbours, (row, col, zero, zero), (1, 1, neighbours.shape[2], 128))[0, 0]
        live_count = lax.dynamic_slice(counts, (row, col, zero), (1, 1, 128))[0, 0]

        def energy_of(place):
            return block_energy(place, window_feat, slot_codes, live_count, w_first, w_second, w_read, w_out)
        energy, pullback = jax.vjp(energy_of, window_pos)
        grad = pullback(jnp.ones_like(energy))[0]
        piece = jnp.moveaxis(grad.reshape(3, 3, 3, 128), 0, 2)
        current = lax.dynamic_slice(forces, (row, col, zero, zero), (3, 3, 3, 128))
        forces = lax.dynamic_update_slice(forces, current - piece, (row, col, zero, zero))
        energies = lax.dynamic_update_slice(energies, energy[None, None], (row, col, zero))
        return (forces, energies)
    start = (jnp.zeros(pos_ext.shape, jnp.float32), jnp.zeros((nrows, ncols, 128), jnp.float32))
    return lax.fori_loop(0, nrows * ncols, visit, start)

def extend(values):
    wrapped = jnp.concatenate([values[:, -1:], values, values[:, :1]], axis=1)
    return jnp.pad(wrapped, ((1, 1), (0, 0), (0, 0), (0, 0)))

def reference(positions, velocities, features, neighbours, counts, w_first, w_second, w_read, w_out, fresh_positions, fresh_velocities):
    pos_ext = extend(positions)
    feat_ext = extend(features)
    forces_ext, energies = sweep(pos_ext, feat_ext, neighbours, counts, w_first, w_second, w_read, w_out)
    ncols = positions.shape[1]
    inner = forces_ext[1:-1]
    folded = inner[:, 1:ncols + 1]
    folded = folded.at[:, ncols - 1].add(inner[:, 0])
    folded = folded.at[:, 0].add(inner[:, ncols + 1])
    new_vel = velocities + KICK_FACTOR * folded
    moved = positions + MOVE_FACTOR * new_vel
    new_positions = jnp.concatenate([moved[1:], fresh_positions[None]], axis=0)
    new_velocities = jnp.concatenate([new_vel[1:], fresh_velocities[None]], axis=0)
    return (energies, new_positions, new_velocities)
```

```python
import functools
import math

import jax
import jax.numpy as jnp
from jax import lax
from jax.experimental import pallas as pl
from jax.experimental.pallas import tpu as pltpu
from jax.sharding import PartitionSpec as P

CUTOFF_RADIUS = 9.5
BLOCK_LENGTH = 13.2
KICK_FACTOR = 4.0
MOVE_FACTOR = 0.5
F32 = jnp.float32
BF16 = jnp.bfloat16
LANES = 128


def extended_2(x, sides, width, wrap):
    for axis, dim in sides:
        count, length = (lax.axis_size(axis), x.shape[dim])
        up = [(i, (i + 1) % count) for i in range(count if wrap else count - 1)]
        down = [(j, i) for i, j in up]
        last = lax.slice_in_dim(x, length - width, length, axis=dim)
        first = lax.slice_in_dim(x, 0, width, axis=dim)
        before = lax.ppermute(last, axis, up)
        after = lax.ppermute(first, axis, down)
        x = jnp.concatenate([before, x, after], axis=dim)
    return x


def shifted(x, axis, by):
    count = lax.axis_size(axis)
    return lax.ppermute(x, axis, [(i, (i + by) % count) for i in range(count)])


def passed_along(block, axis, distance):
    devices = range(lax.axis_size(axis))
    route = [(i - distance, i) for i in devices if i - distance in devices]
    return lax.ppermute(block, axis, route)


def halves(x):
    hi = x.astype(BF16)
    lo = (x - hi.astype(F32)).astype(BF16)
    return hi, lo


def weight_rows(w):
    hi, lo = halves(w)
    return jnp.concatenate([hi, hi, lo], axis=1)


def value_rows(x):
    hi, lo = halves(x)
    return jnp.concatenate([hi, lo, hi], axis=0)


def dot(a, b):
    return jnp.dot(a, b, preferred_element_type=F32)


def sin_cos_half_turns(t):
    n = jnp.floor(t + 0.5)
    r = t - n
    odd = n - 2.0 * jnp.floor(0.5 * n)
    sign = 1.0 - 2.0 * odd
    x = math.pi * r
    y = x * x
    s = 1.0 + y * (
        -1.0 / 6
        + y
        * (
            1.0 / 120
            + y * (-1.0 / 5040 + y * (1.0 / 362880 + y * (-1.0 / 39916800 + y * (1.0 / 6227020800.0))))
        )
    )
    c = 1.0 + y * (
        -0.5
        + y
        * (
            1.0 / 24
            + y
            * (-1.0 / 720 + y * (1.0 / 40320 + y * (-1.0 / 3628800 + y * (1.0 / 479001600.0))))
        )
    )
    return sign * x * s, sign * c


def kernel(
    rows,
    cols,
    channels,
    slots,
    feat_ref,
    pos_ref,
    codes_ref,
    counts_ref,
    w1_ref,
    w2_ref,
    w2t_ref,
    wr_ref,
    wrt_ref,
    wo_ref,
    en_ref,
    force_ref,
    win,
    onehot,
    near,
    xg,
    wsc,
    qsc,
    geo,
    har,
    acc,
    inv,
    dws,
    dys,
    lhs,
):
    blocks = rows * cols
    pairs = slots // 2
    wide = 2 * LANES
    group = 16
    hidden = qsc.shape[2]
    root3, root5, root15 = math.sqrt(3.0), math.sqrt(5.0), math.sqrt(15.0)

    def geometry(b, _):
        r, c = b // cols, b % cols
        for k in range(9):
            win[b, :, k * LANES : (k + 1) * LANES] = feat_ref[r + k // 3, c + k % 3]
        codes = codes_ref[r, c]
        zq = (codes >= 1152).astype(jnp.int32) + (codes >= 2304).astype(jnp.int32)
        slot = codes - 1152 * zq
        near_block = lax.shift_right_logical(slot, 7)
        atom = slot & 127
        row3 = (near_block >= 3).astype(jnp.int32) + (near_block >= 6).astype(jnp.int32)
        shift_x = (row3 - 1).astype(F32) * BLOCK_LENGTH
        shift_y = (near_block - 3 * row3 - 1).astype(F32) * BLOCK_LENGTH
        shift_z = (zq - 1).astype(F32) * BLOCK_LENGTH
        centre = pos_ref[r + 1, c + 1]
        found = [jnp.zeros((slots, LANES), F32) for _ in range(3)]
        for k in range(9):
            place = pos_ref[r + k // 3, c + k % 3]
            here = near_block == k
            for i in range(3):
                line = jnp.broadcast_to(place[i : i + 1], (slots, LANES))
                value = jnp.take_along_axis(line, atom, axis=1, mode="promise_in_bounds")
                found[i] = jnp.where(here, value, found[i])
        rx = found[0] + shift_x - centre[0:1]
        ry = found[1] + shift_y - centre[1:2]
        rz = found[2] + shift_z - centre[2:3]
        dist = jnp.sqrt(rx * rx + ry * ry + rz * rz)
        recip = 1.0 / dist
        ux, uy, uz = rx * recip, ry * recip, rz * recip
        x = dist * (1.0 / CUTOFF_RADIUS)
        x2 = x * x
        x5 = x2 * x2 * x
        live = lax.broadcasted_iota(jnp.int32, (slots, LANES), 0) < counts_ref[r, c]
        scale = jnp.where(live, 1.0 / slots, 0.0)
        env = (1.0 - x5 * x * (28.0 - x * (48.0 - 21.0 * x))) * scale
        denv = (-168.0 / CUTOFF_RADIUS) * x5 * (1.0 - x * (2.0 - x)) * scale
        geo[b, 0] = dist
        geo[b, 1] = recip
        geo[b, 2] = env
        geo[b, 3] = denv
        geo[b, 4] = ux
        geo[b, 5] = uy
        geo[b, 6] = uz
        geo[b, 7] = atom.astype(F32)
        geo[b, 8] = near_block.astype(F32)
        har[b, 0] = root3 * ux
        har[b, 1] = root3 * uy
        har[b, 2] = root3 * uz
        har[b, 3] = root15 * ux * uy
        har[b, 4] = root15 * uy * uz
        har[b, 5] = 0.5 * root5 * (3.0 * uz * uz - 1.0)
        har[b, 6] = root15 * ux * uz
        har[b, 7] = 0.5 * root15 * (ux * ux - uy * uy)
        acc[b] = jnp.zeros(acc.shape[1:], F32)
        return 0

    lax.fori_loop(0, blocks, geometry, 0)

    def wide_row(b, k, p):
        return jnp.concatenate(
            [geo[b, k, pl.ds(2 * p, 1), :], geo[b, k, pl.ds(2 * p + 1, 1), :]], axis=1
        )

    def forward(step, _):
        b, p = step // pairs, step % pairs
        atom = wide_row(b, 7, p)
        place = wide_row(b, 8, p)
        sub = lax.broadcasted_iota(jnp.int32, (LANES, wide), 0).astype(F32)
        hot = jnp.where(sub == atom, 1.0, 0.0).astype(BF16)
        near[step] = hot
        hot3 = hot.reshape(LANES // 16, 16, wide)
        for k in range(9):
            mask = jnp.broadcast_to(jnp.where(place == k, 1.0, 0.0), (16, wide)).astype(BF16)
            onehot[k * LANES : (k + 1) * LANES, :] = (hot3 * mask[None]).reshape(LANES, wide)
        xg[step] = dot(win[b], onehot[...])
        dist, recip = wide_row(b, 0, p), wide_row(b, 1, p)
        env, denv = wide_row(b, 2, p), wide_row(b, 3, p)
        order = (lax.broadcasted_iota(jnp.int32, (8, wide), 0) + 1).astype(F32)
        sin, cos = sin_cos_half_turns(order * (dist * (1.0 / CUTOFF_RADIUS)))
        norm = math.sqrt(2.0 / CUTOFF_RADIUS)
        basis = norm * sin * recip
        slope = ((norm * math.pi / CUTOFF_RADIUS) * order * cos - basis) * recip
        both = jnp.concatenate([basis, slope], axis=1)
        hi = both.astype(BF16).astype(F32)
        lo = both - hi
        pre2 = dot(w1_ref[...], jnp.concatenate([hi, lo, hi, lo], axis=0).astype(BF16))
        pre, dpre = pre2[:, :wide], pre2[:, wide:]
        gate = 1.0 / (1.0 + jnp.exp(-pre))
        h = pre * gate
        dh = gate + h * (1.0 - gate)
        qsc[step] = dh * dpre * env + h * denv
        wsc[step] = dot(w2_ref[...], value_rows(h * env))
        for g in range(channels // group):
            lo_c = g * group
            total = [acc[b, m, lo_c : lo_c + group, :] for m in range(9)]
            for s in range(2):
                ln = slice(s * LANES, (s + 1) * LANES)
                xs = [
                    xg[step, m * channels + lo_c : m * channels + lo_c + group, ln]
                    for m in range(9)
                ]
                w0, w1, w2 = [
                    wsc[step, k * channels + lo_c : k * channels + lo_c + group, ln]
                    for k in range(3)
                ]
                ys = [har[b, m, pl.ds(2 * p + s, 1), :] for m in range(8)]
                t0 = w0 * xs[0]
                vec = xs[1] * ys[0] + xs[2] * ys[1] + xs[3] * ys[2]
                total[0] = total[0] + (t0 + w1 * xs[0]) + w2 * vec
                for m in range(1, 9):
                    total[m] = total[m] + (t0 * ys[m - 1] + w1 * xs[m])
            for m in range(9):
                acc[b, m, lo_c : lo_c + group, :] = total[m]
        return 0

    lax.fori_loop(0, blocks * pairs, forward, 0)

    for b in range(blocks):
        ln = slice(b * LANES, (b + 1) * LANES)
        a = [acc[b, m] for m in range(9)]
        inv[0:channels, ln] = a[0] * a[0]
        inv[channels : 2 * channels, ln] = a[1] * a[1] + a[2] * a[2] + a[3] * a[3]
        inv[2 * channels :, ln] = (
            a[4] * a[4] + a[5] * a[5] + a[6] * a[6] + a[7] * a[7] + a[8] * a[8]
        )
    z = dot(wr_ref[...], value_rows(inv[...]))
    gate = 1.0 / (1.0 + jnp.exp(-z))
    out = z * gate
    wo = wo_ref[...]
    energy = jnp.sum(out * wo, axis=0, keepdims=True)
    dinv = dot(wrt_ref[...], value_rows(wo * (gate + out * (1.0 - gate))))
    for b in range(blocks):
        ln = slice(b * LANES, (b + 1) * LANES)
        en_ref[b // cols, b % cols] = energy[:, ln]
        for m in range(9):
            part = 0 if m == 0 else (1 if m < 4 else 2)
            d = dinv[part * channels : (part + 1) * channels, ln]
            acc[b, m] = 2.0 * acc[b, m] * d

    def backward(step, _):
        b, p = step // pairs, step % pairs
        for s in range(2):
            ln = slice(s * LANES, (s + 1) * LANES)
            ys = [har[b, m, pl.ds(2 * p + s, 1), :] for m in range(8)]
            dy = [jnp.zeros((group, LANES), F32) for _ in range(8)]
            for g in range(channels // group):
                lo_c = g * group
                xs = [
                    xg[step, m * channels + lo_c : m * channels + lo_c + group, ln]
                    for m in range(9)
                ]
                gs = [acc[b, m, lo_c : lo_c + group, :] for m in range(9)]
                w0 = wsc[step, lo_c : lo_c + group, ln]
                w2 = wsc[step, 2 * channels + lo_c : 2 * channels + lo_c + group, ln]
                t0 = w0 * xs[0]
                t2 = w2 * gs[0]
                vec = xs[1] * ys[0] + xs[2] * ys[1] + xs[3] * ys[2]
                along = gs[0]
                direct = gs[0] * xs[0]
                for m in range(1, 9):
                    along = along + gs[m] * ys[m - 1]
                    direct = direct + gs[m] * xs[m]
                    dy[m - 1] = dy[m - 1] + t0 * gs[m]
                    if m < 4:
                        dy[m - 1] = dy[m - 1] + t2 * xs[m]
                dw = [along * xs[0], direct, gs[0] * vec]
                for k in range(3):
                    hi, lo = halves(dw[k])
                    at = k * channels + lo_c
                    dws[at : at + group, ln] = hi
                    dws[3 * channels + at : 3 * channels + at + group, ln] = lo
                    dws[6 * channels + at : 6 * channels + at + group, ln] = hi
            for m in range(8):
                dys[m, pl.ds(2 * p + s, 1), :] = jnp.sum(dy[m], axis=0, keepdims=True)
        dh = dot(w2t_ref[...], dws[...])
        dd = jnp.sum(dh * qsc[step], axis=0, keepdims=True)
        dys[8, pl.ds(2 * p, 1), :] = dd[:, :LANES]
        dys[8, pl.ds(2 * p + 1, 1), :] = dd[:, LANES:]
        return 0

    force_ref[...] = jnp.zeros(force_ref.shape, F32)

    def pull(b, _):
        lax.fori_loop(b * pairs, (b + 1) * pairs, backward, 0)
        r, c = b // cols, b % cols
        ux, uy, uz, recip = geo[b, 4], geo[b, 5], geo[b, 6], geo[b, 1]
        d1, d2, d3, d4, d5, d6, d7, d8 = [dys[m] for m in range(8)]
        gx = root3 * d1 + root15 * (uy * d4 + uz * d7 + ux * d8)
        gy = root3 * d2 + root15 * (ux * d4 + uz * d5 - uy * d8)
        gz = root3 * d3 + root15 * (uy * d5 + ux * d7) + (3.0 * root5) * uz * d6
        radial = dys[8] - (ux * gx + uy * gy + uz * gz) * recip
        grads = [gx * recip + ux * radial, gy * recip + uy * radial, gz * recip + uz * radial]
        for i in range(3):
            here = jnp.sum(grads[i], axis=0, keepdims=True)
            force_ref[r + 1, c + 1, i : i + 1, :] += here
        split = [halves(g) for g in grads]
        which = lax.broadcasted_iota(jnp.int32, (16, LANES), 0).astype(F32)
        place = geo[b, 8]
        for n in range(slots):
            ln = slice(n * LANES, (n + 1) * LANES)
            hit = which == place[n : n + 1]
            for i in range(3):
                for v in range(2):
                    line = split[i][v][n : n + 1].astype(F32)
                    at = (3 * v + i) * 16
                    lhs[at : at + 16, ln] = jnp.where(hit, line, 0.0).astype(BF16)
        total = jnp.zeros((96, LANES), F32)
        for p in range(pairs):
            total = total + lax.dot_general(
                lhs[:, p * wide : (p + 1) * wide],
                near[b * pairs + p],
                (((1,), (1,)), ((), ())),
                preferred_element_type=F32,
            )
        for i in range(3):
            for k in range(9):
                at = i * 16 + k
                value = total[at : at + 1] + total[48 + at : 49 + at]
                force_ref[r + k // 3, c + k % 3, i : i + 1, :] -= value
        return 0

    lax.fori_loop(0, blocks, pull, 0)


def sweep(pos_ext, feat_ext, neighbours, counts, w_first, w_second, w_read, w_out):
    rows, cols, slots = neighbours.shape[0], neighbours.shape[1], neighbours.shape[2]
    hidden, channels = w_first.shape[0], w_second.shape[0] // 3
    units = w_read.shape[0]
    blocks, pairs = rows * cols, slots // 2
    wide = 2 * LANES
    hi, lo = halves(w_first)
    w1 = jnp.concatenate([hi, hi, lo, lo], axis=1)
    vmem = pl.BlockSpec(memory_space=pltpu.VMEM)
    energies, forces = pl.pallas_call(
        functools.partial(kernel, rows, cols, channels, slots),
        out_shape=(
            jax.ShapeDtypeStruct((rows, cols, 1, LANES), F32),
            jax.ShapeDtypeStruct((rows + 2, cols + 2, 3, LANES), F32),
        ),
        in_specs=[vmem] * 10,
        out_specs=(vmem, vmem),
        scratch_shapes=[
            pltpu.VMEM((blocks, 9 * channels, 9 * LANES), BF16),
            pltpu.VMEM((9 * LANES, wide), BF16),
            pltpu.VMEM((blocks * pairs, LANES, wide), BF16),
            pltpu.VMEM((blocks * pairs, 9 * channels, wide), F32),
            pltpu.VMEM((blocks * pairs, 3 * channels, wide), F32),
            pltpu.VMEM((blocks * pairs, hidden, wide), F32),
            pltpu.VMEM((blocks, 9, slots, LANES), F32),
            pltpu.VMEM((blocks, 8, slots, LANES), F32),
            pltpu.VMEM((blocks, 9, channels, LANES), F32),
            pltpu.VMEM((3 * channels, blocks * LANES), F32),
            pltpu.VMEM((9 * channels, wide), BF16),
            pltpu.VMEM((9, slots, LANES), F32),
            pltpu.VMEM((96, slots * LANES), BF16),
        ],
        compiler_params=pltpu.CompilerParams(vmem_limit_bytes=56 * 1024 * 1024),
        cost_estimate=pl.CostEstimate(
            flops=2 * 9 * channels * 9 * LANES * slots * LANES * blocks,
            bytes_accessed=4 * 1024 * 1024,
            transcendentals=0,
        ),
    )(
        feat_ext,
        pos_ext,
        neighbours,
        counts.reshape(rows, cols, 1, LANES),
        w1,
        weight_rows(w_second),
        weight_rows(w_second.T),
        weight_rows(w_read),
        weight_rows(w_read.T),
        w_out.reshape(units, 1),
    )
    return forces, energies.reshape(rows, cols, LANES)


def local(
    positions,
    velocities,
    features,
    neighbours,
    counts,
    w_first,
    w_second,
    w_read,
    w_out,
    fresh_positions,
    fresh_velocities,
):
    nrows, ncols = (positions.shape[0], positions.shape[1])
    shock_place = lax.axis_index("shock")
    front = lax.axis_size("shock") - 1
    pos_side = extended_2(positions, (("trans", 1),), 1, True)
    pos_ext = extended_2(pos_side, (("shock", 0),), 1, False)
    feat_side = extended_2(features, (("trans", 1),), 1, True)
    feat_ext = extended_2(feat_side, (("shock", 0),), 1, False)
    forces_ext, energies = sweep(
        pos_ext, feat_ext, neighbours, counts, w_first, w_second, w_read, w_out
    )
    from_right = shifted(forces_ext[:, 0], "trans", -1)
    from_left = shifted(forces_ext[:, ncols + 1], "trans", 1)
    folded = forces_ext[:, 1 : ncols + 1]
    folded = folded.at[:, ncols - 1].add(from_right)
    folded = folded.at[:, 0].add(from_left)
    packed = jnp.concatenate([folded[:2], velocities[:1], positions[:1]], axis=0)
    ahead = passed_along(packed, "shock", -1)
    force = folded[2 : nrows + 2]
    force = force.at[nrows - 2].add(ahead[0])
    force = force.at[nrows - 1].add(ahead[1])
    old_vel = jnp.concatenate([velocities[1:], ahead[2:3]], axis=0)
    old_pos = jnp.concatenate([positions[1:], ahead[3:4]], axis=0)
    new_vel = old_vel + KICK_FACTOR * force
    moved = old_pos + MOVE_FACTOR * new_vel
    at_front = shock_place == front
    last_pos = jnp.where(at_front, fresh_positions, moved[nrows - 1])
    last_vel = jnp.where(at_front, fresh_velocities, new_vel[nrows - 1])
    new_positions = jnp.concatenate([moved[: nrows - 1], last_pos[None]], axis=0)
    new_velocities = jnp.concatenate([new_vel[: nrows - 1], last_vel[None]], axis=0)
    return (energies, new_positions, new_velocities)


def solution(mesh):
    return jax.shard_map(
        local,
        mesh=mesh,
        in_specs=(
            P("shock", "trans", None, None),
            P("shock", "trans", None, None),
            P("shock", "trans", None, None),
            P("shock", "trans", None, None),
            P("shock", "trans", None),
            P(),
            P(),
            P(),
            P(),
            P("trans", None, None),
            P("trans", None, None),
        ),
        out_specs=(
            P("shock", "trans", None),
            P("shock", "trans", None, None),
            P("shock", "trans", None, None),
        ),
        check_vma=False,
    )
```

```python
import functools
import math

import jax
import jax.numpy as jnp
from jax import lax
from jax.experimental import pallas as pl
from jax.experimental.pallas import tpu as pltpu
from jax.sharding import PartitionSpec as P

CUTOFF_RADIUS = 9.5
BLOCK_LENGTH = 13.2
KICK_FACTOR = 4.0
MOVE_FACTOR = 0.5
F32 = jnp.float32
BF16 = jnp.bfloat16
LANES = 128
QUAD = 4
EDGE_LIMIT = 16
LOCAL_LIMIT = 16


def shifted(x, axis, by):
    count = lax.axis_size(axis)
    return lax.ppermute(x, axis, [(i, (i + by) % count) for i in range(count)])


def passed_along(block, axis, distance):
    devices = range(lax.axis_size(axis))
    route = [(i - distance, i) for i in devices if i - distance in devices]
    return lax.ppermute(block, axis, route)


def halves(x):
    hi = x.astype(BF16)
    lo = (x - hi.astype(F32)).astype(BF16)
    return hi, lo


def value_rows(x):
    hi, lo = halves(x)
    return jnp.concatenate([hi, lo, hi], axis=0)


def dot(a, b):
    return jnp.dot(a, b, preferred_element_type=F32)


def sin_cos_half_turns(t):
    n = jnp.floor(t + 0.5)
    r = t - n
    odd = n - 2.0 * jnp.floor(0.5 * n)
    sign = 1.0 - 2.0 * odd
    x = math.pi * r
    y = x * x
    s = 1.0 + y * (
        -1.0 / 6
        + y
        * (
            1.0 / 120
            + y * (-1.0 / 5040 + y * (1.0 / 362880 + y * (-1.0 / 39916800 + y * (1.0 / 6227020800.0))))
        )
    )
    c = 1.0 + y * (
        -0.5
        + y
        * (
            1.0 / 24
            + y
            * (-1.0 / 720 + y * (1.0 / 40320 + y * (-1.0 / 3628800 + y * (1.0 / 479001600.0))))
        )
    )
    return sign * x * s, sign * c


def weight_halves(w):
    hi = w.astype(BF16).astype(F32)
    return hi, w - hi


def weight_rows(w):
    hi, lo = weight_halves(w)
    return jnp.concatenate([hi, hi, lo], axis=1).astype(BF16)


def joined(ref, b, k, first, count):
    lines = [ref[b, k, pl.ds(first + s, 1), :] for s in range(count)]
    return jnp.concatenate(lines, axis=1)


def window_hot(near, place, first, count):
    lanes = near.shape[1]
    near3 = near.reshape(LANES // 16, 16, lanes)
    parts = []
    for k in range(count):
        mask = jnp.where(place == (first + k).astype(F32), 1.0, 0.0)
        mask = jnp.broadcast_to(mask, (16, lanes)).astype(BF16)
        parts.append((near3 * mask[None]).reshape(LANES, lanes))
    return parts


def edge_kernel(
    rows,
    cols,
    slots,
    own_ref,
    left_ref,
    right_ref,
    prev_ref,
    next_ref,
    codes_ref,
    counts_ref,
    w1_ref,
    w2_ref,
    wr_ref,
    wo_ref,
    geo,
    har,
    near,
    wsc,
    dsc,
    wrs,
    wrt,
    woc,
    pos_ref,
    w1s,
    w2s,
):
    blocks = rows * cols
    quads = slots // QUAD
    wide = QUAD * LANES
    root3, root5, root15 = math.sqrt(3.0), math.sqrt(5.0), math.sqrt(15.0)

    hi, lo = weight_halves(w1_ref[...].T)
    w1s[...] = jnp.concatenate([hi, hi, lo, lo], axis=1).astype(BF16)
    w2s[...] = weight_rows(w2_ref[...].T)
    wrs[...] = weight_rows(wr_ref[...].T)
    wrt[...] = weight_rows(wr_ref[...])
    units = wo_ref.shape[1]
    one = lax.broadcasted_iota(jnp.int32, (units, units), 0)
    two = lax.broadcasted_iota(jnp.int32, (units, units), 1)
    woc[...] = jnp.sum(jnp.where(one == two, wo_ref[...], 0.0), axis=1, keepdims=True)

    for i in range(3):
        pos_ref[0, :, i, :] = prev_ref[0, i]
        pos_ref[rows + 1, :, i, :] = next_ref[0, i]
        for r in range(rows):
            pos_ref[r + 1, 0:1, i, :] = left_ref[r, i]
            pos_ref[r + 1, cols + 1 :, i, :] = right_ref[r, i]
            pos_ref[r + 1, 1 : cols + 1, i, :] = own_ref[r, i]

    def geometry(b, _):
        r, c = b // cols, b % cols
        codes = codes_ref[r, c]
        zq = (codes >= 1152).astype(jnp.int32) + (codes >= 2304).astype(jnp.int32)
        slot = codes - 1152 * zq
        near_block = lax.shift_right_logical(slot, 7)
        atom = slot & 127
        row3 = (near_block >= 3).astype(jnp.int32) + (near_block >= 6).astype(jnp.int32)
        shift_x = (row3 - 1).astype(F32) * BLOCK_LENGTH
        shift_y = (near_block - 3 * row3 - 1).astype(F32) * BLOCK_LENGTH
        shift_z = (zq - 1).astype(F32) * BLOCK_LENGTH
        centre = pos_ref[r + 1, c + 1]
        found = [jnp.zeros((slots, LANES), F32) for _ in range(3)]
        for k in range(9):
            place = pos_ref[r + k // 3, c + k % 3]
            here = near_block == k
            for i in range(3):
                line = jnp.broadcast_to(place[i : i + 1], (slots, LANES))
                value = jnp.take_along_axis(line, atom, axis=1, mode="promise_in_bounds")
                found[i] = jnp.where(here, value, found[i])
        rx = found[0] + shift_x - centre[0:1]
        ry = found[1] + shift_y - centre[1:2]
        rz = found[2] + shift_z - centre[2:3]
        dist = jnp.sqrt(rx * rx + ry * ry + rz * rz)
        recip = 1.0 / dist
        ux, uy, uz = rx * recip, ry * recip, rz * recip
        x = dist * (1.0 / CUTOFF_RADIUS)
        x2 = x * x
        x5 = x2 * x2 * x
        live = lax.broadcasted_iota(jnp.int32, (slots, LANES), 0) < counts_ref[r, c]
        scale = jnp.where(live, 1.0 / slots, 0.0)
        env = (1.0 - x5 * x * (28.0 - x * (48.0 - 21.0 * x))) * scale
        denv = (-168.0 / CUTOFF_RADIUS) * x5 * (1.0 - x * (2.0 - x)) * scale
        geo[b, 0] = dist
        geo[b, 1] = recip
        geo[b, 2] = env
        geo[b, 3] = denv
        geo[b, 4] = ux
        geo[b, 5] = uy
        geo[b, 6] = uz
        geo[b, 7] = atom.astype(F32)
        geo[b, 8] = near_block.astype(F32)
        har[b, 0] = root3 * ux
        har[b, 1] = root3 * uy
        har[b, 2] = root3 * uz
        har[b, 3] = root15 * ux * uy
        har[b, 4] = root15 * uy * uz
        har[b, 5] = 0.5 * root5 * (3.0 * uz * uz - 1.0)
        har[b, 6] = root15 * ux * uz
        har[b, 7] = 0.5 * root15 * (ux * ux - uy * uy)
        return 0

    lax.fori_loop(0, blocks, geometry, 0)

    def network(step, _):
        b, first = step // quads, (step % quads) * QUAD
        atom = joined(geo, b, 7, first, QUAD)
        sub = lax.broadcasted_iota(jnp.int32, (LANES, wide), 0).astype(F32)
        near[step] = jnp.where(sub == atom, 1.0, 0.0).astype(BF16)
        dist, recip, env, denv = [joined(geo, b, k, first, QUAD) for k in range(4)]
        order = (lax.broadcasted_iota(jnp.int32, (8, wide), 0) + 1).astype(F32)
        sin, cos = sin_cos_half_turns(order * (dist * (1.0 / CUTOFF_RADIUS)))
        norm = math.sqrt(2.0 / CUTOFF_RADIUS)
        basis = norm * sin * recip
        slope = ((norm * math.pi / CUTOFF_RADIUS) * order * cos - basis) * recip
        both = jnp.concatenate([basis, slope], axis=1)
        hi = both.astype(BF16).astype(F32)
        lo = both - hi
        pre2 = dot(w1s[...], jnp.concatenate([hi, lo, hi, lo], axis=0).astype(BF16))
        pre, dpre = pre2[:, :wide], pre2[:, wide:]
        gate = 1.0 / (1.0 + jnp.exp(-pre))
        h = pre * gate
        dh = gate + h * (1.0 - gate)
        wsc[step] = dot(w2s[...], value_rows(h * env))
        dsc[step] = dot(w2s[...], value_rows(dh * dpre * env + h * denv))
        return 0

    lax.fori_loop(0, blocks * quads, network, 0)


def local_kernel(rows, cols, own_ref, left_ref, right_ref, near, geo, out, win, onehot):
    blocks = rows * cols
    steps = near.shape[0]
    quads = steps // blocks
    feats = win.shape[1]
    spans = win.shape[2] // LANES

    def first_slot(r):
        return 3 if (spans == 6 and r == 0) else 0

    def place_block(part, r, c):
        for i in range(max(r - 2, 0), min(r + 1, rows)):
            for j in range(max(c - 2, 0), min(c + 1, cols)):
                k = 3 * (r - i) + (c - j) - first_slot(i)
                win[i * cols + j, :, k * LANES : (k + 1) * LANES] = part

    if spans == 9:
        for c in range(cols):
            win[c, :, : 3 * LANES] = jnp.zeros((feats, 3 * LANES), BF16)
            win[blocks - cols + c, :, 6 * LANES :] = jnp.zeros((feats, 3 * LANES), BF16)
    for r in range(rows):
        place_block(left_ref[r, 0], r + 1, 0)
        place_block(right_ref[r, 0], r + 1, cols + 1)
        for c in range(cols):
            place_block(own_ref[r, c], r + 1, c + 1)

    def body(step, _):
        b, first = step // quads, (step % quads) * QUAD
        k0 = jnp.where(b // cols == 0, 3, 0) if spans == 6 else jnp.int32(0)
        place = joined(geo, b, 8, first, QUAD)
        parts = window_hot(near[step], place, k0, spans)
        for k in range(spans):
            onehot[k * LANES : (k + 1) * LANES, :] = parts[k]
        out[step] = dot(win[b], onehot[...]).astype(BF16)
        return 0

    lax.fori_loop(0, steps, body, 0)


RING = 3


def energy_kernel(
    rows,
    cols,
    channels,
    slots,
    prev_ref,
    next_ref,
    geo,
    har,
    near,
    wrs,
    wrt,
    woc,
    wsc_hbm,
    dsc_hbm,
    xl_hbm,
    en_ref,
    fleft_ref,
    fown_ref,
    fright_ref,
    force_ref,
    win,
    xl,
    xg,
    wsc,
    dsc,
    acc,
    inv,
    dys,
    lhs,
    wsem,
    dsem,
    xsem,
    *,
    stream,
):
    blocks = rows * cols
    quads = slots // QUAD
    steps = blocks * quads
    wide = QUAD * LANES
    group = 8
    root3, root5, root15 = math.sqrt(3.0), math.sqrt(5.0), math.sqrt(15.0)

    def w_copy(step):
        return pltpu.make_async_copy(wsc_hbm.at[step], wsc.at[step], wsem.at[step])

    def d_copy(step):
        return pltpu.make_async_copy(dsc_hbm.at[step], dsc.at[step], dsem.at[step])

    def x_copy(step):
        at = step % RING
        return pltpu.make_async_copy(xl_hbm.at[step], xl.at[at], xsem.at[at])

    if stream:
        for i in range(RING):
            x_copy(i).start()
            w_copy(i).start()
        for i in range(RING, steps):
            w_copy(i).start()
        for i in range(steps):
            d_copy(i).start()
    else:
        wsc, dsc = wsc_hbm, dsc_hbm

    for r in range(rows):
        for c in range(cols):
            b = r * cols + c
            for k in range(3):
                if r == 0:
                    win[b, :, k * LANES : (k + 1) * LANES] = prev_ref[0, c + k]
                elif r == rows - 1:
                    win[b, :, k * LANES : (k + 1) * LANES] = next_ref[0, c + k]
                else:
                    win[b, :, k * LANES : (k + 1) * LANES] = jnp.zeros_like(prev_ref[0, 0])
    acc[...] = jnp.zeros(acc.shape, F32)

    def gather(step):
        b, first = step // quads, (step % quads) * QUAD
        r = b // cols
        k0 = jnp.where(r == 0, 0, jnp.where(r == rows - 1, 6, 9))
        place = joined(geo, b, 8, first, QUAD)
        onehot = jnp.concatenate(window_hot(near[step], place, k0, 3), axis=0)
        if stream:
            x_copy(step).wait()
            xg[step] = xl[step % RING].astype(F32) + dot(win[b], onehot)
        else:
            xg[step] = xl_hbm[step].astype(F32) + dot(win[b], onehot)

    def collect(step):
        b, first = step // quads, (step % quads) * QUAD
        for g in range(channels // group):
            at = g * group
            total = [acc[b, m, at : at + group, :] for m in range(9)]
            for s in range(QUAD):
                ln = slice(s * LANES, (s + 1) * LANES)
                xs = [
                    xg[step, m * channels + at : m * channels + at + group, ln]
                    for m in range(9)
                ]
                w0, w1, w2 = [
                    wsc[step, k * channels + at : k * channels + at + group, ln]
                    for k in range(3)
                ]
                ys = [har[b, m, pl.ds(first + s, 1), :] for m in range(8)]
                t0 = w0 * xs[0]
                vec = xs[1] * ys[0] + xs[2] * ys[1] + xs[3] * ys[2]
                total[0] = total[0] + (t0 + w1 * xs[0]) + w2 * vec
                for m in range(1, 9):
                    total[m] = total[m] + (t0 * ys[m - 1] + w1 * xs[m])
            for m in range(9):
                acc[b, m, at : at + group, :] = total[m]

    def forward(step, _):
        if stream:
            w_copy(step - 1).wait()
        collect(step - 1)
        gather(step)
        if stream:

            @pl.when(step + RING - 1 < steps)
            def _():
                x_copy(step + RING - 1).start()

        return 0

    gather(0)
    lax.fori_loop(1, steps, forward, 0)
    if stream:
        w_copy(steps - 1).wait()
    collect(steps - 1)

    for b in range(blocks):
        ln = slice(b * LANES, (b + 1) * LANES)
        a = [acc[b, m] for m in range(9)]
        inv[0:channels, ln] = a[0] * a[0]
        inv[channels : 2 * channels, ln] = a[1] * a[1] + a[2] * a[2] + a[3] * a[3]
        inv[2 * channels :, ln] = (
            a[4] * a[4] + a[5] * a[5] + a[6] * a[6] + a[7] * a[7] + a[8] * a[8]
        )
    z = dot(wrs[...], value_rows(inv[...]))
    gate = 1.0 / (1.0 + jnp.exp(-z))
    out = z * gate
    wo = woc[...]
    energy = jnp.sum(out * wo, axis=0, keepdims=True)
    dinv = dot(wrt[...], value_rows(wo * (gate + out * (1.0 - gate))))
    for b in range(blocks):
        ln = slice(b * LANES, (b + 1) * LANES)
        en_ref[b // cols, b % cols] = energy[:, ln]
        for m in range(9):
            part = 0 if m == 0 else (1 if m < 4 else 2)
            d = dinv[part * channels : (part + 1) * channels, ln]
            acc[b, m] = 2.0 * acc[b, m] * d

    def backward(step, _):
        b, first = step // quads, (step % quads) * QUAD
        if stream:
            d_copy(step).wait()
        for s in range(QUAD):
            ln = slice(s * LANES, (s + 1) * LANES)
            ys = [har[b, m, pl.ds(first + s, 1), :] for m in range(8)]
            dy = [jnp.zeros((group, LANES), F32) for _ in range(9)]
            for g in range(channels // group):
                at = g * group
                xs = [
                    xg[step, m * channels + at : m * channels + at + group, ln]
                    for m in range(9)
                ]
                gs = [acc[b, m, at : at + group, :] for m in range(9)]
                w0 = wsc[step, at : at + group, ln]
                w2 = wsc[step, 2 * channels + at : 2 * channels + at + group, ln]
                d0, d1, d2 = [
                    dsc[step, k * channels + at : k * channels + at + group, ln]
                    for k in range(3)
                ]
                t0 = w0 * xs[0]
                t2 = w2 * gs[0]
                vec = xs[1] * ys[0] + xs[2] * ys[1] + xs[3] * ys[2]
                along = gs[0]
                direct = gs[0] * xs[0]
                for m in range(1, 9):
                    along = along + gs[m] * ys[m - 1]
                    direct = direct + gs[m] * xs[m]
                    dy[m - 1] = dy[m - 1] + t0 * gs[m]
                    if m < 4:
                        dy[m - 1] = dy[m - 1] + t2 * xs[m]
                dy[8] = dy[8] + (d0 * xs[0] * along + d1 * direct + d2 * gs[0] * vec)
            for m in range(9):
                dys[b, m, pl.ds(first + s, 1), :] = jnp.sum(dy[m], axis=0, keepdims=True)
        return 0

    lax.fori_loop(0, steps, backward, 0)
    force_ref[...] = jnp.zeros(force_ref.shape, F32)

    def pull(b, _):
        r, c = b // cols, b % cols
        ux, uy, uz, recip = geo[b, 4], geo[b, 5], geo[b, 6], geo[b, 1]
        d1, d2, d3, d4, d5, d6, d7, d8 = [dys[b, m] for m in range(8)]
        gx = root3 * d1 + root15 * (uy * d4 + uz * d7 + ux * d8)
        gy = root3 * d2 + root15 * (ux * d4 + uz * d5 - uy * d8)
        gz = root3 * d3 + root15 * (uy * d5 + ux * d7) + (3.0 * root5) * uz * d6
        radial = dys[b, 8] - (ux * gx + uy * gy + uz * gz) * recip
        grads = [gx * recip + ux * radial, gy * recip + uy * radial, gz * recip + uz * radial]
        for i in range(3):
            here = jnp.sum(grads[i], axis=0, keepdims=True)
            force_ref[r + 1, c + 1, i : i + 1, :] += here
        split = [halves(g) for g in grads]
        which = lax.broadcasted_iota(jnp.int32, (16, LANES), 0).astype(F32)
        place = geo[b, 8]
        for n in range(slots):
            ln = slice(n * LANES, (n + 1) * LANES)
            hit = which == place[n : n + 1]
            for i in range(3):
                for v in range(2):
                    line = split[i][v][n : n + 1].astype(F32)
                    at = (3 * v + i) * 16
                    lhs[at : at + 16, ln] = jnp.where(hit, line, 0.0).astype(BF16)
        total = jnp.zeros((96, LANES), F32)
        for p in range(quads):
            total = total + lax.dot_general(
                lhs[:, p * wide : (p + 1) * wide],
                near[b * quads + p],
                (((1,), (1,)), ((), ())),
                preferred_element_type=F32,
            )
        for i in range(3):
            for k in range(9):
                at = i * 16 + k
                value = total[at : at + 1] + total[48 + at : 49 + at]
                force_ref[r + k // 3, c + k % 3, i : i + 1, :] -= value
        return 0

    lax.fori_loop(0, blocks, pull, 0)
    for r in range(rows + 2):
        for i in range(3):
            fleft_ref[r, i] = force_ref[r, 0:1, i, :]
            fright_ref[r, i] = force_ref[r, cols + 1 :, i, :]
            fown_ref[r, i] = force_ref[r, 1 : cols + 1, i, :]


def vmem_call(body, name, ins, out_shape, scratch, limit, flops):
    vmem = pl.BlockSpec(memory_space=pltpu.VMEM)
    return pl.pallas_call(
        body,
        out_shape=out_shape,
        in_specs=ins,
        out_specs=[vmem] * len(out_shape),
        scratch_shapes=scratch,
        compiler_params=pltpu.CompilerParams(vmem_limit_bytes=limit * 1024 * 1024),
        cost_estimate=pl.CostEstimate(flops=flops, bytes_accessed=1024 * 1024, transcendentals=0),
        name=name,
    )


def edge_part(pos, neighbours, counts, w_first, w_second, w_read, w_out):
    rows, cols, slots = neighbours.shape[0], neighbours.shape[1], neighbours.shape[2]
    hidden, basis = w_first.shape
    units, reads = w_read.shape
    weights = w_second.shape[0]
    blocks, steps, wide = rows * cols, rows * cols * slots // QUAD, QUAD * LANES
    vmem = pl.BlockSpec(memory_space=pltpu.VMEM)
    sds = jax.ShapeDtypeStruct
    call = vmem_call(
        functools.partial(edge_kernel, rows, cols, slots),
        "edges",
        [vmem] * 11,
        [
            sds((blocks, 9, slots, LANES), F32),
            sds((blocks, 8, slots, LANES), F32),
            sds((steps, LANES, wide), BF16),
            sds((steps, weights, wide), F32),
            sds((steps, weights, wide), F32),
            sds((units, 3 * reads), BF16),
            sds((reads, 3 * units), BF16),
            sds((units, 1), F32),
        ],
        [
            pltpu.VMEM((rows + 2, cols + 2, 3, LANES), F32),
            pltpu.VMEM((hidden, 4 * basis), BF16),
            pltpu.VMEM((weights, 3 * hidden), BF16),
        ],
        EDGE_LIMIT,
        2 * 6 * 2 * weights * hidden * steps * wide,
    )
    return call(
        *pos,
        neighbours,
        counts.reshape(rows, cols, 1, LANES),
        w_first.T,
        w_second.T,
        w_read.T,
        w_out.reshape(1, units),
    )


def local_part(own, left, right, near, geo):
    rows, cols, feats = own.shape[0], own.shape[1], own.shape[2]
    steps, _, wide = near.shape
    spans = 6 if rows == 2 else 9
    vmem = pl.BlockSpec(memory_space=pltpu.VMEM)
    call = vmem_call(
        functools.partial(local_kernel, rows, cols),
        "local",
        [vmem] * 5,
        [jax.ShapeDtypeStruct((steps, feats, wide), BF16)],
        [
            pltpu.VMEM((rows * cols, feats, spans * LANES), BF16),
            pltpu.VMEM((spans * LANES, wide), BF16),
        ],
        LOCAL_LIMIT,
        2 * feats * spans * LANES * steps * wide,
    )
    return call(own, left, right, near, geo)[0]


def energy_part(before, after, edges, gathered, rows, cols):
    geo, har, near, wsc, dsc, wrs, wrt, woc = edges
    slots = geo.shape[2]
    steps, weights, wide = wsc.shape
    channels, blocks, feats = weights // 3, rows * cols, gathered.shape[1]
    vmem = pl.BlockSpec(memory_space=pltpu.VMEM)
    hbm = pl.BlockSpec(memory_space=pl.ANY)
    sds = jax.ShapeDtypeStruct
    side = sds((rows + 2, 3, 1, LANES), F32)
    stream = blocks > 2
    kept = steps if stream else 1
    call = vmem_call(
        functools.partial(energy_kernel, rows, cols, channels, slots, stream=stream),
        "energy",
        [vmem] * 8 + [hbm if stream else vmem] * 3,
        [sds((rows, cols, 1, LANES), F32), side, sds((rows + 2, 3, cols, LANES), F32), side],
        [
            pltpu.VMEM((rows + 2, cols + 2, 3, LANES), F32),
            pltpu.VMEM((blocks, feats, 3 * LANES), BF16),
            pltpu.VMEM((RING, feats, wide) if stream else (1, 16, LANES), BF16),
            pltpu.VMEM((steps, feats, wide), F32),
            pltpu.VMEM((steps, weights, wide) if stream else (1, 8, LANES), F32),
            pltpu.VMEM((steps, weights, wide) if stream else (1, 8, LANES), F32),
            pltpu.VMEM((blocks, 9, channels, LANES), F32),
            pltpu.VMEM((weights, blocks * LANES), F32),
            pltpu.VMEM((blocks, 9, slots, LANES), F32),
            pltpu.VMEM((96, slots * LANES), BF16),
            pltpu.SemaphoreType.DMA((kept,)),
            pltpu.SemaphoreType.DMA((kept,)),
            pltpu.SemaphoreType.DMA((RING,)),
        ],
        56 if stream else 24,
        2 * feats * 9 * LANES * steps * wide,
    )
    energies, f_left, f_own, f_right = call(
        before, after, geo, har, near, wrs, wrt, woc, wsc, dsc, gathered
    )
    return f_left, f_own, f_right, energies.reshape(rows, cols, LANES)


def local(
    positions,
    velocities,
    features,
    neighbours,
    counts,
    w_first,
    w_second,
    w_read,
    w_out,
    fresh_positions,
    fresh_velocities,
):
    nrows, ncols = (positions.shape[0], positions.shape[1])
    shock_place = lax.axis_index("shock")
    front = lax.axis_size("shock") - 1
    assert nrows >= 2 and neighbours.shape[2] % QUAD == 0

    def sides(x, axis):
        last = lax.slice_in_dim(x, ncols - 1, ncols, axis=axis)
        first = lax.slice_in_dim(x, 0, 1, axis=axis)
        return shifted(last, "trans", 1), shifted(first, "trans", -1)

    def ends(x, left, right, axis):
        last = jnp.concatenate([left[nrows - 1 :], x[nrows - 1 :], right[nrows - 1 :]], axis=axis)
        first = jnp.concatenate([left[:1], x[:1], right[:1]], axis=axis)
        return passed_along(last, "shock", 1), passed_along(first, "shock", -1)

    pos = positions.transpose(0, 2, 1, 3)
    vel = velocities.transpose(0, 2, 1, 3)
    pos_left, pos_right = sides(pos, 2)
    left, right = sides(features, 1)
    pos_before, pos_after = ends(pos, pos_left, pos_right, 2)
    left, right, _, _ = lax.optimization_barrier((left, right, pos_before, pos_after))
    placed = (pos, pos_left, pos_right, pos_before, pos_after)
    edges = edge_part(placed, neighbours, counts, w_first, w_second, w_read, w_out)
    before, after = ends(features, left, right, 1)
    gathered = local_part(features, left, right, edges[2], edges[0])
    f_left, f_own, f_right, energies = energy_part(before, after, edges, gathered, nrows, ncols)
    from_right = shifted(f_left, "trans", -1)
    from_left = shifted(f_right, "trans", 1)
    folded = f_own.at[:, :, ncols - 1].add(from_right[:, :, 0])
    folded = folded.at[:, :, 0].add(from_left[:, :, 0])
    packed = jnp.concatenate([folded[:2], vel[:1], pos[:1]], axis=0)
    ahead = passed_along(packed, "shock", -1)
    force = folded[2 : nrows + 2]
    force = jnp.concatenate([force[: nrows - 2], force[nrows - 2 :] + ahead[:2]], axis=0)
    old_vel = jnp.concatenate([vel[1:], ahead[2:3]], axis=0)
    old_pos = jnp.concatenate([pos[1:], ahead[3:4]], axis=0)
    new_vel = old_vel + KICK_FACTOR * force
    moved = old_pos + MOVE_FACTOR * new_vel
    at_front = shock_place == front
    last_pos = jnp.where(at_front, fresh_positions.transpose(1, 0, 2), moved[nrows - 1])
    last_vel = jnp.where(at_front, fresh_velocities.transpose(1, 0, 2), new_vel[nrows - 1])
    new_positions = jnp.concatenate([moved[: nrows - 1], last_pos[None]], axis=0)
    new_velocities = jnp.concatenate([new_vel[: nrows - 1], last_vel[None]], axis=0)
    return (energies, new_positions.transpose(0, 2, 1, 3), new_velocities.transpose(0, 2, 1, 3))


def solution(mesh):
    return jax.shard_map(
        local,
        mesh=mesh,
        in_specs=(
            P("shock", "trans", None, None),
            P("shock", "trans", None, None),
            P("shock", "trans", None, None),
            P("shock", "trans", None, None),
            P("shock", "trans", None),
            P(),
            P(),
            P(),
            P(),
            P("trans", None, None),
            P("trans", None, None),
        ),
        out_specs=(
            P("shock", "trans", None),
            P("shock", "trans", None, None),
            P("shock", "trans", None, None),
        ),
        check_vma=False,
    )
```

```python
import functools
import math

import jax
import jax.numpy as jnp
from jax import lax
from jax.experimental import pallas as pl
from jax.experimental.pallas import tpu as pltpu
from jax.sharding import PartitionSpec as P

CUTOFF_RADIUS = 9.5
BLOCK_LENGTH = 13.2
KICK_FACTOR = 4.0
MOVE_FACTOR = 0.5
F32 = jnp.float32
BF16 = jnp.bfloat16
LANES = 128
QUAD = 4
UNROLL = 2
EDGE_LIMIT = 16
LOCAL_LIMIT = 16


def shifted(x, axis, by):
    count = lax.axis_size(axis)
    return lax.ppermute(x, axis, [(i, (i + by) % count) for i in range(count)])


def passed_along(block, axis, distance):
    devices = range(lax.axis_size(axis))
    route = [(i - distance, i) for i in devices if i - distance in devices]
    return lax.ppermute(block, axis, route)


def halves(x):
    hi = x.astype(BF16)
    lo = (x - hi.astype(F32)).astype(BF16)
    return hi, lo


def value_rows(x):
    hi, lo = halves(x)
    return jnp.concatenate([hi, lo, hi], axis=0)


def dot(a, b):
    return jnp.dot(a, b, preferred_element_type=F32)


def sin_cos_half_turns(t):
    n = jnp.floor(t + 0.5)
    r = t - n
    odd = n - 2.0 * jnp.floor(0.5 * n)
    sign = 1.0 - 2.0 * odd
    x = math.pi * r
    y = x * x
    s = 1.0 + y * (
        -1.0 / 6
        + y
        * (
            1.0 / 120
            + y * (-1.0 / 5040 + y * (1.0 / 362880 + y * (-1.0 / 39916800 + y * (1.0 / 6227020800.0))))
        )
    )
    c = 1.0 + y * (
        -0.5
        + y
        * (
            1.0 / 24
            + y
            * (-1.0 / 720 + y * (1.0 / 40320 + y * (-1.0 / 3628800 + y * (1.0 / 479001600.0))))
        )
    )
    return sign * x * s, sign * c


def weight_halves(w):
    hi = w.astype(BF16).astype(F32)
    return hi, w - hi


def weight_rows(w):
    hi, lo = weight_halves(w)
    return jnp.concatenate([hi, hi, lo], axis=1).astype(BF16)


def joined(ref, b, k, first, count):
    lines = [ref[b, k, pl.ds(first + s, 1), :] for s in range(count)]
    return jnp.concatenate(lines, axis=1)


def window_hot(near, place, first, count):
    lanes = near.shape[1]
    near3 = near.reshape(LANES // 16, 16, lanes)
    parts = []
    for k in range(count):
        mask = jnp.where(place == (first + k).astype(F32), 1.0, 0.0)
        mask = jnp.broadcast_to(mask, (16, lanes)).astype(BF16)
        parts.append((near3 * mask[None]).reshape(LANES, lanes))
    return parts


def edge_kernel(
    rows,
    cols,
    slots,
    left_ref,
    right_ref,
    prev_ref,
    next_ref,
    own_hbm,
    codes_hbm,
    counts_hbm,
    w1_hbm,
    w2_hbm,
    wr_hbm,
    wo_hbm,
    geo,
    har,
    near,
    wsc,
    dsc,
    wrs,
    wrt,
    woc,
    pos_ref,
    w1s,
    w2s,
    own_ref,
    codes_ref,
    counts_ref,
    w1_ref,
    w2_ref,
    wr_ref,
    wo_ref,
    sems,
):
    blocks = rows * cols
    quads = slots // QUAD
    wide = QUAD * LANES
    root3, root5, root15 = math.sqrt(3.0), math.sqrt(5.0), math.sqrt(15.0)

    sources = [own_hbm, codes_hbm, counts_hbm, w1_hbm, w2_hbm, wr_hbm, wo_hbm]
    places = [own_ref, codes_ref, counts_ref, w1_ref, w2_ref, wr_ref, wo_ref]
    copies = [
        pltpu.make_async_copy(x, y, sems.at[i]) for i, (x, y) in enumerate(zip(sources, places))
    ]
    for copy in copies:
        copy.start()
    for copy in copies:
        copy.wait()

    hi, lo = weight_halves(w1_ref[...].T)
    w1s[...] = jnp.concatenate([hi, hi, lo, lo], axis=1).astype(BF16)
    w2s[...] = weight_rows(w2_ref[...].T)
    wrs[...] = weight_rows(wr_ref[...].T)
    wrt[...] = weight_rows(wr_ref[...])
    units = wo_ref.shape[1]
    one = lax.broadcasted_iota(jnp.int32, (units, units), 0)
    two = lax.broadcasted_iota(jnp.int32, (units, units), 1)
    woc[...] = jnp.sum(jnp.where(one == two, wo_ref[...], 0.0), axis=1, keepdims=True)

    for i in range(3):
        pos_ref[0, :, i, :] = prev_ref[0, i]
        pos_ref[rows + 1, :, i, :] = next_ref[0, i]
        for r in range(rows):
            pos_ref[r + 1, 0:1, i, :] = left_ref[r, i]
            pos_ref[r + 1, cols + 1 :, i, :] = right_ref[r, i]
            pos_ref[r + 1, 1 : cols + 1, i, :] = own_ref[r, i]

    def geometry(b, _):
        r, c = b // cols, b % cols
        codes = codes_ref[r, c]
        zq = (codes >= 1152).astype(jnp.int32) + (codes >= 2304).astype(jnp.int32)
        slot = codes - 1152 * zq
        near_block = lax.shift_right_logical(slot, 7)
        atom = slot & 127
        row3 = (near_block >= 3).astype(jnp.int32) + (near_block >= 6).astype(jnp.int32)
        shift_x = (row3 - 1).astype(F32) * BLOCK_LENGTH
        shift_y = (near_block - 3 * row3 - 1).astype(F32) * BLOCK_LENGTH
        shift_z = (zq - 1).astype(F32) * BLOCK_LENGTH
        centre = pos_ref[r + 1, c + 1]
        found = [jnp.zeros((slots, LANES), F32) for _ in range(3)]
        for k in range(9):
            place = pos_ref[r + k // 3, c + k % 3]
            here = near_block == k
            for i in range(3):
                line = jnp.broadcast_to(place[i : i + 1], (slots, LANES))
                value = jnp.take_along_axis(line, atom, axis=1, mode="promise_in_bounds")
                found[i] = jnp.where(here, value, found[i])
        rx = found[0] + shift_x - centre[0:1]
        ry = found[1] + shift_y - centre[1:2]
        rz = found[2] + shift_z - centre[2:3]
        dist = jnp.sqrt(rx * rx + ry * ry + rz * rz)
        recip = 1.0 / dist
        ux, uy, uz = rx * recip, ry * recip, rz * recip
        x = dist * (1.0 / CUTOFF_RADIUS)
        x2 = x * x
        x5 = x2 * x2 * x
        live = lax.broadcasted_iota(jnp.int32, (slots, LANES), 0) < counts_ref[r, c]
        scale = jnp.where(live, 1.0 / slots, 0.0)
        env = (1.0 - x5 * x * (28.0 - x * (48.0 - 21.0 * x))) * scale
        denv = (-168.0 / CUTOFF_RADIUS) * x5 * (1.0 - x * (2.0 - x)) * scale
        geo[b, 0] = dist
        geo[b, 1] = recip
        geo[b, 2] = env
        geo[b, 3] = denv
        geo[b, 4] = ux
        geo[b, 5] = uy
        geo[b, 6] = uz
        geo[b, 7] = atom.astype(F32)
        geo[b, 8] = near_block.astype(F32)
        har[b, 0] = root3 * ux
        har[b, 1] = root3 * uy
        har[b, 2] = root3 * uz
        har[b, 3] = root15 * ux * uy
        har[b, 4] = root15 * uy * uz
        har[b, 5] = 0.5 * root5 * (3.0 * uz * uz - 1.0)
        har[b, 6] = root15 * ux * uz
        har[b, 7] = 0.5 * root15 * (ux * ux - uy * uy)
        return 0

    lax.fori_loop(0, blocks, geometry, 0)

    def network(step, _):
        b, first = step // quads, (step % quads) * QUAD
        atom = joined(geo, b, 7, first, QUAD)
        sub = lax.broadcasted_iota(jnp.int32, (LANES, wide), 0).astype(F32)
        near[step] = jnp.where(sub == atom, 1.0, 0.0).astype(BF16)
        dist, recip, env, denv = [joined(geo, b, k, first, QUAD) for k in range(4)]
        order = (lax.broadcasted_iota(jnp.int32, (8, wide), 0) + 1).astype(F32)
        sin, cos = sin_cos_half_turns(order * (dist * (1.0 / CUTOFF_RADIUS)))
        norm = math.sqrt(2.0 / CUTOFF_RADIUS)
        basis = norm * sin * recip
        slope = ((norm * math.pi / CUTOFF_RADIUS) * order * cos - basis) * recip
        both = jnp.concatenate([basis, slope], axis=1)
        hi = both.astype(BF16).astype(F32)
        lo = both - hi
        pre2 = dot(w1s[...], jnp.concatenate([hi, lo, hi, lo], axis=0).astype(BF16))
        pre, dpre = pre2[:, :wide], pre2[:, wide:]
        gate = 1.0 / (1.0 + jnp.exp(-pre))
        h = pre * gate
        dh = gate + h * (1.0 - gate)
        wsc[step] = dot(w2s[...], value_rows(h * env))
        dsc[step] = dot(w2s[...], value_rows(dh * dpre * env + h * denv))
        return 0

    lax.fori_loop(0, blocks * quads, network, 0, unroll=UNROLL)


def local_kernel(rows, cols, own_ref, left_ref, right_ref, near, geo, out, win, onehot_even, onehot_odd):
    blocks = rows * cols
    steps = near.shape[0]
    quads = steps // blocks
    feats = win.shape[1]
    spans = win.shape[2] // LANES

    def first_slot(r):
        return 3 if (spans == 6 and r == 0) else 0

    def place_block(part, r, c):
        for i in range(max(r - 2, 0), min(r + 1, rows)):
            for j in range(max(c - 2, 0), min(c + 1, cols)):
                k = 3 * (r - i) + (c - j) - first_slot(i)
                win[i * cols + j, :, k * LANES : (k + 1) * LANES] = part

    if spans == 9:
        for c in range(cols):
            win[c, :, : 3 * LANES] = jnp.zeros((feats, 3 * LANES), BF16)
            win[blocks - cols + c, :, 6 * LANES :] = jnp.zeros((feats, 3 * LANES), BF16)
    for r in range(rows):
        place_block(left_ref[r, 0], r + 1, 0)
        place_block(right_ref[r, 0], r + 1, cols + 1)
        for c in range(cols):
            place_block(own_ref[r, c], r + 1, c + 1)

    def pick(onehot, step):
        b, first = step // quads, (step % quads) * QUAD
        k0 = jnp.where(b // cols == 0, 3, 0) if spans == 6 else jnp.int32(0)
        place = joined(geo, b, 8, first, QUAD)
        parts = window_hot(near[step], place, k0, spans)
        for k in range(spans):
            onehot[k * LANES : (k + 1) * LANES, :] = parts[k]
        out[step] = dot(win[b], onehot[...]).astype(BF16)

    def body(i, _):
        pick(onehot_even, 2 * i)
        pick(onehot_odd, 2 * i + 1)
        return 0

    lax.fori_loop(0, steps // 2, body, 0)


RING = 3


def energy_kernel(
    rows,
    cols,
    channels,
    slots,
    prev_ref,
    next_ref,
    geo,
    har,
    near,
    wrs,
    wrt,
    woc,
    wsc_hbm,
    dsc_hbm,
    xl_hbm,
    en_ref,
    fleft_ref,
    fown_ref,
    fright_ref,
    force_ref,
    win,
    xl,
    xg_even,
    xg_odd,
    wsc,
    dsc,
    acc,
    inv,
    dys,
    lhs,
    wsem,
    dsem,
    xsem,
    *,
    stream,
):
    blocks = rows * cols
    quads = slots // QUAD
    steps = blocks * quads
    wide = QUAD * LANES
    group = 8
    root3, root5, root15 = math.sqrt(3.0), math.sqrt(5.0), math.sqrt(15.0)

    def w_copy(step):
        return pltpu.make_async_copy(wsc_hbm.at[step], wsc.at[step], wsem.at[step])

    def d_copy(step):
        return pltpu.make_async_copy(dsc_hbm.at[step], dsc.at[step], dsem.at[step])

    def x_copy(step):
        at = step % RING
        return pltpu.make_async_copy(xl_hbm.at[step], xl.at[at], xsem.at[at])

    if stream:
        for i in range(RING):
            x_copy(i).start()
            w_copy(i).start()
        for i in range(RING, steps):
            w_copy(i).start()
        for i in range(steps):
            d_copy(i).start()
    else:
        wsc, dsc = wsc_hbm, dsc_hbm

    for r in range(rows):
        for c in range(cols):
            b = r * cols + c
            for k in range(3):
                if r == 0:
                    win[b, :, k * LANES : (k + 1) * LANES] = prev_ref[0, c + k]
                elif r == rows - 1:
                    win[b, :, k * LANES : (k + 1) * LANES] = next_ref[0, c + k]
                else:
                    win[b, :, k * LANES : (k + 1) * LANES] = jnp.zeros_like(prev_ref[0, 0])
    acc[...] = jnp.zeros(acc.shape, F32)

    def gather(xg, step):
        b, first = step // quads, (step % quads) * QUAD
        r = b // cols
        k0 = jnp.where(r == 0, 0, jnp.where(r == rows - 1, 6, 9))
        place = joined(geo, b, 8, first, QUAD)
        onehot = jnp.concatenate(window_hot(near[step], place, k0, 3), axis=0)
        if stream:
            x_copy(step).wait()
            xg[step // 2] = xl[step % RING].astype(F32) + dot(win[b], onehot)
        else:
            xg[step // 2] = xl_hbm[step].astype(F32) + dot(win[b], onehot)

    def collect(xg, step):
        b, first = step // quads, (step % quads) * QUAD
        for g in range(channels // group):
            at = g * group
            total = [acc[b, m, at : at + group, :] for m in range(9)]
            for s in range(QUAD):
                ln = slice(s * LANES, (s + 1) * LANES)
                xs = [
                    xg[step // 2, m * channels + at : m * channels + at + group, ln]
                    for m in range(9)
                ]
                w0, w1, w2 = [
                    wsc[step, k * channels + at : k * channels + at + group, ln]
                    for k in range(3)
                ]
                ys = [har[b, m, pl.ds(first + s, 1), :] for m in range(8)]
                t0 = w0 * xs[0]
                vec = xs[1] * ys[0] + xs[2] * ys[1] + xs[3] * ys[2]
                total[0] = total[0] + (t0 + w1 * xs[0]) + w2 * vec
                for m in range(1, 9):
                    total[m] = total[m] + (t0 * ys[m - 1] + w1 * xs[m])
            for m in range(9):
                acc[b, m, at : at + group, :] = total[m]

    def advance(xg, xg_last, step, last):
        if stream:
            w_copy(step - 1).wait()
        gather(xg, step)
        collect(xg_last, step - 1)
        if stream and not last:

            @pl.when(step + RING - 1 < steps)
            def _():
                x_copy(step + RING - 1).start()

    def forward(i, _):
        advance(xg_even, xg_odd, 2 * i, False)
        advance(xg_odd, xg_even, 2 * i + 1, False)
        return 0

    gather(xg_even, 0)
    advance(xg_odd, xg_even, 1, False)
    lax.fori_loop(1, steps // 2, forward, 0)
    if stream:
        w_copy(steps - 1).wait()
    collect(xg_odd, steps - 1)

    for b in range(blocks):
        ln = slice(b * LANES, (b + 1) * LANES)
        a = [acc[b, m] for m in range(9)]
        inv[0:channels, ln] = a[0] * a[0]
        inv[channels : 2 * channels, ln] = a[1] * a[1] + a[2] * a[2] + a[3] * a[3]
        inv[2 * channels :, ln] = (
            a[4] * a[4] + a[5] * a[5] + a[6] * a[6] + a[7] * a[7] + a[8] * a[8]
        )
    z = dot(wrs[...], value_rows(inv[...]))
    gate = 1.0 / (1.0 + jnp.exp(-z))
    out = z * gate
    wo = woc[...]
    energy = jnp.sum(out * wo, axis=0, keepdims=True)
    dinv = dot(wrt[...], value_rows(wo * (gate + out * (1.0 - gate))))
    for b in range(blocks):
        ln = slice(b * LANES, (b + 1) * LANES)
        en_ref[b // cols, b % cols] = energy[:, ln]
        for m in range(9):
            part = 0 if m == 0 else (1 if m < 4 else 2)
            d = dinv[part * channels : (part + 1) * channels, ln]
            acc[b, m] = 2.0 * acc[b, m] * d

    def edge_terms(xg, step):
        b, first = step // quads, (step % quads) * QUAD
        if stream:
            d_copy(step).wait()
        for s in range(QUAD):
            ln = slice(s * LANES, (s + 1) * LANES)
            ys = [har[b, m, pl.ds(first + s, 1), :] for m in range(8)]
            dy = [jnp.zeros((group, LANES), F32) for _ in range(9)]
            for g in range(channels // group):
                at = g * group
                xs = [
                    xg[step // 2, m * channels + at : m * channels + at + group, ln]
                    for m in range(9)
                ]
                gs = [acc[b, m, at : at + group, :] for m in range(9)]
                w0 = wsc[step, at : at + group, ln]
                w2 = wsc[step, 2 * channels + at : 2 * channels + at + group, ln]
                d0, d1, d2 = [
                    dsc[step, k * channels + at : k * channels + at + group, ln]
                    for k in range(3)
                ]
                t0 = w0 * xs[0]
                t2 = w2 * gs[0]
                vec = xs[1] * ys[0] + xs[2] * ys[1] + xs[3] * ys[2]
                along = gs[0]
                direct = gs[0] * xs[0]
                for m in range(1, 9):
                    along = along + gs[m] * ys[m - 1]
                    direct = direct + gs[m] * xs[m]
                    dy[m - 1] = dy[m - 1] + t0 * gs[m]
                    if m < 4:
                        dy[m - 1] = dy[m - 1] + t2 * xs[m]
                dy[8] = dy[8] + (d0 * xs[0] * along + d1 * direct + d2 * gs[0] * vec)
            for m in range(9):
                dys[b, m, pl.ds(first + s, 1), :] = jnp.sum(dy[m], axis=0, keepdims=True)

    def backward(i, _):
        edge_terms(xg_even, 2 * i)
        edge_terms(xg_odd, 2 * i + 1)
        return 0

    lax.fori_loop(0, steps // 2, backward, 0)
    force_ref[...] = jnp.zeros(force_ref.shape, F32)

    def pull(b, _):
        r, c = b // cols, b % cols
        ux, uy, uz, recip = geo[b, 4], geo[b, 5], geo[b, 6], geo[b, 1]
        d1, d2, d3, d4, d5, d6, d7, d8 = [dys[b, m] for m in range(8)]
        gx = root3 * d1 + root15 * (uy * d4 + uz * d7 + ux * d8)
        gy = root3 * d2 + root15 * (ux * d4 + uz * d5 - uy * d8)
        gz = root3 * d3 + root15 * (uy * d5 + ux * d7) + (3.0 * root5) * uz * d6
        radial = dys[b, 8] - (ux * gx + uy * gy + uz * gz) * recip
        grads = [gx * recip + ux * radial, gy * recip + uy * radial, gz * recip + uz * radial]
        for i in range(3):
            here = jnp.sum(grads[i], axis=0, keepdims=True)
            force_ref[r + 1, c + 1, i : i + 1, :] += here
        split = [halves(g) for g in grads]
        which = lax.broadcasted_iota(jnp.int32, (16, LANES), 0).astype(F32)
        place = geo[b, 8]
        for n in range(slots):
            ln = slice(n * LANES, (n + 1) * LANES)
            hit = which == place[n : n + 1]
            for i in range(3):
                for v in range(2):
                    line = split[i][v][n : n + 1].astype(F32)
                    at = (3 * v + i) * 16
                    lhs[at : at + 16, ln] = jnp.where(hit, line, 0.0).astype(BF16)
        total = jnp.zeros((96, LANES), F32)
        for p in range(quads):
            total = total + lax.dot_general(
                lhs[:, p * wide : (p + 1) * wide],
                near[b * quads + p],
                (((1,), (1,)), ((), ())),
                preferred_element_type=F32,
            )
        for i in range(3):
            for k in range(9):
                at = i * 16 + k
                value = total[at : at + 1] + total[48 + at : 49 + at]
                force_ref[r + k // 3, c + k % 3, i : i + 1, :] -= value
        return 0

    lax.fori_loop(0, blocks, pull, 0)
    for r in range(rows + 2):
        for i in range(3):
            fleft_ref[r, i] = force_ref[r, 0:1, i, :]
            fright_ref[r, i] = force_ref[r, cols + 1 :, i, :]
            fown_ref[r, i] = force_ref[r, 1 : cols + 1, i, :]


def vmem_call(body, name, ins, out_shape, scratch, limit, flops):
    vmem = pl.BlockSpec(memory_space=pltpu.VMEM)
    return pl.pallas_call(
        body,
        out_shape=out_shape,
        in_specs=ins,
        out_specs=[vmem] * len(out_shape),
        scratch_shapes=scratch,
        compiler_params=pltpu.CompilerParams(vmem_limit_bytes=limit * 1024 * 1024),
        cost_estimate=pl.CostEstimate(flops=flops, bytes_accessed=1024 * 1024, transcendentals=0),
        name=name,
    )


def edge_part(pos, neighbours, counts, w_first, w_second, w_read, w_out):
    rows, cols, slots = neighbours.shape[0], neighbours.shape[1], neighbours.shape[2]
    hidden, basis = w_first.shape
    units, reads = w_read.shape
    weights = w_second.shape[0]
    blocks, steps, wide = rows * cols, rows * cols * slots // QUAD, QUAD * LANES
    vmem = pl.BlockSpec(memory_space=pltpu.VMEM)
    hbm = pl.BlockSpec(memory_space=pltpu.HBM)
    sds = jax.ShapeDtypeStruct
    call = vmem_call(
        functools.partial(edge_kernel, rows, cols, slots),
        "edges",
        [vmem] * 4 + [hbm] * 7,
        [
            sds((blocks, 9, slots, LANES), F32),
            sds((blocks, 8, slots, LANES), F32),
            sds((steps, LANES, wide), BF16),
            sds((steps, weights, wide), F32),
            sds((steps, weights, wide), F32),
            sds((units, 3 * reads), BF16),
            sds((reads, 3 * units), BF16),
            sds((units, 1), F32),
        ],
        [
            pltpu.VMEM((rows + 2, cols + 2, 3, LANES), F32),
            pltpu.VMEM((hidden, 4 * basis), BF16),
            pltpu.VMEM((weights, 3 * hidden), BF16),
            pltpu.VMEM((rows, 3, cols, LANES), F32),
            pltpu.VMEM((rows, cols, slots, LANES), jnp.int32),
            pltpu.VMEM((rows, cols, 1, LANES), jnp.int32),
            pltpu.VMEM((basis, hidden), F32),
            pltpu.VMEM((hidden, weights), F32),
            pltpu.VMEM((reads, units), F32),
            pltpu.VMEM((1, units), F32),
            pltpu.SemaphoreType.DMA((7,)),
        ],
        EDGE_LIMIT,
        2 * 6 * 2 * weights * hidden * steps * wide,
    )
    args = [
        pos[0],
        neighbours,
        counts.reshape(rows, cols, 1, LANES),
        w_first.T,
        w_second.T,
        w_read.T,
        w_out.reshape(1, units),
    ]
    return call(*pos[1:], *[pltpu.with_memory_space_constraint(x, pltpu.HBM) for x in args])


def local_part(own, left, right, near, geo):
    rows, cols, feats = own.shape[0], own.shape[1], own.shape[2]
    steps, _, wide = near.shape
    spans = 6 if rows == 2 else 9
    vmem = pl.BlockSpec(memory_space=pltpu.VMEM)
    call = vmem_call(
        functools.partial(local_kernel, rows, cols),
        "local",
        [vmem] * 5,
        [jax.ShapeDtypeStruct((steps, feats, wide), BF16)],
        [
            pltpu.VMEM((rows * cols, feats, spans * LANES), BF16),
            pltpu.VMEM((spans * LANES, wide), BF16),
            pltpu.VMEM((spans * LANES, wide), BF16),
        ],
        LOCAL_LIMIT,
        2 * feats * spans * LANES * steps * wide,
    )
    return call(own, left, right, near, geo)[0]


def energy_part(before, after, edges, gathered, rows, cols):
    geo, har, near, wsc, dsc, wrs, wrt, woc = edges
    slots = geo.shape[2]
    steps, weights, wide = wsc.shape
    channels, blocks, feats = weights // 3, rows * cols, gathered.shape[1]
    vmem = pl.BlockSpec(memory_space=pltpu.VMEM)
    hbm = pl.BlockSpec(memory_space=pl.ANY)
    sds = jax.ShapeDtypeStruct
    side = sds((rows + 2, 3, 1, LANES), F32)
    stream = blocks > 2
    kept = steps if stream else 1
    call = vmem_call(
        functools.partial(energy_kernel, rows, cols, channels, slots, stream=stream),
        "energy",
        [vmem] * 8 + [hbm if stream else vmem] * 3,
        [sds((rows, cols, 1, LANES), F32), side, sds((rows + 2, 3, cols, LANES), F32), side],
        [
            pltpu.VMEM((rows + 2, cols + 2, 3, LANES), F32),
            pltpu.VMEM((blocks, feats, 3 * LANES), BF16),
            pltpu.VMEM((RING, feats, wide) if stream else (1, 16, LANES), BF16),
            pltpu.VMEM((steps // 2, feats, wide), F32),
            pltpu.VMEM((steps // 2, feats, wide), F32),
            pltpu.VMEM((steps, weights, wide) if stream else (1, 8, LANES), F32),
            pltpu.VMEM((steps, weights, wide) if stream else (1, 8, LANES), F32),
            pltpu.VMEM((blocks, 9, channels, LANES), F32),
            pltpu.VMEM((weights, blocks * LANES), F32),
            pltpu.VMEM((blocks, 9, slots, LANES), F32),
            pltpu.VMEM((96, slots * LANES), BF16),
            pltpu.SemaphoreType.DMA((kept,)),
            pltpu.SemaphoreType.DMA((kept,)),
            pltpu.SemaphoreType.DMA((RING,)),
        ],
        56 if stream else 24,
        2 * feats * 9 * LANES * steps * wide,
    )
    energies, f_left, f_own, f_right = call(
        before, after, geo, har, near, wrs, wrt, woc, wsc, dsc, gathered
    )
    return f_left, f_own, f_right, energies.reshape(rows, cols, LANES)


def local(
    positions,
    velocities,
    features,
    neighbours,
    counts,
    w_first,
    w_second,
    w_read,
    w_out,
    fresh_positions,
    fresh_velocities,
):
    nrows, ncols = (positions.shape[0], positions.shape[1])
    shock_place = lax.axis_index("shock")
    front = lax.axis_size("shock") - 1
    assert nrows >= 2 and neighbours.shape[2] % (2 * QUAD) == 0

    def sides(x, axis):
        last = lax.slice_in_dim(x, ncols - 1, ncols, axis=axis)
        first = lax.slice_in_dim(x, 0, 1, axis=axis)
        return shifted(last, "trans", 1), shifted(first, "trans", -1)

    def ends(x, left, right, axis):
        last = jnp.concatenate([left[nrows - 1 :], x[nrows - 1 :], right[nrows - 1 :]], axis=axis)
        first = jnp.concatenate([left[:1], x[:1], right[:1]], axis=axis)
        return passed_along(last, "shock", 1), passed_along(first, "shock", -1)

    pos = positions.transpose(0, 2, 1, 3)
    vel = velocities.transpose(0, 2, 1, 3)
    pos_left, pos_right = sides(pos, 2)
    left, right = sides(features, 1)
    pos_before, pos_after = ends(pos, pos_left, pos_right, 2)
    left, right, _, _ = lax.optimization_barrier((left, right, pos_before, pos_after))
    placed = (pos, pos_left, pos_right, pos_before, pos_after)
    edges = edge_part(placed, neighbours, counts, w_first, w_second, w_read, w_out)
    before, after = ends(features, left, right, 1)
    gathered = local_part(features, left, right, edges[2], edges[0])
    f_left, f_own, f_right, energies = energy_part(before, after, edges, gathered, nrows, ncols)
    from_right = shifted(f_left, "trans", -1)
    from_left = shifted(f_right, "trans", 1)
    folded = f_own.at[:, :, ncols - 1].add(from_right[:, :, 0])
    folded = folded.at[:, :, 0].add(from_left[:, :, 0])
    packed = jnp.concatenate([folded[:2], vel[:1], pos[:1]], axis=0)
    ahead = passed_along(packed, "shock", -1)
    force = folded[2 : nrows + 2]
    force = jnp.concatenate([force[: nrows - 2], force[nrows - 2 :] + ahead[:2]], axis=0)
    old_vel = jnp.concatenate([vel[1:], ahead[2:3]], axis=0)
    old_pos = jnp.concatenate([pos[1:], ahead[3:4]], axis=0)
    new_vel = old_vel + KICK_FACTOR * force
    moved = old_pos + MOVE_FACTOR * new_vel
    at_front = shock_place == front
    last_pos = jnp.where(at_front, fresh_positions.transpose(1, 0, 2), moved[nrows - 1])
    last_vel = jnp.where(at_front, fresh_velocities.transpose(1, 0, 2), new_vel[nrows - 1])
    new_positions = jnp.concatenate([moved[: nrows - 1], last_pos[None]], axis=0)
    new_velocities = jnp.concatenate([new_vel[: nrows - 1], last_vel[None]], axis=0)
    return (energies, new_positions.transpose(0, 2, 1, 3), new_velocities.transpose(0, 2, 1, 3))


def solution(mesh):
    return jax.shard_map(
        local,
        mesh=mesh,
        in_specs=(
            P("shock", "trans", None, None),
            P("shock", "trans", None, None),
            P("shock", "trans", None, None),
            P("shock", "trans", None, None),
            P("shock", "trans", None),
            P(),
            P(),
            P(),
            P(),
            P("trans", None, None),
            P("trans", None, None),
        ),
        out_specs=(
            P("shock", "trans", None),
            P("shock", "trans", None, None),
            P("shock", "trans", None, None),
        ),
        check_vma=False,
    )
```

```python
import functools
import math

import jax
import jax.numpy as jnp
from jax import lax
from jax.experimental import pallas as pl
from jax.experimental.pallas import tpu as pltpu
from jax.sharding import PartitionSpec as P

CUTOFF_RADIUS = 9.5
BLOCK_LENGTH = 13.2
KICK_FACTOR = 4.0
MOVE_FACTOR = 0.5
F32 = jnp.float32
BF16 = jnp.bfloat16
LANES = 128
QUAD = 4


def shifted(x, axis, by):
    count = lax.axis_size(axis)
    return lax.ppermute(x, axis, [(i, (i + by) % count) for i in range(count)])


def passed_along(block, axis, distance):
    devices = range(lax.axis_size(axis))
    route = [(i - distance, i) for i in devices if i - distance in devices]
    return lax.ppermute(block, axis, route)


def halves(x):
    hi = x.astype(BF16)
    lo = (x - hi.astype(F32)).astype(BF16)
    return hi, lo


def value_rows(x):
    hi, lo = halves(x)
    return jnp.concatenate([hi, lo, hi], axis=0)


def dot(a, b):
    return jnp.dot(a, b, preferred_element_type=F32)


def sin_cos_half_turns(t):
    n = jnp.floor(t + 0.5)
    r = t - n
    odd = n - 2.0 * jnp.floor(0.5 * n)
    sign = 1.0 - 2.0 * odd
    x = math.pi * r
    y = x * x
    s = 1.0 + y * (
        -1.0 / 6
        + y
        * (
            1.0 / 120
            + y * (-1.0 / 5040 + y * (1.0 / 362880 + y * (-1.0 / 39916800 + y * (1.0 / 6227020800.0))))
        )
    )
    c = 1.0 + y * (
        -0.5
        + y
        * (
            1.0 / 24
            + y
            * (-1.0 / 720 + y * (1.0 / 40320 + y * (-1.0 / 3628800 + y * (1.0 / 479001600.0))))
        )
    )
    return sign * x * s, sign * c


def weight_halves(w):
    hi = w.astype(BF16).astype(F32)
    return hi, w - hi


def weight_rows(w):
    hi, lo = weight_halves(w)
    return jnp.concatenate([hi, hi, lo], axis=1).astype(BF16)


def joined(ref, b, k, first, count):
    lines = [ref[b, k, pl.ds(first + s, 1), :] for s in range(count)]
    return jnp.concatenate(lines, axis=1)


def lines(ref, b, first, count):
    return jnp.concatenate([ref[b, pl.ds(first + s, 1), :] for s in range(count)], axis=1)


def first_row(rows, r):
    return 1 if (rows == 2 and r == 0) else 0


def window_hot(near, place, wanted):
    lanes = near.shape[1]
    near3 = near.reshape(LANES // 16, 16, lanes)
    parts = []
    for k in wanted:
        mask = jnp.where(place == jnp.asarray(k).astype(F32), 1.0, 0.0)
        mask = jnp.broadcast_to(mask, (16, lanes)).astype(BF16)
        parts.append((near3 * mask[None]).reshape(LANES, lanes))
    return parts


def decoded(codes):
    zq = (codes >= 1152).astype(jnp.int32) + (codes >= 2304).astype(jnp.int32)
    slot = codes - 1152 * zq
    return zq, lax.shift_right_logical(slot, 7), slot & 127


def copied(sources, places, sems):
    copies = [
        pltpu.make_async_copy(x, y, sems.at[i]) for i, (x, y) in enumerate(zip(sources, places))
    ]
    for copy in copies:
        copy.start()
    return copies


def prepare_kernel(
    rows,
    cols,
    slots,
    own_ref,
    codes_hbm,
    w1_hbm,
    w2_hbm,
    wr_hbm,
    wo_hbm,
    near,
    place,
    w1s,
    w2s,
    wrs,
    wrt,
    woc,
    out,
    codes_ref,
    w1_ref,
    w2_ref,
    wr_ref,
    wo_ref,
    atoms,
    win,
    onehot_even,
    onehot_odd,
    sems,
):
    blocks = rows * cols
    quads = slots // QUAD
    wide = QUAD * LANES
    spans = win.shape[2] // LANES
    copies = copied(
        [codes_hbm, w1_hbm, w2_hbm, wr_hbm, wo_hbm],
        [codes_ref, w1_ref, w2_ref, wr_ref, wo_ref],
        sems,
    )
    copies[0].wait()
    for r in range(rows):
        for c in range(cols):
            _, block, atom = decoded(codes_ref[r, c])
            place[r * cols + c] = block.astype(F32)
            atoms[r * cols + c] = atom.astype(F32)
    feats = win.shape[1]
    for r in range(rows):
        first = first_row(rows, r)
        for c in range(cols):
            for k in range(spans):
                ln = slice(k * LANES, (k + 1) * LANES)
                if 0 <= r - 1 + first + k < rows:
                    win[r * cols + c, :, ln] = own_ref[r - 1 + first + k, c, :feats]
                else:
                    win[r * cols + c, :, ln] = jnp.zeros((feats, LANES), BF16)

    def pick(onehot, step):
        b, at = step // quads, (step % quads) * QUAD
        atom = lines(atoms, b, at, QUAD)
        sub = lax.broadcasted_iota(jnp.int32, (LANES, wide), 0).astype(F32)
        hot = jnp.where(sub == atom, 1.0, 0.0).astype(BF16)
        near[step] = hot
        first = jnp.where(b // cols == 0, first_row(rows, 0), 0)
        wanted = [3 * (first + k) + 1 for k in range(spans)]
        parts = window_hot(hot, lines(place, b, at, QUAD), wanted)
        for k in range(spans):
            onehot[k * LANES : (k + 1) * LANES, :] = parts[k]
        out[step] = dot(win[b], onehot[...]).astype(BF16)

    def body(i, _):
        pick(onehot_even, 2 * i)
        pick(onehot_odd, 2 * i + 1)
        return 0

    lax.fori_loop(0, blocks * quads // 2, body, 0)

    for copy in copies[1:]:
        copy.wait()
    hi, lo = weight_halves(w1_ref[...].T)
    line = jnp.concatenate([hi, hi, lo, lo], axis=1)
    none = jnp.zeros_like(line)
    w1s[...] = jnp.concatenate(
        [jnp.concatenate([line, none], axis=1), jnp.concatenate([none, line], axis=1)], axis=0
    ).astype(BF16)
    w2s[...] = weight_rows(w2_ref[...].T)
    wrs[...] = weight_rows(wr_ref[...].T)
    wrt[...] = weight_rows(wr_ref[...])
    units = wo_ref.shape[1]
    one = lax.broadcasted_iota(jnp.int32, (units, units), 0)
    two = lax.broadcasted_iota(jnp.int32, (units, units), 1)
    woc[...] = jnp.sum(jnp.where(one == two, wo_ref[...], 0.0), axis=1, keepdims=True)


def pack_kernel(rows, cols, feat_hbm, pos_hbm, out, pos_ref, sems):
    feats = feat_hbm.shape[2]
    copies = copied(
        [pos_hbm] + [feat_hbm.at[r, c] for r in range(rows) for c in range(cols)],
        [pos_ref] + [out.at[r, c, pl.ds(0, feats)] for r in range(rows) for c in range(cols)],
        sems,
    )
    copies[0].wait()
    for r in range(rows):
        for c in range(cols):
            rest = jnp.concatenate([pos_ref[r, i, c : c + 1, :] for i in range(3)], axis=0)
            parts = []
            for _ in range(3):
                part = rest.astype(BF16).astype(F32)
                parts.append(part)
                rest = rest - part
            parts.append(jnp.zeros((7, LANES), F32))
            out[r, c, feats:] = jnp.concatenate(parts, axis=0).astype(BF16)
    for copy in copies[1:]:
        copy.wait()


def place_of(block, feats):
    rest = block[feats : feats + 16].astype(F32)
    return rest[0:3] + rest[3:6] + rest[6:9]


def ends_kernel(rows, left_ref, right_ref, up, down):
    for out, r in ((up, rows - 1), (down, 0)):
        out[:, :LANES] = left_ref[r, 0]
        out[:, LANES:] = right_ref[r, 0]


def local_kernel(
    rows,
    cols,
    prev_ref,
    next_ref,
    left_ref,
    right_ref,
    own_ref,
    near,
    place,
    xa,
    out,
    win,
    hot_even,
    hot_odd,
):
    blocks = rows * cols
    steps = near.shape[0]
    quads = steps // blocks
    feats = out.shape[1]

    def columns(r, c):
        found = []
        for k in range(3):
            row = r - 1 + k
            for col in (c - 1, c, c + 1):
                slot = 3 * k + col - c + 1
                if 0 <= row < rows and col != c:
                    if col < 0:
                        found.append((slot, left_ref[row, 0, :feats]))
                    elif col >= cols:
                        found.append((slot, right_ref[row, 0, :feats]))
                    else:
                        found.append((slot, own_ref[row, col, :feats]))
                elif not 0 <= row < rows and 0 <= col < cols:
                    ref = prev_ref if row < 0 else next_ref
                    found.append((slot, ref[0, col, :feats]))
        return found

    for b in range(blocks):
        found = columns(b // cols, b % cols)
        count = len(found)
        for k, (_, block) in enumerate(found):
            win[b, :, k * LANES : (k + 1) * LANES] = block

        def pick(hot, step):
            first = (step % quads) * QUAD
            parts = window_hot(near[step], lines(place, b, first, QUAD), [x for x, _ in found])
            for k in range(count):
                hot[k * LANES : (k + 1) * LANES, :] = parts[k]
            picked = dot(win[b, :, : count * LANES], hot[: count * LANES, :])
            out[step] = xa[step] + picked.astype(BF16)

        def body(i, _):
            pick(hot_even, b * quads + 2 * i)
            pick(hot_odd, b * quads + 2 * i + 1)
            return 0

        lax.fori_loop(0, quads // 2, body, 0)


RING = 3


def energy_kernel(
    rows,
    cols,
    channels,
    slots,
    prev_ref,
    next_ref,
    prev_own_ref,
    next_own_ref,
    own_ref,
    left_ref,
    right_ref,
    codes_hbm,
    counts_hbm,
    near,
    w1s,
    w2s,
    wrs,
    wrt,
    woc,
    xl_hbm,
    en_ref,
    fleft_ref,
    fown_ref,
    fright_ref,
    force_ref,
    pos_ref,
    codes_ref,
    counts_ref,
    geo,
    har,
    win,
    xl,
    xg_even,
    xg_odd,
    w_even,
    w_odd,
    d_even,
    d_odd,
    acc,
    inv,
    dys,
    lhs,
    sems,
    xsem,
    *,
    stream,
):
    blocks = rows * cols
    quads = slots // QUAD
    steps = blocks * quads
    wide = QUAD * LANES
    group = 8
    feats = 9 * channels
    root3, root5, root15 = math.sqrt(3.0), math.sqrt(5.0), math.sqrt(15.0)
    even, odd = (xg_even, w_even, d_even), (xg_odd, w_odd, d_odd)

    def x_copy(step):
        at = step % RING
        return pltpu.make_async_copy(xl_hbm.at[step], xl.at[at], xsem.at[at])

    copies = copied([codes_hbm, counts_hbm], [codes_ref, counts_ref], sems)
    if stream:
        for i in range(RING):
            x_copy(i).start()

    for side, middle, r in ((prev_ref, prev_own_ref, 0), (next_ref, next_own_ref, rows + 1)):
        pos_ref[r, 0] = place_of(side[:, :LANES], feats)
        pos_ref[r, cols + 1] = place_of(side[:, LANES:], feats)
        for c in range(cols):
            pos_ref[r, c + 1] = place_of(middle[0, c], feats)
    for r in range(rows):
        pos_ref[r + 1, 0] = place_of(left_ref[r, 0], feats)
        pos_ref[r + 1, cols + 1] = place_of(right_ref[r, 0], feats)
        for c in range(cols):
            pos_ref[r + 1, c + 1] = place_of(own_ref[r, c], feats)
            none = jnp.zeros((feats, LANES), BF16)
            ref = prev_ref if r == 0 else next_ref
            ends = r == 0 or r == rows - 1
            b = r * cols + c
            win[b, :, :LANES] = ref[:feats, :LANES] if ends and c == 0 else none
            win[b, :, LANES:] = ref[:feats, LANES:] if ends and c == cols - 1 else none
    acc[...] = jnp.zeros(acc.shape, F32)
    for copy in copies:
        copy.wait()

    def geometry(b, _):
        r, c = b // cols, b % cols
        zq, near_block, atom = decoded(codes_ref[r, c])
        row3 = (near_block >= 3).astype(jnp.int32) + (near_block >= 6).astype(jnp.int32)
        shift_x = (row3 - 1).astype(F32) * BLOCK_LENGTH
        shift_y = (near_block - 3 * row3 - 1).astype(F32) * BLOCK_LENGTH
        shift_z = (zq - 1).astype(F32) * BLOCK_LENGTH
        centre = pos_ref[r + 1, c + 1]
        found = [jnp.zeros((slots, LANES), F32) for _ in range(3)]
        for k in range(9):
            place = pos_ref[r + k // 3, c + k % 3]
            here = near_block == k
            for i in range(3):
                line = jnp.broadcast_to(place[i : i + 1], (slots, LANES))
                value = jnp.take_along_axis(line, atom, axis=1, mode="promise_in_bounds")
                found[i] = jnp.where(here, value, found[i])
        rx = found[0] + shift_x - centre[0:1]
        ry = found[1] + shift_y - centre[1:2]
        rz = found[2] + shift_z - centre[2:3]
        dist = jnp.sqrt(rx * rx + ry * ry + rz * rz)
        recip = 1.0 / dist
        ux, uy, uz = rx * recip, ry * recip, rz * recip
        x = dist * (1.0 / CUTOFF_RADIUS)
        x2 = x * x
        x5 = x2 * x2 * x
        live = lax.broadcasted_iota(jnp.int32, (slots, LANES), 0) < counts_ref[r, c]
        scale = jnp.where(live, 1.0 / slots, 0.0)
        env = (1.0 - x5 * x * (28.0 - x * (48.0 - 21.0 * x))) * scale
        denv = (-168.0 / CUTOFF_RADIUS) * x5 * (1.0 - x * (2.0 - x)) * scale
        geo[b, 0] = dist
        geo[b, 1] = recip
        geo[b, 2] = env
        geo[b, 3] = denv
        geo[b, 4] = ux
        geo[b, 5] = uy
        geo[b, 6] = uz
        geo[b, 7] = near_block.astype(F32)
        har[b, 0] = root3 * ux
        har[b, 1] = root3 * uy
        har[b, 2] = root3 * uz
        har[b, 3] = root15 * ux * uy
        har[b, 4] = root15 * uy * uz
        har[b, 5] = 0.5 * root5 * (3.0 * uz * uz - 1.0)
        har[b, 6] = root15 * ux * uz
        har[b, 7] = 0.5 * root15 * (ux * ux - uy * uy)
        return 0

    lax.fori_loop(0, blocks, geometry, 0)

    def network(buffers, step):
        _, wsc, dsc = buffers
        b, first = step // quads, (step % quads) * QUAD
        dist, recip, env, denv = [joined(geo, b, k, first, QUAD) for k in range(4)]
        order = (lax.broadcasted_iota(jnp.int32, (8, wide), 0) + 1).astype(F32)
        sin, cos = sin_cos_half_turns(order * (dist * (1.0 / CUTOFF_RADIUS)))
        norm = math.sqrt(2.0 / CUTOFF_RADIUS)
        basis = norm * sin * recip
        slope = ((norm * math.pi / CUTOFF_RADIUS) * order * cos - basis) * recip
        split = []
        for x in (basis, slope):
            hi = x.astype(BF16).astype(F32)
            split += [hi, x - hi] * 2
        pre2 = dot(w1s[...], jnp.concatenate(split, axis=0).astype(BF16))
        pre, dpre = pre2[: pre2.shape[0] // 2], pre2[pre2.shape[0] // 2 :]
        gate = 1.0 / (1.0 + jnp.exp(-pre))
        h = pre * gate
        dh = gate + h * (1.0 - gate)
        wsc[step // 2] = dot(w2s[...], value_rows(h * env))
        dsc[step // 2] = dot(w2s[...], value_rows(dh * dpre * env + h * denv))

    def gather(buffers, step):
        b, first = step // quads, (step % quads) * QUAD
        r = b // cols
        k0 = jnp.where(r == 0, 0, jnp.where(r == rows - 1, 6, 9))
        parts = window_hot(near[step], joined(geo, b, 7, first, QUAD), [k0, k0 + 2])
        if stream:
            x_copy(step).wait()
            held = xl[step % RING]
        else:
            held = xl_hbm[step]
        buffers[0][step // 2] = held.astype(F32) + dot(win[b], jnp.concatenate(parts, axis=0))

    def collect(buffers, step):
        xg, wsc, _ = buffers
        b, first = step // quads, (step % quads) * QUAD
        for g in range(channels // group):
            at = g * group
            total = [acc[b, m, at : at + group, :] for m in range(9)]
            for s in range(QUAD):
                ln = slice(s * LANES, (s + 1) * LANES)
                xs = [
                    xg[step // 2, m * channels + at : m * channels + at + group, ln]
                    for m in range(9)
                ]
                w0, w1, w2 = [
                    wsc[step // 2, k * channels + at : k * channels + at + group, ln]
                    for k in range(3)
                ]
                ys = [har[b, m, pl.ds(first + s, 1), :] for m in range(8)]
                t0 = w0 * xs[0]
                vec = xs[1] * ys[0] + xs[2] * ys[1] + xs[3] * ys[2]
                total[0] = total[0] + (t0 + w1 * xs[0]) + w2 * vec
                for m in range(1, 9):
                    total[m] = total[m] + (t0 * ys[m - 1] + w1 * xs[m])
            for m in range(9):
                acc[b, m, at : at + group, :] = total[m]

    def advance(new, old, step):
        gather(new, step)
        network(new, step)
        collect(old, step - 1)
        if stream:

            @pl.when(step + RING - 1 < steps)
            def _():
                x_copy(step + RING - 1).start()

    def forward(i, _):
        advance(even, odd, 2 * i)
        advance(odd, even, 2 * i + 1)
        return 0

    gather(even, 0)
    network(even, 0)
    advance(odd, even, 1)
    lax.fori_loop(1, steps // 2, forward, 0)
    collect(odd, steps - 1)

    for b in range(blocks):
        ln = slice(b * LANES, (b + 1) * LANES)
        a = [acc[b, m] for m in range(9)]
        inv[0:channels, ln] = a[0] * a[0]
        inv[channels : 2 * channels, ln] = a[1] * a[1] + a[2] * a[2] + a[3] * a[3]
        inv[2 * channels :, ln] = (
            a[4] * a[4] + a[5] * a[5] + a[6] * a[6] + a[7] * a[7] + a[8] * a[8]
        )
    z = dot(wrs[...], value_rows(inv[...]))
    gate = 1.0 / (1.0 + jnp.exp(-z))
    out = z * gate
    wo = woc[...]
    energy = jnp.sum(out * wo, axis=0, keepdims=True)
    dinv = dot(wrt[...], value_rows(wo * (gate + out * (1.0 - gate))))
    for b in range(blocks):
        ln = slice(b * LANES, (b + 1) * LANES)
        en_ref[b // cols, b % cols] = energy[:, ln]
        for m in range(9):
            part = 0 if m == 0 else (1 if m < 4 else 2)
            d = dinv[part * channels : (part + 1) * channels, ln]
            acc[b, m] = 2.0 * acc[b, m] * d

    def edge_terms(buffers, step):
        xg, wsc, dsc = buffers
        b, first = step // quads, (step % quads) * QUAD
        for s in range(QUAD):
            ln = slice(s * LANES, (s + 1) * LANES)
            ys = [har[b, m, pl.ds(first + s, 1), :] for m in range(8)]
            dy = [jnp.zeros((group, LANES), F32) for _ in range(9)]
            for g in range(channels // group):
                at = g * group
                xs = [
                    xg[step // 2, m * channels + at : m * channels + at + group, ln]
                    for m in range(9)
                ]
                gs = [acc[b, m, at : at + group, :] for m in range(9)]
                w0 = wsc[step // 2, at : at + group, ln]
                w2 = wsc[step // 2, 2 * channels + at : 2 * channels + at + group, ln]
                d0, d1, d2 = [
                    dsc[step // 2, k * channels + at : k * channels + at + group, ln]
                    for k in range(3)
                ]
                t0 = w0 * xs[0]
                t2 = w2 * gs[0]
                vec = xs[1] * ys[0] + xs[2] * ys[1] + xs[3] * ys[2]
                along = gs[0]
                direct = gs[0] * xs[0]
                for m in range(1, 9):
                    along = along + gs[m] * ys[m - 1]
                    direct = direct + gs[m] * xs[m]
                    dy[m - 1] = dy[m - 1] + t0 * gs[m]
                    if m < 4:
                        dy[m - 1] = dy[m - 1] + t2 * xs[m]
                dy[8] = dy[8] + (d0 * xs[0] * along + d1 * direct + d2 * gs[0] * vec)
            for m in range(9):
                dys[b, m, pl.ds(first + s, 1), :] = jnp.sum(dy[m], axis=0, keepdims=True)

    def backward(i, _):
        edge_terms(even, 2 * i)
        edge_terms(odd, 2 * i + 1)
        return 0

    lax.fori_loop(0, steps // 2, backward, 0)
    force_ref[...] = jnp.zeros(force_ref.shape, F32)

    def pull(b, _):
        r, c = b // cols, b % cols
        ux, uy, uz, recip = geo[b, 4], geo[b, 5], geo[b, 6], geo[b, 1]
        d1, d2, d3, d4, d5, d6, d7, d8 = [dys[b, m] for m in range(8)]
        gx = root3 * d1 + root15 * (uy * d4 + uz * d7 + ux * d8)
        gy = root3 * d2 + root15 * (ux * d4 + uz * d5 - uy * d8)
        gz = root3 * d3 + root15 * (uy * d5 + ux * d7) + (3.0 * root5) * uz * d6
        radial = dys[b, 8] - (ux * gx + uy * gy + uz * gz) * recip
        grads = [gx * recip + ux * radial, gy * recip + uy * radial, gz * recip + uz * radial]
        for i in range(3):
            here = jnp.sum(grads[i], axis=0, keepdims=True)
            force_ref[r + 1, c + 1, i : i + 1, :] += here
        split = [halves(g) for g in grads]
        which = lax.broadcasted_iota(jnp.int32, (16, LANES), 0).astype(F32)
        place = geo[b, 7]
        for n in range(slots):
            ln = slice(n * LANES, (n + 1) * LANES)
            hit = which == place[n : n + 1]
            for i in range(3):
                for v in range(2):
                    line = split[i][v][n : n + 1].astype(F32)
                    at = (3 * v + i) * 16
                    lhs[at : at + 16, ln] = jnp.where(hit, line, 0.0).astype(BF16)
        total = jnp.zeros((96, LANES), F32)
        for p in range(quads):
            total = total + lax.dot_general(
                lhs[:, p * wide : (p + 1) * wide],
                near[b * quads + p],
                (((1,), (1,)), ((), ())),
                preferred_element_type=F32,
            )
        for i in range(3):
            for k in range(9):
                at = i * 16 + k
                value = total[at : at + 1] + total[48 + at : 49 + at]
                force_ref[r + k // 3, c + k % 3, i : i + 1, :] -= value
        return 0

    lax.fori_loop(0, blocks, pull, 0)
    for r in range(rows + 2):
        for i in range(3):
            fleft_ref[r, i] = force_ref[r, 0:1, i, :]
            fright_ref[r, i] = force_ref[r, cols + 1 :, i, :]
            fown_ref[r, i] = force_ref[r, 1 : cols + 1, i, :]


def vmem_call(body, name, ins, out_shape, scratch, limit, flops):
    vmem = pl.BlockSpec(memory_space=pltpu.VMEM)
    return pl.pallas_call(
        body,
        out_shape=out_shape,
        in_specs=ins,
        out_specs=[vmem] * len(out_shape),
        scratch_shapes=scratch,
        compiler_params=pltpu.CompilerParams(vmem_limit_bytes=limit * 1024 * 1024),
        cost_estimate=pl.CostEstimate(flops=flops, bytes_accessed=1024 * 1024, transcendentals=0),
        name=name,
    )


def pinned(*args):
    return [pltpu.with_memory_space_constraint(x, pltpu.HBM) for x in args]


def prepare_part(own, feats, neighbours, w_first, w_second, w_read, w_out):
    rows, cols, slots = neighbours.shape[0], neighbours.shape[1], neighbours.shape[2]
    hidden, basis = w_first.shape
    units, reads = w_read.shape
    weights = w_second.shape[0]
    blocks, steps, wide = rows * cols, rows * cols * slots // QUAD, QUAD * LANES
    spans = min(rows, 3)
    vmem = pl.BlockSpec(memory_space=pltpu.VMEM)
    hbm = pl.BlockSpec(memory_space=pltpu.HBM)
    sds = jax.ShapeDtypeStruct
    call = vmem_call(
        functools.partial(prepare_kernel, rows, cols, slots),
        "prepare",
        [vmem] + [hbm] * 5,
        [
            sds((steps, LANES, wide), BF16),
            sds((blocks, slots, LANES), F32),
            sds((2 * hidden, 8 * basis), BF16),
            sds((weights, 3 * hidden), BF16),
            sds((units, 3 * reads), BF16),
            sds((reads, 3 * units), BF16),
            sds((units, 1), F32),
            sds((steps, feats, wide), BF16),
        ],
        [
            pltpu.VMEM(neighbours.shape, jnp.int32),
            pltpu.VMEM((basis, hidden), F32),
            pltpu.VMEM((hidden, weights), F32),
            pltpu.VMEM((reads, units), F32),
            pltpu.VMEM((1, units), F32),
            pltpu.VMEM((blocks, slots, LANES), F32),
            pltpu.VMEM((blocks, feats, spans * LANES), BF16),
            pltpu.VMEM((spans * LANES, wide), BF16),
            pltpu.VMEM((spans * LANES, wide), BF16),
            pltpu.SemaphoreType.DMA((5,)),
        ],
        16,
        2 * feats * spans * LANES * steps * wide,
    )
    return call(
        own, *pinned(neighbours, w_first.T, w_second.T, w_read.T, w_out.reshape(1, units))
    )


def pack_part(features, pos):
    rows, cols, feats, _ = features.shape
    vmem = pl.BlockSpec(memory_space=pltpu.VMEM)
    hbm = pl.BlockSpec(memory_space=pltpu.HBM)
    call = vmem_call(
        functools.partial(pack_kernel, rows, cols),
        "pack",
        [hbm] * 2,
        [jax.ShapeDtypeStruct((rows, cols, feats + 16, LANES), BF16)],
        [pltpu.VMEM(pos.shape, F32), pltpu.SemaphoreType.DMA((1 + rows * cols,))],
        2,
        1000000,
    )
    return call(*pinned(features, pos))[0]


def ends_part(left, right):
    vmem = pl.BlockSpec(memory_space=pltpu.VMEM)
    message = jax.ShapeDtypeStruct((left.shape[2], 2 * LANES), BF16)
    call = vmem_call(
        functools.partial(ends_kernel, left.shape[0]),
        "ends",
        [vmem] * 2,
        [message] * 2,
        [],
        2,
        1000000,
    )
    return call(left, right)


def local_part(before, after, left, right, own, near, place, xa):
    rows, cols, feats = own.shape[0], own.shape[1], xa.shape[1]
    steps, _, wide = near.shape
    most = 5 if rows == 2 else 6
    vmem = pl.BlockSpec(memory_space=pltpu.VMEM)
    call = vmem_call(
        functools.partial(local_kernel, rows, cols),
        "local",
        [vmem] * 8,
        [jax.ShapeDtypeStruct((steps, feats, wide), BF16)],
        [
            pltpu.VMEM((rows * cols, feats, most * LANES), BF16),
            pltpu.VMEM((most * LANES, wide), BF16),
            pltpu.VMEM((most * LANES, wide), BF16),
        ],
        16,
        2 * feats * most * LANES * steps * wide,
    )
    return call(before, after, left, right, own, near, place, xa)[0]


def energy_part(ghosts, own, left, right, neighbours, counts, prepared, gathered):
    near, place, w1s, w2s, wrs, wrt, woc = prepared[:7]
    rows, cols, slots = neighbours.shape[0], neighbours.shape[1], neighbours.shape[2]
    steps, _, wide = near.shape
    weights = w2s.shape[0]
    channels, blocks, feats = weights // 3, rows * cols, gathered.shape[1]
    vmem = pl.BlockSpec(memory_space=pltpu.VMEM)
    hbm = pl.BlockSpec(memory_space=pltpu.HBM)
    sds = jax.ShapeDtypeStruct
    side = sds((rows + 2, 3, 1, LANES), F32)
    stream = blocks > 2
    half = steps // 2
    call = vmem_call(
        functools.partial(energy_kernel, rows, cols, channels, slots, stream=stream),
        "energy",
        [vmem] * 7 + [hbm] * 2 + [vmem] * 6 + [hbm if stream else vmem],
        [sds((rows, cols, 1, LANES), F32), side, sds((rows + 2, 3, cols, LANES), F32), side],
        [
            pltpu.VMEM((rows + 2, cols + 2, 3, LANES), F32),
            pltpu.VMEM((rows + 2, cols + 2, 3, LANES), F32),
            pltpu.VMEM((rows, cols, slots, LANES), jnp.int32),
            pltpu.VMEM((rows, cols, 1, LANES), jnp.int32),
            pltpu.VMEM((blocks, 8, slots, LANES), F32),
            pltpu.VMEM((blocks, 8, slots, LANES), F32),
            pltpu.VMEM((blocks, feats, 2 * LANES), BF16),
            pltpu.VMEM((RING, feats, wide) if stream else (1, 16, LANES), BF16),
            pltpu.VMEM((half, feats, wide), F32),
            pltpu.VMEM((half, feats, wide), F32),
            pltpu.VMEM((half, weights, wide), F32),
            pltpu.VMEM((half, weights, wide), F32),
            pltpu.VMEM((half, weights, wide), F32),
            pltpu.VMEM((half, weights, wide), F32),
            pltpu.VMEM((blocks, 9, channels, LANES), F32),
            pltpu.VMEM((weights, blocks * LANES), F32),
            pltpu.VMEM((blocks, 9, slots, LANES), F32),
            pltpu.VMEM((96, slots * LANES), BF16),
            pltpu.SemaphoreType.DMA((2,)),
            pltpu.SemaphoreType.DMA((RING,)),
        ],
        56 if stream else 32,
        2 * feats * 9 * LANES * steps * wide,
    )
    energies, f_left, f_own, f_right = call(
        *ghosts,
        own,
        left,
        right,
        *pinned(neighbours, counts.reshape(rows, cols, 1, LANES)),
        near,
        w1s,
        w2s,
        wrs,
        wrt,
        woc,
        gathered,
    )
    return f_left, f_own, f_right, energies.reshape(rows, cols, LANES)


def local(
    positions,
    velocities,
    features,
    neighbours,
    counts,
    w_first,
    w_second,
    w_read,
    w_out,
    fresh_positions,
    fresh_velocities,
):
    nrows, ncols = (positions.shape[0], positions.shape[1])
    shock_place = lax.axis_index("shock")
    front = lax.axis_size("shock") - 1
    assert nrows >= 2 and neighbours.shape[2] % (2 * QUAD) == 0

    def sides(x, axis):
        last = lax.slice_in_dim(x, ncols - 1, ncols, axis=axis)
        first = lax.slice_in_dim(x, 0, 1, axis=axis)
        return shifted(last, "trans", 1), shifted(first, "trans", -1)

    pos = positions.transpose(0, 2, 1, 3)
    vel = velocities.transpose(0, 2, 1, 3)
    own = pack_part(features, pos)
    left, right = sides(own, 1)
    before = passed_along(own[nrows - 1 :], "shock", 1)
    after = passed_along(own[:1], "shock", -1)
    feats = features.shape[2]
    prepared = prepare_part(own, feats, neighbours, w_first, w_second, w_read, w_out)
    near, place, xa = prepared[0], prepared[1], prepared[7]
    left, right, near = lax.optimization_barrier((left, right, near))
    last, first = ends_part(left, right)
    ghosts = (
        passed_along(last, "shock", 1),
        passed_along(first, "shock", -1),
        before,
        after,
    )
    gathered = local_part(before, after, left, right, own, near, place, xa)
    f_left, f_own, f_right, energies = energy_part(
        ghosts, own, left, right, neighbours, counts, prepared, gathered
    )
    from_right = shifted(f_left, "trans", -1)
    from_left = shifted(f_right, "trans", 1)
    folded = f_own.at[:, :, ncols - 1].add(from_right[:, :, 0])
    folded = folded.at[:, :, 0].add(from_left[:, :, 0])
    packed = jnp.concatenate([folded[:2], vel[:1], pos[:1]], axis=0)
    ahead = passed_along(packed, "shock", -1)
    force = folded[2 : nrows + 2]
    force = jnp.concatenate([force[: nrows - 2], force[nrows - 2 :] + ahead[:2]], axis=0)
    old_vel = jnp.concatenate([vel[1:], ahead[2:3]], axis=0)
    old_pos = jnp.concatenate([pos[1:], ahead[3:4]], axis=0)
    new_vel = old_vel + KICK_FACTOR * force
    moved = old_pos + MOVE_FACTOR * new_vel
    at_front = shock_place == front
    last_pos = jnp.where(at_front, fresh_positions.transpose(1, 0, 2), moved[nrows - 1])
    last_vel = jnp.where(at_front, fresh_velocities.transpose(1, 0, 2), new_vel[nrows - 1])
    new_positions = jnp.concatenate([moved[: nrows - 1], last_pos[None]], axis=0)
    new_velocities = jnp.concatenate([new_vel[: nrows - 1], last_vel[None]], axis=0)
    return (energies, new_positions.transpose(0, 2, 1, 3), new_velocities.transpose(0, 2, 1, 3))


def solution(mesh):
    return jax.shard_map(
        local,
        mesh=mesh,
        in_specs=(
            P("shock", "trans", None, None),
            P("shock", "trans", None, None),
            P("shock", "trans", None, None),
            P("shock", "trans", None, None),
            P("shock", "trans", None),
            P(),
            P(),
            P(),
            P(),
            P("trans", None, None),
            P("trans", None, None),
        ),
        out_specs=(
            P("shock", "trans", None),
            P("shock", "trans", None, None),
            P("shock", "trans", None, None),
        ),
        check_vma=False,
    )
```

```python
import functools
import math

import jax
import jax.numpy as jnp
from jax import lax
from jax.experimental import pallas as pl
from jax.experimental.pallas import tpu as pltpu
from jax.sharding import PartitionSpec as P

CUTOFF_RADIUS = 9.5
BLOCK_LENGTH = 13.2
KICK_FACTOR = 4.0
MOVE_FACTOR = 0.5
F32 = jnp.float32
BF16 = jnp.bfloat16
LANES = 128
QUAD = 4


def shifted(x, axis, by):
    count = lax.axis_size(axis)
    return lax.ppermute(x, axis, [(i, (i + by) % count) for i in range(count)])


def passed_along(block, axis, distance):
    devices = range(lax.axis_size(axis))
    route = [(i - distance, i) for i in devices if i - distance in devices]
    return lax.ppermute(block, axis, route)


def halves(x):
    hi = x.astype(BF16)
    lo = (x - hi.astype(F32)).astype(BF16)
    return hi, lo


def value_rows(x):
    hi, lo = halves(x)
    return jnp.concatenate([hi, lo, hi], axis=0)


def dot(a, b):
    return jnp.dot(a, b, preferred_element_type=F32)


def sin_cos_half_turns(t):
    n = jnp.floor(t + 0.5)
    r = t - n
    odd = n - 2.0 * jnp.floor(0.5 * n)
    sign = 1.0 - 2.0 * odd
    x = math.pi * r
    y = x * x
    s = 1.0 + y * (
        -1.0 / 6
        + y
        * (
            1.0 / 120
            + y * (-1.0 / 5040 + y * (1.0 / 362880 + y * (-1.0 / 39916800 + y * (1.0 / 6227020800.0))))
        )
    )
    c = 1.0 + y * (
        -0.5
        + y
        * (
            1.0 / 24
            + y
            * (-1.0 / 720 + y * (1.0 / 40320 + y * (-1.0 / 3628800 + y * (1.0 / 479001600.0))))
        )
    )
    return sign * x * s, sign * c


def weight_halves(w):
    hi = w.astype(BF16).astype(F32)
    return hi, w - hi


def weight_rows(w):
    hi, lo = weight_halves(w)
    return jnp.concatenate([hi, hi, lo], axis=1).astype(BF16)


def joined(ref, b, k, first, count):
    lines = [ref[b, k, pl.ds(first + s, 1), :] for s in range(count)]
    return jnp.concatenate(lines, axis=1)


def lines(ref, b, first, count):
    return jnp.concatenate([ref[b, pl.ds(first + s, 1), :] for s in range(count)], axis=1)


def first_row(rows, r):
    return 1 if (rows == 2 and r == 0) else 0


def window_hot(near, place, wanted):
    lanes = near.shape[1]
    near3 = near.reshape(LANES // 16, 16, lanes)
    parts = []
    for k in wanted:
        mask = jnp.where(place == jnp.asarray(k).astype(F32), 1.0, 0.0)
        mask = jnp.broadcast_to(mask, (16, lanes)).astype(BF16)
        parts.append((near3 * mask[None]).reshape(LANES, lanes))
    return parts


def decoded(codes):
    zq = (codes >= 1152).astype(jnp.int32) + (codes >= 2304).astype(jnp.int32)
    slot = codes - 1152 * zq
    return zq, lax.shift_right_logical(slot, 7), slot & 127


def copied(sources, places, sems):
    copies = [
        pltpu.make_async_copy(x, y, sems.at[i]) for i, (x, y) in enumerate(zip(sources, places))
    ]
    for copy in copies:
        copy.start()
    return copies


def prepare_kernel(
    rows,
    cols,
    slots,
    own_ref,
    codes_hbm,
    w1_hbm,
    w2_hbm,
    wr_hbm,
    wo_hbm,
    near,
    place,
    w1s,
    w2s,
    wrs,
    wrt,
    woc,
    out,
    codes_ref,
    w1_ref,
    w2_ref,
    wr_ref,
    wo_ref,
    atoms,
    win,
    onehot_even,
    onehot_odd,
    sems,
):
    blocks = rows * cols
    quads = slots // QUAD
    wide = QUAD * LANES
    spans = win.shape[2] // LANES
    copies = copied(
        [codes_hbm, w1_hbm, w2_hbm, wr_hbm, wo_hbm],
        [codes_ref, w1_ref, w2_ref, wr_ref, wo_ref],
        sems,
    )
    copies[0].wait()
    for r in range(rows):
        for c in range(cols):
            _, block, atom = decoded(codes_ref[r, c])
            place[r * cols + c] = block.astype(F32)
            atoms[r * cols + c] = atom.astype(F32)
    feats = win.shape[1]
    for r in range(rows):
        first = first_row(rows, r)
        for c in range(cols):
            for k in range(spans):
                ln = slice(k * LANES, (k + 1) * LANES)
                if 0 <= r - 1 + first + k < rows:
                    win[r * cols + c, :, ln] = own_ref[r - 1 + first + k, c, :feats]
                else:
                    win[r * cols + c, :, ln] = jnp.zeros((feats, LANES), BF16)

    def pick(onehot, step):
        b, at = step // quads, (step % quads) * QUAD
        atom = lines(atoms, b, at, QUAD)
        sub = lax.broadcasted_iota(jnp.int32, (LANES, wide), 0).astype(F32)
        hot = jnp.where(sub == atom, 1.0, 0.0).astype(BF16)
        near[step] = hot
        first = jnp.where(b // cols == 0, first_row(rows, 0), 0)
        wanted = [3 * (first + k) + 1 for k in range(spans)]
        parts = window_hot(hot, lines(place, b, at, QUAD), wanted)
        for k in range(spans):
            onehot[k * LANES : (k + 1) * LANES, :] = parts[k]
        out[step] = dot(win[b], onehot[...]).astype(BF16)

    def body(i, _):
        pick(onehot_even, 2 * i)
        pick(onehot_odd, 2 * i + 1)
        return 0

    lax.fori_loop(0, blocks * quads // 2, body, 0)

    for copy in copies[1:]:
        copy.wait()
    hi, lo = weight_halves(w1_ref[...].T)
    line = jnp.concatenate([hi, hi, lo, lo], axis=1)
    none = jnp.zeros_like(line)
    w1s[...] = jnp.concatenate(
        [jnp.concatenate([line, none], axis=1), jnp.concatenate([none, line], axis=1)], axis=0
    ).astype(BF16)
    w2s[...] = weight_rows(w2_ref[...].T)
    wrs[...] = weight_rows(wr_ref[...].T)
    wrt[...] = weight_rows(wr_ref[...])
    units = wo_ref.shape[1]
    one = lax.broadcasted_iota(jnp.int32, (units, units), 0)
    two = lax.broadcasted_iota(jnp.int32, (units, units), 1)
    woc[...] = jnp.sum(jnp.where(one == two, wo_ref[...], 0.0), axis=1, keepdims=True)


def pack_kernel(rows, cols, feat_hbm, pos_hbm, out, pos_ref, sems):
    feats = feat_hbm.shape[2]
    copies = copied(
        [pos_hbm] + [feat_hbm.at[r, c] for r in range(rows) for c in range(cols)],
        [pos_ref] + [out.at[r, c, pl.ds(0, feats)] for r in range(rows) for c in range(cols)],
        sems,
    )
    copies[0].wait()
    for r in range(rows):
        for c in range(cols):
            rest = jnp.concatenate([pos_ref[r, i, c : c + 1, :] for i in range(3)], axis=0)
            parts = []
            for _ in range(3):
                part = rest.astype(BF16).astype(F32)
                parts.append(part)
                rest = rest - part
            parts.append(jnp.zeros((7, LANES), F32))
            out[r, c, feats:] = jnp.concatenate(parts, axis=0).astype(BF16)
    for copy in copies[1:]:
        copy.wait()


def place_of(block, feats):
    rest = block[feats : feats + 16].astype(F32)
    return rest[0:3] + rest[3:6] + rest[6:9]


def ends_kernel(rows, left_ref, right_ref, up, down):
    for out, r in ((up, rows - 1), (down, 0)):
        out[:, :LANES] = left_ref[r, 0]
        out[:, LANES:] = right_ref[r, 0]


def ghost_kernel(rows, cols, prev_ref, next_ref, near, place, xa, out):
    steps = near.shape[0]
    quads = steps // (rows * cols)
    feats = out.shape[1]
    for b in range(rows * cols):
        r, c = b // cols, b % cols

        def pick(step):
            first = (step % quads) * QUAD
            if r == 0 or r == rows - 1:
                ref, slot = (prev_ref, 1) if r == 0 else (next_ref, 7)
                hot = window_hot(near[step], lines(place, b, first, QUAD), [slot])[0]
                out[step] = xa[step] + dot(ref[0, c, :feats], hot).astype(BF16)
            else:
                out[step] = xa[step]

        def body(i, _):
            pick(b * quads + 2 * i)
            pick(b * quads + 2 * i + 1)
            return 0

        lax.fori_loop(0, quads // 2, body, 0)


def finish_kernel(
    rows, front_ref, force, ahead, vel, pos, fresh_pos, fresh_vel, new_pos, new_vel
):
    front = front_ref[0] == 1
    for r in range(rows):
        total = force[r + 2]
        if r >= rows - 2:
            total = total + ahead[r - rows + 2]
        old_vel = vel[r + 1] if r < rows - 1 else ahead[2]
        old_pos = pos[r + 1] if r < rows - 1 else ahead[3]
        v = old_vel + KICK_FACTOR * total
        p = old_pos + MOVE_FACTOR * v
        if r == rows - 1:
            v = jnp.where(front, fresh_vel[...], v)
            p = jnp.where(front, fresh_pos[...], p)
        new_vel[r] = v
        new_pos[r] = p


def local_kernel(
    rows,
    cols,
    left_ref,
    right_ref,
    own_ref,
    near,
    place,
    xa,
    out,
    win,
    hot_even,
    hot_odd,
):
    blocks = rows * cols
    steps = near.shape[0]
    quads = steps // blocks
    feats = out.shape[1]

    def columns(r, c):
        found = []
        for k in range(3):
            row = r - 1 + k
            for col in (c - 1, c, c + 1):
                slot = 3 * k + col - c + 1
                if 0 <= row < rows and col != c:
                    if col < 0:
                        found.append((slot, left_ref[row, 0, :feats]))
                    elif col >= cols:
                        found.append((slot, right_ref[row, 0, :feats]))
                    else:
                        found.append((slot, own_ref[row, col, :feats]))
        return found

    for b in range(blocks):
        found = columns(b // cols, b % cols)
        count = len(found)
        for k, (_, block) in enumerate(found):
            win[b, :, k * LANES : (k + 1) * LANES] = block

        def pick(hot, step):
            first = (step % quads) * QUAD
            parts = window_hot(near[step], lines(place, b, first, QUAD), [x for x, _ in found])
            for k in range(count):
                hot[k * LANES : (k + 1) * LANES, :] = parts[k]
            picked = dot(win[b, :, : count * LANES], hot[: count * LANES, :])
            out[step] = xa[step] + picked.astype(BF16)

        def body(i, _):
            pick(hot_even, b * quads + 2 * i)
            pick(hot_odd, b * quads + 2 * i + 1)
            return 0

        lax.fori_loop(0, quads // 2, body, 0)


RING = 3


def energy_kernel(
    rows,
    cols,
    channels,
    slots,
    prev_ref,
    next_ref,
    prev_own_ref,
    next_own_ref,
    own_ref,
    left_ref,
    right_ref,
    codes_hbm,
    counts_hbm,
    near,
    w1s,
    w2s,
    wrs,
    wrt,
    woc,
    xl_hbm,
    en_ref,
    fleft_ref,
    fown_ref,
    fright_ref,
    force_ref,
    pos_ref,
    codes_ref,
    counts_ref,
    geo,
    har,
    win,
    xl,
    xg_even,
    xg_odd,
    w_even,
    w_odd,
    d_even,
    d_odd,
    held_even,
    held_odd,
    acc,
    inv,
    dys,
    lhs,
    sems,
    xsem,
    *,
    stream,
):
    blocks = rows * cols
    quads = slots // QUAD
    steps = blocks * quads
    wide = QUAD * LANES
    group = 8
    feats = 9 * channels
    root3, root5, root15 = math.sqrt(3.0), math.sqrt(5.0), math.sqrt(15.0)
    even, odd = (xg_even, w_even, d_even, held_even), (xg_odd, w_odd, d_odd, held_odd)

    def x_copy(step):
        at = step % RING
        return pltpu.make_async_copy(xl_hbm.at[step], xl.at[at], xsem.at[at])

    copies = copied([codes_hbm, counts_hbm], [codes_ref, counts_ref], sems)
    if stream:
        for i in range(RING):
            x_copy(i).start()

    for side, middle, r in ((prev_ref, prev_own_ref, 0), (next_ref, next_own_ref, rows + 1)):
        pos_ref[r, 0] = place_of(side[:, :LANES], feats)
        pos_ref[r, cols + 1] = place_of(side[:, LANES:], feats)
        for c in range(cols):
            pos_ref[r, c + 1] = place_of(middle[0, c], feats)
    for r in range(rows):
        pos_ref[r + 1, 0] = place_of(left_ref[r, 0], feats)
        pos_ref[r + 1, cols + 1] = place_of(right_ref[r, 0], feats)
        for c in range(cols):
            pos_ref[r + 1, c + 1] = place_of(own_ref[r, c], feats)
            none = jnp.zeros((feats, LANES), BF16)
            ref = prev_ref if r == 0 else next_ref
            ends = r == 0 or r == rows - 1
            b = r * cols + c
            win[b, :, :LANES] = ref[:feats, :LANES] if ends and c == 0 else none
            win[b, :, LANES:] = ref[:feats, LANES:] if ends and c == cols - 1 else none
    acc[...] = jnp.zeros(acc.shape, F32)
    for copy in copies:
        copy.wait()

    def geometry(b, _):
        r, c = b // cols, b % cols
        zq, near_block, atom = decoded(codes_ref[r, c])
        row3 = (near_block >= 3).astype(jnp.int32) + (near_block >= 6).astype(jnp.int32)
        shift_x = (row3 - 1).astype(F32) * BLOCK_LENGTH
        shift_y = (near_block - 3 * row3 - 1).astype(F32) * BLOCK_LENGTH
        shift_z = (zq - 1).astype(F32) * BLOCK_LENGTH
        centre = pos_ref[r + 1, c + 1]
        found = [jnp.zeros((slots, LANES), F32) for _ in range(3)]
        for k in range(9):
            place = pos_ref[r + k // 3, c + k % 3]
            here = near_block == k
            for i in range(3):
                line = jnp.broadcast_to(place[i : i + 1], (slots, LANES))
                value = jnp.take_along_axis(line, atom, axis=1, mode="promise_in_bounds")
                found[i] = jnp.where(here, value, found[i])
        rx = found[0] + shift_x - centre[0:1]
        ry = found[1] + shift_y - centre[1:2]
        rz = found[2] + shift_z - centre[2:3]
        dist = jnp.sqrt(rx * rx + ry * ry + rz * rz)
        recip = 1.0 / dist
        ux, uy, uz = rx * recip, ry * recip, rz * recip
        x = dist * (1.0 / CUTOFF_RADIUS)
        x2 = x * x
        x5 = x2 * x2 * x
        live = lax.broadcasted_iota(jnp.int32, (slots, LANES), 0) < counts_ref[r, c]
        scale = jnp.where(live, 1.0 / slots, 0.0)
        env = (1.0 - x5 * x * (28.0 - x * (48.0 - 21.0 * x))) * scale
        denv = (-168.0 / CUTOFF_RADIUS) * x5 * (1.0 - x * (2.0 - x)) * scale
        geo[b, 0] = dist
        geo[b, 1] = recip
        geo[b, 2] = env
        geo[b, 3] = denv
        geo[b, 4] = ux
        geo[b, 5] = uy
        geo[b, 6] = uz
        geo[b, 7] = near_block.astype(F32)
        har[b, 0] = root3 * ux
        har[b, 1] = root3 * uy
        har[b, 2] = root3 * uz
        har[b, 3] = root15 * ux * uy
        har[b, 4] = root15 * uy * uz
        har[b, 5] = 0.5 * root5 * (3.0 * uz * uz - 1.0)
        har[b, 6] = root15 * ux * uz
        har[b, 7] = 0.5 * root15 * (ux * ux - uy * uy)
        return 0

    lax.fori_loop(0, blocks, geometry, 0)

    def hidden_rows(buffers, step):
        held = buffers[3]
        b, first = step // quads, (step % quads) * QUAD
        dist, recip, env, denv = [joined(geo, b, k, first, QUAD) for k in range(4)]
        order = (lax.broadcasted_iota(jnp.int32, (8, wide), 0) + 1).astype(F32)
        sin, cos = sin_cos_half_turns(order * (dist * (1.0 / CUTOFF_RADIUS)))
        norm = math.sqrt(2.0 / CUTOFF_RADIUS)
        basis = norm * sin * recip
        slope = ((norm * math.pi / CUTOFF_RADIUS) * order * cos - basis) * recip
        split = []
        for x in (basis, slope):
            hi = x.astype(BF16).astype(F32)
            split += [hi, x - hi] * 2
        pre2 = dot(w1s[...], jnp.concatenate(split, axis=0).astype(BF16))
        pre, dpre = pre2[: pre2.shape[0] // 2], pre2[pre2.shape[0] // 2 :]
        gate = 1.0 / (1.0 + jnp.exp(-pre))
        h = pre * gate
        dh = gate + h * (1.0 - gate)
        held[0] = value_rows(h * env)
        held[1] = value_rows(dh * dpre * env + h * denv)

    def radial_rows(buffers, step):
        _, wsc, dsc, held = buffers
        wsc[step // 2] = dot(w2s[...], held[0])
        dsc[step // 2] = dot(w2s[...], held[1])

    def gather(buffers, step):
        b, first = step // quads, (step % quads) * QUAD
        r = b // cols
        k0 = jnp.where(r == 0, 0, jnp.where(r == rows - 1, 6, 9))
        parts = window_hot(near[step], joined(geo, b, 7, first, QUAD), [k0, k0 + 2])
        if stream:
            x_copy(step).wait()
            held = xl[step % RING]
        else:
            held = xl_hbm[step]
        buffers[0][step // 2] = held.astype(F32) + dot(win[b], jnp.concatenate(parts, axis=0))

    def collect(buffers, step):
        xg, wsc = buffers[:2]
        b, first = step // quads, (step % quads) * QUAD
        for g in range(channels // group):
            at = g * group
            total = [acc[b, m, at : at + group, :] for m in range(9)]
            for s in range(QUAD):
                ln = slice(s * LANES, (s + 1) * LANES)
                xs = [
                    xg[step // 2, m * channels + at : m * channels + at + group, ln]
                    for m in range(9)
                ]
                w0, w1, w2 = [
                    wsc[step // 2, k * channels + at : k * channels + at + group, ln]
                    for k in range(3)
                ]
                ys = [har[b, m, pl.ds(first + s, 1), :] for m in range(8)]
                t0 = w0 * xs[0]
                vec = xs[1] * ys[0] + xs[2] * ys[1] + xs[3] * ys[2]
                total[0] = total[0] + (t0 + w1 * xs[0]) + w2 * vec
                for m in range(1, 9):
                    total[m] = total[m] + (t0 * ys[m - 1] + w1 * xs[m])
            for m in range(9):
                acc[b, m, at : at + group, :] = total[m]

    def advance(new, old, step, last=False):
        radial_rows(new, step)
        gather(new, step)
        collect(old, step - 1)
        if not last:
            hidden_rows(old, step + 1)
        if stream:

            @pl.when(step + RING - 1 < steps)
            def _():
                x_copy(step + RING - 1).start()

    def forward(i, _):
        advance(even, odd, 2 * i)
        advance(odd, even, 2 * i + 1)
        return 0

    hidden_rows(even, 0)
    hidden_rows(odd, 1)
    radial_rows(even, 0)
    gather(even, 0)
    advance(odd, even, 1)
    lax.fori_loop(1, steps // 2 - 1, forward, 0)
    advance(even, odd, steps - 2)
    advance(odd, even, steps - 1, last=True)
    collect(odd, steps - 1)

    for b in range(blocks):
        ln = slice(b * LANES, (b + 1) * LANES)
        a = [acc[b, m] for m in range(9)]
        inv[0:channels, ln] = a[0] * a[0]
        inv[channels : 2 * channels, ln] = a[1] * a[1] + a[2] * a[2] + a[3] * a[3]
        inv[2 * channels :, ln] = (
            a[4] * a[4] + a[5] * a[5] + a[6] * a[6] + a[7] * a[7] + a[8] * a[8]
        )
    z = dot(wrs[...], value_rows(inv[...]))
    gate = 1.0 / (1.0 + jnp.exp(-z))
    out = z * gate
    wo = woc[...]
    energy = jnp.sum(out * wo, axis=0, keepdims=True)
    dinv = dot(wrt[...], value_rows(wo * (gate + out * (1.0 - gate))))
    for b in range(blocks):
        ln = slice(b * LANES, (b + 1) * LANES)
        en_ref[b // cols, b % cols] = energy[:, ln]
        for m in range(9):
            part = 0 if m == 0 else (1 if m < 4 else 2)
            d = dinv[part * channels : (part + 1) * channels, ln]
            acc[b, m] = 2.0 * acc[b, m] * d

    def edge_terms(buffers, step):
        xg, wsc, dsc = buffers[:3]
        b, first = step // quads, (step % quads) * QUAD
        for s in range(QUAD):
            ln = slice(s * LANES, (s + 1) * LANES)
            ys = [har[b, m, pl.ds(first + s, 1), :] for m in range(8)]
            dy = [jnp.zeros((group, LANES), F32) for _ in range(9)]
            for g in range(channels // group):
                at = g * group
                xs = [
                    xg[step // 2, m * channels + at : m * channels + at + group, ln]
                    for m in range(9)
                ]
                gs = [acc[b, m, at : at + group, :] for m in range(9)]
                w0 = wsc[step // 2, at : at + group, ln]
                w2 = wsc[step // 2, 2 * channels + at : 2 * channels + at + group, ln]
                d0, d1, d2 = [
                    dsc[step // 2, k * channels + at : k * channels + at + group, ln]
                    for k in range(3)
                ]
                t0 = w0 * xs[0]
                t2 = w2 * gs[0]
                vec = xs[1] * ys[0] + xs[2] * ys[1] + xs[3] * ys[2]
                along = gs[0]
                direct = gs[0] * xs[0]
                for m in range(1, 9):
                    along = along + gs[m] * ys[m - 1]
                    direct = direct + gs[m] * xs[m]
                    dy[m - 1] = dy[m - 1] + t0 * gs[m]
                    if m < 4:
                        dy[m - 1] = dy[m - 1] + t2 * xs[m]
                dy[8] = dy[8] + (d0 * xs[0] * along + d1 * direct + d2 * gs[0] * vec)
            for m in range(9):
                dys[b, m, pl.ds(first + s, 1), :] = jnp.sum(dy[m], axis=0, keepdims=True)

    def backward(i, _):
        edge_terms(even, 2 * i)
        edge_terms(odd, 2 * i + 1)
        return 0

    lax.fori_loop(0, steps // 2, backward, 0)
    force_ref[...] = jnp.zeros(force_ref.shape, F32)

    def pull(b, _):
        r, c = b // cols, b % cols
        ux, uy, uz, recip = geo[b, 4], geo[b, 5], geo[b, 6], geo[b, 1]
        d1, d2, d3, d4, d5, d6, d7, d8 = [dys[b, m] for m in range(8)]
        gx = root3 * d1 + root15 * (uy * d4 + uz * d7 + ux * d8)
        gy = root3 * d2 + root15 * (ux * d4 + uz * d5 - uy * d8)
        gz = root3 * d3 + root15 * (uy * d5 + ux * d7) + (3.0 * root5) * uz * d6
        radial = dys[b, 8] - (ux * gx + uy * gy + uz * gz) * recip
        grads = [gx * recip + ux * radial, gy * recip + uy * radial, gz * recip + uz * radial]
        for i in range(3):
            here = jnp.sum(grads[i], axis=0, keepdims=True)
            force_ref[r + 1, c + 1, i : i + 1, :] += here
        split = [halves(g) for g in grads]
        which = lax.broadcasted_iota(jnp.int32, (16, LANES), 0).astype(F32)
        place = geo[b, 7]
        for n in range(slots):
            ln = slice(n * LANES, (n + 1) * LANES)
            hit = which == place[n : n + 1]
            for i in range(3):
                for v in range(2):
                    line = split[i][v][n : n + 1].astype(F32)
                    at = (3 * v + i) * 16
                    lhs[at : at + 16, ln] = jnp.where(hit, line, 0.0).astype(BF16)
        total = jnp.zeros((96, LANES), F32)
        for p in range(quads):
            total = total + lax.dot_general(
                lhs[:, p * wide : (p + 1) * wide],
                near[b * quads + p],
                (((1,), (1,)), ((), ())),
                preferred_element_type=F32,
            )
        for i in range(3):
            for k in range(9):
                at = i * 16 + k
                value = total[at : at + 1] + total[48 + at : 49 + at]
                force_ref[r + k // 3, c + k % 3, i : i + 1, :] -= value
        return 0

    lax.fori_loop(0, blocks, pull, 0)
    for r in range(rows + 2):
        for i in range(3):
            fleft_ref[r, i] = force_ref[r, 0:1, i, :]
            fright_ref[r, i] = force_ref[r, cols + 1 :, i, :]
            fown_ref[r, i] = force_ref[r, 1 : cols + 1, i, :]


def vmem_call(body, name, ins, out_shape, scratch, limit, flops):
    vmem = pl.BlockSpec(memory_space=pltpu.VMEM)
    return pl.pallas_call(
        body,
        out_shape=out_shape,
        in_specs=ins,
        out_specs=[vmem] * len(out_shape),
        scratch_shapes=scratch,
        compiler_params=pltpu.CompilerParams(vmem_limit_bytes=limit * 1024 * 1024),
        cost_estimate=pl.CostEstimate(flops=flops, bytes_accessed=1024 * 1024, transcendentals=0),
        name=name,
    )


def pinned(*args):
    return [pltpu.with_memory_space_constraint(x, pltpu.HBM) for x in args]


def prepare_part(own, feats, neighbours, w_first, w_second, w_read, w_out):
    rows, cols, slots = neighbours.shape[0], neighbours.shape[1], neighbours.shape[2]
    hidden, basis = w_first.shape
    units, reads = w_read.shape
    weights = w_second.shape[0]
    blocks, steps, wide = rows * cols, rows * cols * slots // QUAD, QUAD * LANES
    spans = min(rows, 3)
    vmem = pl.BlockSpec(memory_space=pltpu.VMEM)
    hbm = pl.BlockSpec(memory_space=pltpu.HBM)
    sds = jax.ShapeDtypeStruct
    call = vmem_call(
        functools.partial(prepare_kernel, rows, cols, slots),
        "prepare",
        [vmem] + [hbm] * 5,
        [
            sds((steps, LANES, wide), BF16),
            sds((blocks, slots, LANES), F32),
            sds((2 * hidden, 8 * basis), BF16),
            sds((weights, 3 * hidden), BF16),
            sds((units, 3 * reads), BF16),
            sds((reads, 3 * units), BF16),
            sds((units, 1), F32),
            sds((steps, feats, wide), BF16),
        ],
        [
            pltpu.VMEM(neighbours.shape, jnp.int32),
            pltpu.VMEM((basis, hidden), F32),
            pltpu.VMEM((hidden, weights), F32),
            pltpu.VMEM((reads, units), F32),
            pltpu.VMEM((1, units), F32),
            pltpu.VMEM((blocks, slots, LANES), F32),
            pltpu.VMEM((blocks, feats, spans * LANES), BF16),
            pltpu.VMEM((spans * LANES, wide), BF16),
            pltpu.VMEM((spans * LANES, wide), BF16),
            pltpu.SemaphoreType.DMA((5,)),
        ],
        16,
        2 * feats * spans * LANES * steps * wide,
    )
    return call(
        own, *pinned(neighbours, w_first.T, w_second.T, w_read.T, w_out.reshape(1, units))
    )


def pack_part(features, pos):
    rows, cols, feats, _ = features.shape
    vmem = pl.BlockSpec(memory_space=pltpu.VMEM)
    hbm = pl.BlockSpec(memory_space=pltpu.HBM)
    call = vmem_call(
        functools.partial(pack_kernel, rows, cols),
        "pack",
        [hbm] * 2,
        [jax.ShapeDtypeStruct((rows, cols, feats + 16, LANES), BF16)],
        [pltpu.VMEM(pos.shape, F32), pltpu.SemaphoreType.DMA((1 + rows * cols,))],
        2,
        1000000,
    )
    return call(*pinned(features, pos))[0]


def ends_part(left, right):
    vmem = pl.BlockSpec(memory_space=pltpu.VMEM)
    message = jax.ShapeDtypeStruct((left.shape[2], 2 * LANES), BF16)
    call = vmem_call(
        functools.partial(ends_kernel, left.shape[0]),
        "ends",
        [vmem] * 2,
        [message] * 2,
        [],
        2,
        1000000,
    )
    return call(left, right)


def ghost_part(before, after, near, place, xa, rows, cols):
    vmem = pl.BlockSpec(memory_space=pltpu.VMEM)
    steps, feats, wide = xa.shape
    call = vmem_call(
        functools.partial(ghost_kernel, rows, cols),
        "ghost",
        [vmem] * 5,
        [jax.ShapeDtypeStruct(xa.shape, BF16)],
        [],
        8,
        2 * feats * LANES * steps * wide,
    )
    return call(before, after, near, place, xa)[0]


def finish_part(front, force, ahead, vel, pos, fresh_pos, fresh_vel):
    vmem = pl.BlockSpec(memory_space=pltpu.VMEM)
    smem = pl.BlockSpec(memory_space=pltpu.SMEM)
    call = vmem_call(
        functools.partial(finish_kernel, vel.shape[0]),
        "finish",
        [smem] + [vmem] * 6,
        [jax.ShapeDtypeStruct(vel.shape, F32)] * 2,
        [],
        2,
        100000,
    )
    return call(front, force, ahead, vel, pos, fresh_pos, fresh_vel)


def local_part(left, right, own, near, place, xa):
    rows, cols, feats = own.shape[0], own.shape[1], xa.shape[1]
    steps, _, wide = near.shape
    most = 2 * min(rows, 3)
    vmem = pl.BlockSpec(memory_space=pltpu.VMEM)
    call = vmem_call(
        functools.partial(local_kernel, rows, cols),
        "local",
        [vmem] * 6,
        [jax.ShapeDtypeStruct((steps, feats, wide), BF16)],
        [
            pltpu.VMEM((rows * cols, feats, most * LANES), BF16),
            pltpu.VMEM((most * LANES, wide), BF16),
            pltpu.VMEM((most * LANES, wide), BF16),
        ],
        16,
        2 * feats * most * LANES * steps * wide,
    )
    return call(left, right, own, near, place, xa)[0]


def energy_part(ghosts, own, left, right, neighbours, counts, prepared, gathered):
    near, place, w1s, w2s, wrs, wrt, woc = prepared[:7]
    rows, cols, slots = neighbours.shape[0], neighbours.shape[1], neighbours.shape[2]
    steps, _, wide = near.shape
    weights = w2s.shape[0]
    channels, blocks, feats = weights // 3, rows * cols, gathered.shape[1]
    vmem = pl.BlockSpec(memory_space=pltpu.VMEM)
    hbm = pl.BlockSpec(memory_space=pltpu.HBM)
    sds = jax.ShapeDtypeStruct
    side = sds((rows + 2, 3, 1, LANES), F32)
    stream = blocks > 2
    half = steps // 2
    call = vmem_call(
        functools.partial(energy_kernel, rows, cols, channels, slots, stream=stream),
        "energy",
        [vmem] * 7 + [hbm] * 2 + [vmem] * 6 + [hbm if stream else vmem],
        [sds((rows, cols, 1, LANES), F32), side, sds((rows + 2, 3, cols, LANES), F32), side],
        [
            pltpu.VMEM((rows + 2, cols + 2, 3, LANES), F32),
            pltpu.VMEM((rows + 2, cols + 2, 3, LANES), F32),
            pltpu.VMEM((rows, cols, slots, LANES), jnp.int32),
            pltpu.VMEM((rows, cols, 1, LANES), jnp.int32),
            pltpu.VMEM((blocks, 8, slots, LANES), F32),
            pltpu.VMEM((blocks, 8, slots, LANES), F32),
            pltpu.VMEM((blocks, feats, 2 * LANES), BF16),
            pltpu.VMEM((RING, feats, wide) if stream else (1, 16, LANES), BF16),
            pltpu.VMEM((half, feats, wide), F32),
            pltpu.VMEM((half, feats, wide), F32),
            pltpu.VMEM((half, weights, wide), F32),
            pltpu.VMEM((half, weights, wide), F32),
            pltpu.VMEM((half, weights, wide), F32),
            pltpu.VMEM((half, weights, wide), F32),
            pltpu.VMEM((2, 3 * (w1s.shape[0] // 2), wide), BF16),
            pltpu.VMEM((2, 3 * (w1s.shape[0] // 2), wide), BF16),
            pltpu.VMEM((blocks, 9, channels, LANES), F32),
            pltpu.VMEM((weights, blocks * LANES), F32),
            pltpu.VMEM((blocks, 9, slots, LANES), F32),
            pltpu.VMEM((96, slots * LANES), BF16),
            pltpu.SemaphoreType.DMA((2,)),
            pltpu.SemaphoreType.DMA((RING,)),
        ],
        56 if stream else 32,
        2 * feats * 9 * LANES * steps * wide,
    )
    energies, f_left, f_own, f_right = call(
        *ghosts,
        own,
        left,
        right,
        *pinned(neighbours, counts.reshape(rows, cols, 1, LANES)),
        near,
        w1s,
        w2s,
        wrs,
        wrt,
        woc,
        gathered,
    )
    return f_left, f_own, f_right, energies.reshape(rows, cols, LANES)


def local(
    positions,
    velocities,
    features,
    neighbours,
    counts,
    w_first,
    w_second,
    w_read,
    w_out,
    fresh_positions,
    fresh_velocities,
):
    nrows, ncols = (positions.shape[0], positions.shape[1])
    shock_place = lax.axis_index("shock")
    front = lax.axis_size("shock") - 1
    assert nrows >= 2 and neighbours.shape[2] % (2 * QUAD) == 0

    def sides(x, axis):
        last = lax.slice_in_dim(x, ncols - 1, ncols, axis=axis)
        first = lax.slice_in_dim(x, 0, 1, axis=axis)
        return shifted(last, "trans", 1), shifted(first, "trans", -1)

    pos = positions.transpose(0, 2, 1, 3)
    vel = velocities.transpose(0, 2, 1, 3)
    own = pack_part(features, pos)
    left, right = sides(own, 1)
    before = passed_along(own[nrows - 1 :], "shock", 1)
    after = passed_along(own[:1], "shock", -1)
    feats = features.shape[2]
    prepared = prepare_part(own, feats, neighbours, w_first, w_second, w_read, w_out)
    near, place, xa = prepared[0], prepared[1], prepared[7]
    xa = ghost_part(before, after, near, place, xa, nrows, ncols)
    left, right, xa = lax.optimization_barrier((left, right, xa))
    last, first = ends_part(left, right)
    ghosts = (
        passed_along(last, "shock", 1),
        passed_along(first, "shock", -1),
        before,
        after,
    )
    gathered = local_part(left, right, own, near, place, xa)
    f_left, f_own, f_right, energies = energy_part(
        ghosts, own, left, right, neighbours, counts, prepared, gathered
    )
    from_right = shifted(f_left, "trans", -1)
    from_left = shifted(f_right, "trans", 1)
    folded = f_own.at[:, :, ncols - 1].add(from_right[:, :, 0])
    folded = folded.at[:, :, 0].add(from_left[:, :, 0])
    packed = jnp.concatenate([folded[:2], vel[:1], pos[:1]], axis=0)
    ahead = passed_along(packed, "shock", -1)
    at_front = (shock_place == front).astype(jnp.int32).reshape(1)
    new_positions, new_velocities = finish_part(
        at_front,
        folded,
        ahead,
        vel,
        pos,
        fresh_positions.transpose(1, 0, 2),
        fresh_velocities.transpose(1, 0, 2),
    )
    return (energies, new_positions.transpose(0, 2, 1, 3), new_velocities.transpose(0, 2, 1, 3))


def solution(mesh):
    return jax.shard_map(
        local,
        mesh=mesh,
        in_specs=(
            P("shock", "trans", None, None),
            P("shock", "trans", None, None),
            P("shock", "trans", None, None),
            P("shock", "trans", None, None),
            P("shock", "trans", None),
            P(),
            P(),
            P(),
            P(),
            P("trans", None, None),
            P("trans", None, None),
        ),
        out_specs=(
            P("shock", "trans", None),
            P("shock", "trans", None, None),
            P("shock", "trans", None, None),
        ),
        check_vma=False,
    )
```

```python
import functools
import math

import jax
import jax.numpy as jnp
from jax import lax
from jax.experimental import pallas as pl
from jax.experimental.pallas import tpu as pltpu
from jax.sharding import PartitionSpec as P

CUTOFF_RADIUS = 9.5
BLOCK_LENGTH = 13.2
KICK_FACTOR = 4.0
MOVE_FACTOR = 0.5
F32 = jnp.float32
BF16 = jnp.bfloat16
LANES = 128
QUAD = 4


def shifted(x, axis, by):
    count = lax.axis_size(axis)
    return lax.ppermute(x, axis, [(i, (i + by) % count) for i in range(count)])


def passed_along(block, axis, distance):
    devices = range(lax.axis_size(axis))
    route = [(i - distance, i) for i in devices if i - distance in devices]
    return lax.ppermute(block, axis, route)


def halves(x):
    hi = x.astype(BF16)
    lo = (x - hi.astype(F32)).astype(BF16)
    return hi, lo


def value_rows(x):
    hi, lo = halves(x)
    return jnp.concatenate([hi, lo, hi], axis=0)


def dot(a, b):
    return jnp.dot(a, b, preferred_element_type=F32)


def sin_cos_half_turns(t):
    n = jnp.floor(t + 0.5)
    r = t - n
    odd = n - 2.0 * jnp.floor(0.5 * n)
    sign = 1.0 - 2.0 * odd
    x = math.pi * r
    y = x * x
    s = 1.0 + y * (
        -1.0 / 6
        + y
        * (
            1.0 / 120
            + y * (-1.0 / 5040 + y * (1.0 / 362880 + y * (-1.0 / 39916800 + y * (1.0 / 6227020800.0))))
        )
    )
    c = 1.0 + y * (
        -0.5
        + y
        * (
            1.0 / 24
            + y
            * (-1.0 / 720 + y * (1.0 / 40320 + y * (-1.0 / 3628800 + y * (1.0 / 479001600.0))))
        )
    )
    return sign * x * s, sign * c


def weight_halves(w):
    hi = w.astype(BF16).astype(F32)
    return hi, w - hi


def weight_rows(w):
    hi, lo = weight_halves(w)
    return jnp.concatenate([hi, hi, lo], axis=1).astype(BF16)


def joined(ref, b, k, first, count):
    lines = [ref[b, k, pl.ds(first + s, 1), :] for s in range(count)]
    return jnp.concatenate(lines, axis=1)


def lines(ref, b, first, count):
    return jnp.concatenate([ref[b, pl.ds(first + s, 1), :] for s in range(count)], axis=1)


def first_row(rows, r):
    return 1 if (rows == 2 and r == 0) else 0


def window_hot(near, place, wanted):
    lanes = near.shape[1]
    near3 = near.reshape(LANES // 16, 16, lanes)
    parts = []
    for k in wanted:
        mask = jnp.where(place == jnp.asarray(k).astype(F32), 1.0, 0.0)
        mask = jnp.broadcast_to(mask, (16, lanes)).astype(BF16)
        parts.append((near3 * mask[None]).reshape(LANES, lanes))
    return parts


def decoded(codes):
    zq = (codes >= 1152).astype(jnp.int32) + (codes >= 2304).astype(jnp.int32)
    slot = codes - 1152 * zq
    return zq, lax.shift_right_logical(slot, 7), slot & 127


def copied(sources, places, sems):
    copies = [
        pltpu.make_async_copy(x, y, sems.at[i]) for i, (x, y) in enumerate(zip(sources, places))
    ]
    for copy in copies:
        copy.start()
    return copies


def prepare_kernel(
    rows,
    cols,
    slots,
    own_ref,
    codes_hbm,
    w1_hbm,
    w2_hbm,
    wr_hbm,
    wo_hbm,
    near,
    place,
    w1s,
    w2s,
    wrs,
    wrt,
    woc,
    out,
    codes_ref,
    w1_ref,
    w2_ref,
    wr_ref,
    wo_ref,
    atoms,
    win,
    onehot_even,
    onehot_odd,
    sems,
):
    blocks = rows * cols
    quads = slots // QUAD
    wide = QUAD * LANES
    spans = win.shape[2] // LANES
    copies = copied(
        [codes_hbm, w1_hbm, w2_hbm, wr_hbm, wo_hbm],
        [codes_ref, w1_ref, w2_ref, wr_ref, wo_ref],
        sems,
    )
    copies[0].wait()
    for r in range(rows):
        for c in range(cols):
            _, block, atom = decoded(codes_ref[r, c])
            place[r * cols + c] = block.astype(F32)
            atoms[r * cols + c] = atom.astype(F32)
    feats = win.shape[1]
    for r in range(rows):
        first = first_row(rows, r)
        for c in range(cols):
            for k in range(spans):
                ln = slice(k * LANES, (k + 1) * LANES)
                if 0 <= r - 1 + first + k < rows:
                    win[r * cols + c, :, ln] = own_ref[r - 1 + first + k, c, :feats]
                else:
                    win[r * cols + c, :, ln] = jnp.zeros((feats, LANES), BF16)

    def pick(onehot, step):
        b, at = step // quads, (step % quads) * QUAD
        atom = lines(atoms, b, at, QUAD)
        sub = lax.broadcasted_iota(jnp.int32, (LANES, wide), 0).astype(F32)
        hot = jnp.where(sub == atom, 1.0, 0.0).astype(BF16)
        near[step] = hot
        first = jnp.where(b // cols == 0, first_row(rows, 0), 0)
        wanted = [3 * (first + k) + 1 for k in range(spans)]
        parts = window_hot(hot, lines(place, b, at, QUAD), wanted)
        for k in range(spans):
            onehot[k * LANES : (k + 1) * LANES, :] = parts[k]
        out[step] = dot(win[b], onehot[...]).astype(BF16)

    def body(i, _):
        pick(onehot_even, 2 * i)
        pick(onehot_odd, 2 * i + 1)
        return 0

    lax.fori_loop(0, blocks * quads // 2, body, 0)

    for copy in copies[1:]:
        copy.wait()
    hi, lo = weight_halves(w1_ref[...].T)
    line = jnp.concatenate([hi, hi, lo, lo], axis=1)
    none = jnp.zeros_like(line)
    w1s[...] = jnp.concatenate(
        [jnp.concatenate([line, none], axis=1), jnp.concatenate([none, line], axis=1)], axis=0
    ).astype(BF16)
    w2s[...] = weight_rows(w2_ref[...].T)
    wrs[...] = weight_rows(wr_ref[...].T)
    wrt[...] = weight_rows(wr_ref[...])
    units = wo_ref.shape[1]
    one = lax.broadcasted_iota(jnp.int32, (units, units), 0)
    two = lax.broadcasted_iota(jnp.int32, (units, units), 1)
    woc[...] = jnp.sum(jnp.where(one == two, wo_ref[...], 0.0), axis=1, keepdims=True)


def pack_kernel(rows, cols, feat_hbm, pos_hbm, out, pos_ref, sems):
    feats = feat_hbm.shape[2]
    copies = copied(
        [pos_hbm] + [feat_hbm.at[r, c] for r in range(rows) for c in range(cols)],
        [pos_ref] + [out.at[r, c, pl.ds(0, feats)] for r in range(rows) for c in range(cols)],
        sems,
    )
    copies[0].wait()
    for r in range(rows):
        for c in range(cols):
            rest = jnp.concatenate([pos_ref[r, i, c : c + 1, :] for i in range(3)], axis=0)
            parts = []
            for _ in range(3):
                part = rest.astype(BF16).astype(F32)
                parts.append(part)
                rest = rest - part
            parts.append(jnp.zeros((7, LANES), F32))
            out[r, c, feats:] = jnp.concatenate(parts, axis=0).astype(BF16)
    for copy in copies[1:]:
        copy.wait()


def place_of(block, feats):
    rest = block[feats : feats + 16].astype(F32)
    return rest[0:3] + rest[3:6] + rest[6:9]


def ends_kernel(rows, left_ref, right_ref, up, down):
    for out, r in ((up, rows - 1), (down, 0)):
        out[:, :LANES] = left_ref[r, 0]
        out[:, LANES:] = right_ref[r, 0]


def ghost_kernel(rows, cols, prev_ref, next_ref, near, place, xa, out):
    steps = near.shape[0]
    quads = steps // (rows * cols)
    feats = out.shape[1]
    for b in range(rows * cols):
        r, c = b // cols, b % cols

        def pick(step):
            first = (step % quads) * QUAD
            if r == 0 or r == rows - 1:
                ref, slot = (prev_ref, 1) if r == 0 else (next_ref, 7)
                hot = window_hot(near[step], lines(place, b, first, QUAD), [slot])[0]
                out[step] = xa[step] + dot(ref[0, c, :feats], hot).astype(BF16)
            else:
                out[step] = xa[step]

        def body(i, _):
            pick(b * quads + 2 * i)
            pick(b * quads + 2 * i + 1)
            return 0

        lax.fori_loop(0, quads // 2, body, 0)


def finish_kernel(
    rows, front_ref, force, ahead, vel, pos, fresh_pos, fresh_vel, new_pos, new_vel
):
    front = front_ref[0] == 1
    for r in range(rows):
        total = force[r + 2]
        if r >= rows - 2:
            total = total + ahead[r - rows + 2]
        old_vel = vel[r + 1] if r < rows - 1 else ahead[2]
        old_pos = pos[r + 1] if r < rows - 1 else ahead[3]
        v = old_vel + KICK_FACTOR * total
        p = old_pos + MOVE_FACTOR * v
        if r == rows - 1:
            v = jnp.where(front, fresh_vel[...], v)
            p = jnp.where(front, fresh_pos[...], p)
        new_vel[r] = v
        new_pos[r] = p


def local_kernel(
    rows,
    cols,
    left_ref,
    right_ref,
    own_ref,
    near,
    place,
    xa,
    out,
    win,
    hot_even,
    hot_odd,
):
    blocks = rows * cols
    steps = near.shape[0]
    quads = steps // blocks
    feats = out.shape[1]

    def columns(r, c):
        found = []
        for k in range(3):
            row = r - 1 + k
            for col in (c - 1, c, c + 1):
                slot = 3 * k + col - c + 1
                if 0 <= row < rows and col != c:
                    if col < 0:
                        found.append((slot, left_ref[row, 0, :feats]))
                    elif col >= cols:
                        found.append((slot, right_ref[row, 0, :feats]))
                    else:
                        found.append((slot, own_ref[row, col, :feats]))
        return found

    for b in range(blocks):
        found = columns(b // cols, b % cols)
        count = len(found)
        for k, (_, block) in enumerate(found):
            win[b, :, k * LANES : (k + 1) * LANES] = block

        def pick(hot, step):
            first = (step % quads) * QUAD
            parts = window_hot(near[step], lines(place, b, first, QUAD), [x for x, _ in found])
            for k in range(count):
                hot[k * LANES : (k + 1) * LANES, :] = parts[k]
            picked = dot(win[b, :, : count * LANES], hot[: count * LANES, :])
            out[step] = xa[step] + picked.astype(BF16)

        def body(i, _):
            pick(hot_even, b * quads + 2 * i)
            pick(hot_odd, b * quads + 2 * i + 1)
            return 0

        lax.fori_loop(0, quads // 2, body, 0)


RING = 3


def energy_kernel(
    rows,
    cols,
    channels,
    slots,
    prev_ref,
    next_ref,
    prev_own_ref,
    next_own_ref,
    own_ref,
    left_ref,
    right_ref,
    codes_hbm,
    counts_hbm,
    near,
    w1s,
    w2s,
    wrs,
    wrt,
    woc,
    xl_hbm,
    en_ref,
    fleft_ref,
    fown_ref,
    fright_ref,
    force_ref,
    pos_ref,
    codes_ref,
    counts_ref,
    geo,
    har,
    win,
    xl,
    xg_even,
    xg_odd,
    w_even,
    w_odd,
    d_even,
    d_odd,
    held_even,
    held_odd,
    acc,
    inv,
    dys,
    lhs,
    sems,
    xsem,
    *,
    stream,
):
    blocks = rows * cols
    quads = slots // QUAD
    steps = blocks * quads
    wide = QUAD * LANES
    group = 8
    feats = 9 * channels
    root3, root5, root15 = math.sqrt(3.0), math.sqrt(5.0), math.sqrt(15.0)
    even, odd = (xg_even, w_even, d_even, held_even), (xg_odd, w_odd, d_odd, held_odd)

    def x_copy(step):
        at = step % RING
        return pltpu.make_async_copy(xl_hbm.at[step], xl.at[at], xsem.at[at])

    copies = copied([codes_hbm, counts_hbm], [codes_ref, counts_ref], sems)
    if stream:
        for i in range(RING):
            x_copy(i).start()

    for side, middle, r in ((prev_ref, prev_own_ref, 0), (next_ref, next_own_ref, rows + 1)):
        pos_ref[r, 0] = place_of(side[:, :LANES], feats)
        pos_ref[r, cols + 1] = place_of(side[:, LANES:], feats)
        for c in range(cols):
            pos_ref[r, c + 1] = place_of(middle[0, c], feats)
    for r in range(rows):
        pos_ref[r + 1, 0] = place_of(left_ref[r, 0], feats)
        pos_ref[r + 1, cols + 1] = place_of(right_ref[r, 0], feats)
        for c in range(cols):
            pos_ref[r + 1, c + 1] = place_of(own_ref[r, c], feats)
            none = jnp.zeros((feats, LANES), BF16)
            ref = prev_ref if r == 0 else next_ref
            ends = r == 0 or r == rows - 1
            b = r * cols + c
            win[b, :, :LANES] = ref[:feats, :LANES] if ends and c == 0 else none
            win[b, :, LANES:] = ref[:feats, LANES:] if ends and c == cols - 1 else none
    acc[...] = jnp.zeros(acc.shape, F32)
    for copy in copies:
        copy.wait()

    def geometry(b, _):
        r, c = b // cols, b % cols
        zq, near_block, atom = decoded(codes_ref[r, c])
        row3 = (near_block >= 3).astype(jnp.int32) + (near_block >= 6).astype(jnp.int32)
        shift_x = (row3 - 1).astype(F32) * BLOCK_LENGTH
        shift_y = (near_block - 3 * row3 - 1).astype(F32) * BLOCK_LENGTH
        shift_z = (zq - 1).astype(F32) * BLOCK_LENGTH
        centre = pos_ref[r + 1, c + 1]
        found = [jnp.zeros((slots, LANES), F32) for _ in range(3)]
        for k in range(9):
            place = pos_ref[r + k // 3, c + k % 3]
            here = near_block == k
            for i in range(3):
                line = jnp.broadcast_to(place[i : i + 1], (slots, LANES))
                value = jnp.take_along_axis(line, atom, axis=1, mode="promise_in_bounds")
                found[i] = jnp.where(here, value, found[i])
        rx = found[0] + shift_x - centre[0:1]
        ry = found[1] + shift_y - centre[1:2]
        rz = found[2] + shift_z - centre[2:3]
        dist = jnp.sqrt(rx * rx + ry * ry + rz * rz)
        recip = 1.0 / dist
        ux, uy, uz = rx * recip, ry * recip, rz * recip
        x = dist * (1.0 / CUTOFF_RADIUS)
        x2 = x * x
        x5 = x2 * x2 * x
        live = lax.broadcasted_iota(jnp.int32, (slots, LANES), 0) < counts_ref[r, c]
        scale = jnp.where(live, 1.0 / slots, 0.0)
        env = (1.0 - x5 * x * (28.0 - x * (48.0 - 21.0 * x))) * scale
        denv = (-168.0 / CUTOFF_RADIUS) * x5 * (1.0 - x * (2.0 - x)) * scale
        geo[b, 0] = dist
        geo[b, 1] = recip
        geo[b, 2] = env
        geo[b, 3] = denv
        geo[b, 4] = ux
        geo[b, 5] = uy
        geo[b, 6] = uz
        geo[b, 7] = near_block.astype(F32)
        har[b, 0] = root3 * ux
        har[b, 1] = root3 * uy
        har[b, 2] = root3 * uz
        har[b, 3] = root15 * ux * uy
        har[b, 4] = root15 * uy * uz
        har[b, 5] = 0.5 * root5 * (3.0 * uz * uz - 1.0)
        har[b, 6] = root15 * ux * uz
        har[b, 7] = 0.5 * root15 * (ux * ux - uy * uy)
        return 0

    lax.fori_loop(0, blocks, geometry, 0)

    def hidden_rows(buffers, step):
        held = buffers[3]
        b, first = step // quads, (step % quads) * QUAD
        dist, recip, env, denv = [joined(geo, b, k, first, QUAD) for k in range(4)]
        order = (lax.broadcasted_iota(jnp.int32, (8, wide), 0) + 1).astype(F32)
        sin, cos = sin_cos_half_turns(order * (dist * (1.0 / CUTOFF_RADIUS)))
        norm = math.sqrt(2.0 / CUTOFF_RADIUS)
        basis = norm * sin * recip
        slope = ((norm * math.pi / CUTOFF_RADIUS) * order * cos - basis) * recip
        split = []
        for x in (basis, slope):
            hi = x.astype(BF16).astype(F32)
            split += [hi, x - hi] * 2
        pre2 = dot(w1s[...], jnp.concatenate(split, axis=0).astype(BF16))
        pre, dpre = pre2[: pre2.shape[0] // 2], pre2[pre2.shape[0] // 2 :]
        gate = 1.0 / (1.0 + jnp.exp(-pre))
        h = pre * gate
        dh = gate + h * (1.0 - gate)
        held[0] = value_rows(h * env)
        held[1] = value_rows(dh * dpre * env + h * denv)

    def radial_rows(buffers, step):
        _, wsc, dsc, held = buffers
        wsc[step // 2] = dot(w2s[...], held[0])
        dsc[step // 2] = dot(w2s[...], held[1])

    def gather(buffers, step):
        b, first = step // quads, (step % quads) * QUAD
        r = b // cols
        k0 = jnp.where(r == 0, 0, jnp.where(r == rows - 1, 6, 9))
        parts = window_hot(near[step], joined(geo, b, 7, first, QUAD), [k0, k0 + 2])
        if stream:
            x_copy(step).wait()
            held = xl[step % RING]
        else:
            held = xl_hbm[step]
        buffers[0][step // 2] = held.astype(F32) + dot(win[b], jnp.concatenate(parts, axis=0))

    def collect(buffers, step):
        xg, wsc = buffers[:2]
        b, first = step // quads, (step % quads) * QUAD
        for g in range(channels // group):
            at = g * group
            total = [acc[b, m, at : at + group, :] for m in range(9)]
            for s in range(QUAD):
                ln = slice(s * LANES, (s + 1) * LANES)
                xs = [
                    xg[step // 2, m * channels + at : m * channels + at + group, ln]
                    for m in range(9)
                ]
                w0, w1, w2 = [
                    wsc[step // 2, k * channels + at : k * channels + at + group, ln]
                    for k in range(3)
                ]
                ys = [har[b, m, pl.ds(first + s, 1), :] for m in range(8)]
                t0 = w0 * xs[0]
                vec = xs[1] * ys[0] + xs[2] * ys[1] + xs[3] * ys[2]
                total[0] = total[0] + (t0 + w1 * xs[0]) + w2 * vec
                for m in range(1, 9):
                    total[m] = total[m] + (t0 * ys[m - 1] + w1 * xs[m])
            for m in range(9):
                acc[b, m, at : at + group, :] = total[m]

    def advance(new, old, step, last=False):
        collect(old, step - 1)
        if not last:
            hidden_rows(old, step + 1)
        gather(new, step)
        radial_rows(new, step)
        if stream:

            @pl.when(step + RING - 1 < steps)
            def _():
                x_copy(step + RING - 1).start()

    def forward(i, _):
        advance(even, odd, 2 * i)
        advance(odd, even, 2 * i + 1)
        return 0

    hidden_rows(even, 0)
    hidden_rows(odd, 1)
    radial_rows(even, 0)
    gather(even, 0)
    advance(odd, even, 1)
    lax.fori_loop(1, steps // 2 - 1, forward, 0)
    advance(even, odd, steps - 2)
    advance(odd, even, steps - 1, last=True)
    collect(odd, steps - 1)

    for b in range(blocks):
        ln = slice(b * LANES, (b + 1) * LANES)
        a = [acc[b, m] for m in range(9)]
        inv[0:channels, ln] = a[0] * a[0]
        inv[channels : 2 * channels, ln] = a[1] * a[1] + a[2] * a[2] + a[3] * a[3]
        inv[2 * channels :, ln] = (
            a[4] * a[4] + a[5] * a[5] + a[6] * a[6] + a[7] * a[7] + a[8] * a[8]
        )
    z = dot(wrs[...], value_rows(inv[...]))
    gate = 1.0 / (1.0 + jnp.exp(-z))
    out = z * gate
    wo = woc[...]
    energy = jnp.sum(out * wo, axis=0, keepdims=True)
    dinv = dot(wrt[...], value_rows(wo * (gate + out * (1.0 - gate))))
    for b in range(blocks):
        ln = slice(b * LANES, (b + 1) * LANES)
        en_ref[b // cols, b % cols] = energy[:, ln]
        for m in range(9):
            part = 0 if m == 0 else (1 if m < 4 else 2)
            d = dinv[part * channels : (part + 1) * channels, ln]
            acc[b, m] = 2.0 * acc[b, m] * d

    def edge_terms(buffers, step):
        xg, wsc, dsc = buffers[:3]
        b, first = step // quads, (step % quads) * QUAD
        for s in range(QUAD):
            ln = slice(s * LANES, (s + 1) * LANES)
            ys = [har[b, m, pl.ds(first + s, 1), :] for m in range(8)]
            dy = [jnp.zeros((group, LANES), F32) for _ in range(9)]
            for g in range(channels // group):
                at = g * group
                xs = [
                    xg[step // 2, m * channels + at : m * channels + at + group, ln]
                    for m in range(9)
                ]
                gs = [acc[b, m, at : at + group, :] for m in range(9)]
                w0 = wsc[step // 2, at : at + group, ln]
                w2 = wsc[step // 2, 2 * channels + at : 2 * channels + at + group, ln]
                d0, d1, d2 = [
                    dsc[step // 2, k * channels + at : k * channels + at + group, ln]
                    for k in range(3)
                ]
                t0 = w0 * xs[0]
                t2 = w2 * gs[0]
                vec = xs[1] * ys[0] + xs[2] * ys[1] + xs[3] * ys[2]
                along = gs[0]
                direct = gs[0] * xs[0]
                for m in range(1, 9):
                    along = along + gs[m] * ys[m - 1]
                    direct = direct + gs[m] * xs[m]
                    dy[m - 1] = dy[m - 1] + t0 * gs[m]
                    if m < 4:
                        dy[m - 1] = dy[m - 1] + t2 * xs[m]
                dy[8] = dy[8] + (d0 * xs[0] * along + d1 * direct + d2 * gs[0] * vec)
            for m in range(9):
                dys[b, m, pl.ds(first + s, 1), :] = jnp.sum(dy[m], axis=0, keepdims=True)

    def backward(i, _):
        edge_terms(even, 2 * i)
        edge_terms(odd, 2 * i + 1)
        return 0

    lax.fori_loop(0, steps // 2, backward, 0)
    force_ref[...] = jnp.zeros(force_ref.shape, F32)

    def pull(b, _):
        r, c = b // cols, b % cols
        ux, uy, uz, recip = geo[b, 4], geo[b, 5], geo[b, 6], geo[b, 1]
        d1, d2, d3, d4, d5, d6, d7, d8 = [dys[b, m] for m in range(8)]
        gx = root3 * d1 + root15 * (uy * d4 + uz * d7 + ux * d8)
        gy = root3 * d2 + root15 * (ux * d4 + uz * d5 - uy * d8)
        gz = root3 * d3 + root15 * (uy * d5 + ux * d7) + (3.0 * root5) * uz * d6
        radial = dys[b, 8] - (ux * gx + uy * gy + uz * gz) * recip
        grads = [gx * recip + ux * radial, gy * recip + uy * radial, gz * recip + uz * radial]
        for i in range(3):
            here = jnp.sum(grads[i], axis=0, keepdims=True)
            force_ref[r + 1, c + 1, i : i + 1, :] += here
        split = [halves(g) for g in grads]
        which = lax.broadcasted_iota(jnp.int32, (16, LANES), 0).astype(F32)
        place = geo[b, 7]
        for n in range(slots):
            ln = slice(n * LANES, (n + 1) * LANES)
            hit = which == place[n : n + 1]
            for i in range(3):
                for v in range(2):
                    line = split[i][v][n : n + 1].astype(F32)
                    at = (3 * v + i) * 16
                    lhs[at : at + 16, ln] = jnp.where(hit, line, 0.0).astype(BF16)
        total = jnp.zeros((96, LANES), F32)
        for p in range(quads):
            total = total + lax.dot_general(
                lhs[:, p * wide : (p + 1) * wide],
                near[b * quads + p],
                (((1,), (1,)), ((), ())),
                preferred_element_type=F32,
            )
        for i in range(3):
            for k in range(9):
                at = i * 16 + k
                value = total[at : at + 1] + total[48 + at : 49 + at]
                force_ref[r + k // 3, c + k % 3, i : i + 1, :] -= value
        return 0

    lax.fori_loop(0, blocks, pull, 0)
    for r in range(rows + 2):
        for i in range(3):
            fleft_ref[r, i] = force_ref[r, 0:1, i, :]
            fright_ref[r, i] = force_ref[r, cols + 1 :, i, :]
            fown_ref[r, i] = force_ref[r, 1 : cols + 1, i, :]


def vmem_call(body, name, ins, out_shape, scratch, limit, flops):
    vmem = pl.BlockSpec(memory_space=pltpu.VMEM)
    return pl.pallas_call(
        body,
        out_shape=out_shape,
        in_specs=ins,
        out_specs=[vmem] * len(out_shape),
        scratch_shapes=scratch,
        compiler_params=pltpu.CompilerParams(vmem_limit_bytes=limit * 1024 * 1024),
        cost_estimate=pl.CostEstimate(flops=flops, bytes_accessed=1024 * 1024, transcendentals=0),
        name=name,
    )


def pinned(*args):
    return [pltpu.with_memory_space_constraint(x, pltpu.HBM) for x in args]


def prepare_part(own, feats, neighbours, w_first, w_second, w_read, w_out):
    rows, cols, slots = neighbours.shape[0], neighbours.shape[1], neighbours.shape[2]
    hidden, basis = w_first.shape
    units, reads = w_read.shape
    weights = w_second.shape[0]
    blocks, steps, wide = rows * cols, rows * cols * slots // QUAD, QUAD * LANES
    spans = min(rows, 3)
    vmem = pl.BlockSpec(memory_space=pltpu.VMEM)
    hbm = pl.BlockSpec(memory_space=pltpu.HBM)
    sds = jax.ShapeDtypeStruct
    call = vmem_call(
        functools.partial(prepare_kernel, rows, cols, slots),
        "prepare",
        [vmem] + [hbm] * 5,
        [
            sds((steps, LANES, wide), BF16),
            sds((blocks, slots, LANES), F32),
            sds((2 * hidden, 8 * basis), BF16),
            sds((weights, 3 * hidden), BF16),
            sds((units, 3 * reads), BF16),
            sds((reads, 3 * units), BF16),
            sds((units, 1), F32),
            sds((steps, feats, wide), BF16),
        ],
        [
            pltpu.VMEM(neighbours.shape, jnp.int32),
            pltpu.VMEM((basis, hidden), F32),
            pltpu.VMEM((hidden, weights), F32),
            pltpu.VMEM((reads, units), F32),
            pltpu.VMEM((1, units), F32),
            pltpu.VMEM((blocks, slots, LANES), F32),
            pltpu.VMEM((blocks, feats, spans * LANES), BF16),
            pltpu.VMEM((spans * LANES, wide), BF16),
            pltpu.VMEM((spans * LANES, wide), BF16),
            pltpu.SemaphoreType.DMA((5,)),
        ],
        16,
        2 * feats * spans * LANES * steps * wide,
    )
    return call(
        own, *pinned(neighbours, w_first.T, w_second.T, w_read.T, w_out.reshape(1, units))
    )


def pack_part(features, pos):
    rows, cols, feats, _ = features.shape
    vmem = pl.BlockSpec(memory_space=pltpu.VMEM)
    hbm = pl.BlockSpec(memory_space=pltpu.HBM)
    call = vmem_call(
        functools.partial(pack_kernel, rows, cols),
        "pack",
        [hbm] * 2,
        [jax.ShapeDtypeStruct((rows, cols, feats + 16, LANES), BF16)],
        [pltpu.VMEM(pos.shape, F32), pltpu.SemaphoreType.DMA((1 + rows * cols,))],
        2,
        1000000,
    )
    return call(*pinned(features, pos))[0]


def ends_part(left, right):
    vmem = pl.BlockSpec(memory_space=pltpu.VMEM)
    message = jax.ShapeDtypeStruct((left.shape[2], 2 * LANES), BF16)
    call = vmem_call(
        functools.partial(ends_kernel, left.shape[0]),
        "ends",
        [vmem] * 2,
        [message] * 2,
        [],
        2,
        1000000,
    )
    return call(left, right)


def ghost_part(before, after, near, place, xa, rows, cols):
    vmem = pl.BlockSpec(memory_space=pltpu.VMEM)
    steps, feats, wide = xa.shape
    call = vmem_call(
        functools.partial(ghost_kernel, rows, cols),
        "ghost",
        [vmem] * 5,
        [jax.ShapeDtypeStruct(xa.shape, BF16)],
        [],
        8,
        2 * feats * LANES * steps * wide,
    )
    return call(before, after, near, place, xa)[0]


def finish_part(front, force, ahead, vel, pos, fresh_pos, fresh_vel):
    vmem = pl.BlockSpec(memory_space=pltpu.VMEM)
    smem = pl.BlockSpec(memory_space=pltpu.SMEM)
    call = vmem_call(
        functools.partial(finish_kernel, vel.shape[0]),
        "finish",
        [smem] + [vmem] * 6,
        [jax.ShapeDtypeStruct(vel.shape, F32)] * 2,
        [],
        2,
        100000,
    )
    return call(front, force, ahead, vel, pos, fresh_pos, fresh_vel)


def local_part(left, right, own, near, place, xa):
    rows, cols, feats = own.shape[0], own.shape[1], xa.shape[1]
    steps, _, wide = near.shape
    most = 2 * min(rows, 3)
    vmem = pl.BlockSpec(memory_space=pltpu.VMEM)
    call = vmem_call(
        functools.partial(local_kernel, rows, cols),
        "local",
        [vmem] * 6,
        [jax.ShapeDtypeStruct((steps, feats, wide), BF16)],
        [
            pltpu.VMEM((rows * cols, feats, most * LANES), BF16),
            pltpu.VMEM((most * LANES, wide), BF16),
            pltpu.VMEM((most * LANES, wide), BF16),
        ],
        16,
        2 * feats * most * LANES * steps * wide,
    )
    return call(left, right, own, near, place, xa)[0]


def energy_part(ghosts, own, left, right, neighbours, counts, prepared, gathered):
    near, place, w1s, w2s, wrs, wrt, woc = prepared[:7]
    rows, cols, slots = neighbours.shape[0], neighbours.shape[1], neighbours.shape[2]
    steps, _, wide = near.shape
    weights = w2s.shape[0]
    channels, blocks, feats = weights // 3, rows * cols, gathered.shape[1]
    vmem = pl.BlockSpec(memory_space=pltpu.VMEM)
    hbm = pl.BlockSpec(memory_space=pltpu.HBM)
    sds = jax.ShapeDtypeStruct
    side = sds((rows + 2, 3, 1, LANES), F32)
    stream = blocks > 2
    half = steps // 2
    call = vmem_call(
        functools.partial(energy_kernel, rows, cols, channels, slots, stream=stream),
        "energy",
        [vmem] * 7 + [hbm] * 2 + [vmem] * 6 + [hbm if stream else vmem],
        [sds((rows, cols, 1, LANES), F32), side, sds((rows + 2, 3, cols, LANES), F32), side],
        [
            pltpu.VMEM((rows + 2, cols + 2, 3, LANES), F32),
            pltpu.VMEM((rows + 2, cols + 2, 3, LANES), F32),
            pltpu.VMEM((rows, cols, slots, LANES), jnp.int32),
            pltpu.VMEM((rows, cols, 1, LANES), jnp.int32),
            pltpu.VMEM((blocks, 8, slots, LANES), F32),
            pltpu.VMEM((blocks, 8, slots, LANES), F32),
            pltpu.VMEM((blocks, feats, 2 * LANES), BF16),
            pltpu.VMEM((RING, feats, wide) if stream else (1, 16, LANES), BF16),
            pltpu.VMEM((half, feats, wide), F32),
            pltpu.VMEM((half, feats, wide), F32),
            pltpu.VMEM((half, weights, wide), F32),
            pltpu.VMEM((half, weights, wide), F32),
            pltpu.VMEM((half, weights, wide), F32),
            pltpu.VMEM((half, weights, wide), F32),
            pltpu.VMEM((2, 3 * (w1s.shape[0] // 2), wide), BF16),
            pltpu.VMEM((2, 3 * (w1s.shape[0] // 2), wide), BF16),
            pltpu.VMEM((blocks, 9, channels, LANES), F32),
            pltpu.VMEM((weights, blocks * LANES), F32),
            pltpu.VMEM((blocks, 9, slots, LANES), F32),
            pltpu.VMEM((96, slots * LANES), BF16),
            pltpu.SemaphoreType.DMA((2,)),
            pltpu.SemaphoreType.DMA((RING,)),
        ],
        56 if stream else 32,
        2 * feats * 9 * LANES * steps * wide,
    )
    energies, f_left, f_own, f_right = call(
        *ghosts,
        own,
        left,
        right,
        *pinned(neighbours, counts.reshape(rows, cols, 1, LANES)),
        near,
        w1s,
        w2s,
        wrs,
        wrt,
        woc,
        gathered,
    )
    return f_left, f_own, f_right, energies.reshape(rows, cols, LANES)


def local(
    positions,
    velocities,
    features,
    neighbours,
    counts,
    w_first,
    w_second,
    w_read,
    w_out,
    fresh_positions,
    fresh_velocities,
):
    nrows, ncols = (positions.shape[0], positions.shape[1])
    shock_place = lax.axis_index("shock")
    front = lax.axis_size("shock") - 1
    assert nrows >= 2 and neighbours.shape[2] % (2 * QUAD) == 0

    def sides(x, axis):
        last = lax.slice_in_dim(x, ncols - 1, ncols, axis=axis)
        first = lax.slice_in_dim(x, 0, 1, axis=axis)
        return shifted(last, "trans", 1), shifted(first, "trans", -1)

    pos = positions.transpose(0, 2, 1, 3)
    vel = velocities.transpose(0, 2, 1, 3)
    own = pack_part(features, pos)
    left, right = sides(own, 1)
    before = passed_along(own[nrows - 1 :], "shock", 1)
    after = passed_along(own[:1], "shock", -1)
    feats = features.shape[2]
    prepared = prepare_part(own, feats, neighbours, w_first, w_second, w_read, w_out)
    near, place, xa = prepared[0], prepared[1], prepared[7]
    xa = ghost_part(before, after, near, place, xa, nrows, ncols)
    left, right, xa = lax.optimization_barrier((left, right, xa))
    last, first = ends_part(left, right)
    ghosts = (
        passed_along(last, "shock", 1),
        passed_along(first, "shock", -1),
        before,
        after,
    )
    gathered = local_part(left, right, own, near, place, xa)
    f_left, f_own, f_right, energies = energy_part(
        ghosts, own, left, right, neighbours, counts, prepared, gathered
    )
    from_right = shifted(f_left, "trans", -1)
    from_left = shifted(f_right, "trans", 1)
    folded = f_own.at[:, :, ncols - 1].add(from_right[:, :, 0])
    folded = folded.at[:, :, 0].add(from_left[:, :, 0])
    packed = jnp.concatenate([folded[:2], vel[:1], pos[:1]], axis=0)
    ahead = passed_along(packed, "shock", -1)
    at_front = (shock_place == front).astype(jnp.int32).reshape(1)
    new_positions, new_velocities = finish_part(
        at_front,
        folded,
        ahead,
        vel,
        pos,
        fresh_positions.transpose(1, 0, 2),
        fresh_velocities.transpose(1, 0, 2),
    )
    return (energies, new_positions.transpose(0, 2, 1, 3), new_velocities.transpose(0, 2, 1, 3))


def solution(mesh):
    return jax.shard_map(
        local,
        mesh=mesh,
        in_specs=(
            P("shock", "trans", None, None),
            P("shock", "trans", None, None),
            P("shock", "trans", None, None),
            P("shock", "trans", None, None),
            P("shock", "trans", None),
            P(),
            P(),
            P(),
            P(),
            P("trans", None, None),
            P("trans", None, None),
        ),
        out_specs=(
            P("shock", "trans", None),
            P("shock", "trans", None, None),
            P("shock", "trans", None, None),
        ),
        check_vma=False,
    )
```

```python
import functools
import math

import jax
import jax.numpy as jnp
from jax import lax
from jax.experimental import pallas as pl
from jax.experimental.pallas import tpu as pltpu
from jax.sharding import PartitionSpec as P

CUTOFF_RADIUS = 9.5
BLOCK_LENGTH = 13.2
KICK_FACTOR = 4.0
MOVE_FACTOR = 0.5
F32 = jnp.float32
BF16 = jnp.bfloat16
LANES = 128
QUAD = 4


def shifted(x, axis, by):
    count = lax.axis_size(axis)
    return lax.ppermute(x, axis, [(i, (i + by) % count) for i in range(count)])


def passed_along(block, axis, distance):
    devices = range(lax.axis_size(axis))
    route = [(i - distance, i) for i in devices if i - distance in devices]
    return lax.ppermute(block, axis, route)


def halves(x):
    hi = x.astype(BF16)
    lo = (x - hi.astype(F32)).astype(BF16)
    return hi, lo


def value_rows(x):
    hi, lo = halves(x)
    return jnp.concatenate([hi, lo, hi], axis=0)


def dot(a, b):
    return jnp.dot(a, b, preferred_element_type=F32)


def sin_cos_half_turns(t):
    n = jnp.floor(t + 0.5)
    r = t - n
    odd = n - 2.0 * jnp.floor(0.5 * n)
    sign = 1.0 - 2.0 * odd
    x = math.pi * r
    y = x * x
    s = 1.0 + y * (
        -1.0 / 6
        + y
        * (
            1.0 / 120
            + y * (-1.0 / 5040 + y * (1.0 / 362880 + y * (-1.0 / 39916800 + y * (1.0 / 6227020800.0))))
        )
    )
    c = 1.0 + y * (
        -0.5
        + y
        * (
            1.0 / 24
            + y
            * (-1.0 / 720 + y * (1.0 / 40320 + y * (-1.0 / 3628800 + y * (1.0 / 479001600.0))))
        )
    )
    return sign * x * s, sign * c


def weight_halves(w):
    hi = w.astype(BF16).astype(F32)
    return hi, w - hi


def weight_rows(w):
    hi, lo = weight_halves(w)
    return jnp.concatenate([hi, hi, lo], axis=1).astype(BF16)


def joined(ref, b, k, first, count):
    lines = [ref[b, k, pl.ds(first + s, 1), :] for s in range(count)]
    return jnp.concatenate(lines, axis=1)


def lines(ref, b, first, count):
    return jnp.concatenate([ref[b, pl.ds(first + s, 1), :] for s in range(count)], axis=1)


def first_row(rows, r):
    return 1 if (rows == 2 and r == 0) else 0


def window_hot(near, place, wanted):
    lanes = near.shape[1]
    near3 = near.reshape(LANES // 16, 16, lanes)
    parts = []
    for k in wanted:
        mask = jnp.where(place == jnp.asarray(k).astype(F32), 1.0, 0.0)
        mask = jnp.broadcast_to(mask, (16, lanes)).astype(BF16)
        parts.append((near3 * mask[None]).reshape(LANES, lanes))
    return parts


def decoded(codes):
    zq = (codes >= 1152).astype(jnp.int32) + (codes >= 2304).astype(jnp.int32)
    slot = codes - 1152 * zq
    return zq, lax.shift_right_logical(slot, 7), slot & 127


def copied(sources, places, sems):
    copies = [
        pltpu.make_async_copy(x, y, sems.at[i]) for i, (x, y) in enumerate(zip(sources, places))
    ]
    for copy in copies:
        copy.start()
    return copies


def prepare_kernel(
    rows,
    cols,
    slots,
    own_ref,
    codes_hbm,
    w1_hbm,
    w2_hbm,
    wr_hbm,
    wo_hbm,
    near,
    place,
    w1s,
    w2s,
    wrs,
    wrt,
    woc,
    out,
    codes_ref,
    w1_ref,
    w2_ref,
    wr_ref,
    wo_ref,
    atoms,
    win,
    onehot_even,
    onehot_odd,
    sems,
):
    blocks = rows * cols
    quads = slots // QUAD
    wide = QUAD * LANES
    spans = win.shape[2] // LANES
    copies = copied(
        [codes_hbm, w1_hbm, w2_hbm, wr_hbm, wo_hbm],
        [codes_ref, w1_ref, w2_ref, wr_ref, wo_ref],
        sems,
    )
    copies[0].wait()
    for r in range(rows):
        for c in range(cols):
            _, block, atom = decoded(codes_ref[r, c])
            place[r * cols + c] = block.astype(F32)
            atoms[r * cols + c] = atom.astype(F32)
    feats = win.shape[1]
    for r in range(rows):
        first = first_row(rows, r)
        for c in range(cols):
            for k in range(spans):
                ln = slice(k * LANES, (k + 1) * LANES)
                if 0 <= r - 1 + first + k < rows:
                    win[r * cols + c, :, ln] = own_ref[r - 1 + first + k, c, :feats]
                else:
                    win[r * cols + c, :, ln] = jnp.zeros((feats, LANES), BF16)

    def pick(onehot, step):
        b, at = step // quads, (step % quads) * QUAD
        atom = lines(atoms, b, at, QUAD)
        sub = lax.broadcasted_iota(jnp.int32, (LANES, wide), 0).astype(F32)
        hot = jnp.where(sub == atom, 1.0, 0.0).astype(BF16)
        near[step] = hot
        first = jnp.where(b // cols == 0, first_row(rows, 0), 0)
        wanted = [3 * (first + k) + 1 for k in range(spans)]
        parts = window_hot(hot, lines(place, b, at, QUAD), wanted)
        for k in range(spans):
            onehot[k * LANES : (k + 1) * LANES, :] = parts[k]
        out[step] = dot(win[b], onehot[...]).astype(BF16)

    def body(i, _):
        pick(onehot_even, 2 * i)
        pick(onehot_odd, 2 * i + 1)
        return 0

    lax.fori_loop(0, blocks * quads // 2, body, 0)

    for copy in copies[1:]:
        copy.wait()
    hi, lo = weight_halves(w1_ref[...].T)
    line = jnp.concatenate([hi, hi, lo, lo], axis=1)
    none = jnp.zeros_like(line)
    w1s[...] = jnp.concatenate(
        [jnp.concatenate([line, none], axis=1), jnp.concatenate([none, line], axis=1)], axis=0
    ).astype(BF16)
    w2s[...] = weight_rows(w2_ref[...].T)
    wrs[...] = weight_rows(wr_ref[...].T)
    wrt[...] = weight_rows(wr_ref[...])
    units = wo_ref.shape[1]
    one = lax.broadcasted_iota(jnp.int32, (units, units), 0)
    two = lax.broadcasted_iota(jnp.int32, (units, units), 1)
    woc[...] = jnp.sum(jnp.where(one == two, wo_ref[...], 0.0), axis=1, keepdims=True)


def pack_kernel(rows, cols, feat_hbm, pos_hbm, out, pos_ref, sems):
    feats = feat_hbm.shape[2]
    copies = copied(
        [pos_hbm] + [feat_hbm.at[r, c] for r in range(rows) for c in range(cols)],
        [pos_ref] + [out.at[r, c, pl.ds(0, feats)] for r in range(rows) for c in range(cols)],
        sems,
    )
    copies[0].wait()
    for r in range(rows):
        for c in range(cols):
            rest = jnp.concatenate([pos_ref[r, i, c : c + 1, :] for i in range(3)], axis=0)
            parts = []
            for _ in range(3):
                part = rest.astype(BF16).astype(F32)
                parts.append(part)
                rest = rest - part
            parts.append(jnp.zeros((7, LANES), F32))
            out[r, c, feats:] = jnp.concatenate(parts, axis=0).astype(BF16)
    for copy in copies[1:]:
        copy.wait()


def place_of(block, feats):
    rest = block[feats : feats + 16].astype(F32)
    return rest[0:3] + rest[3:6] + rest[6:9]


def ends_kernel(rows, left_ref, right_ref, up, down):
    for out, r in ((up, rows - 1), (down, 0)):
        out[:, :LANES] = left_ref[r, 0]
        out[:, LANES:] = right_ref[r, 0]


def ghost_kernel(rows, cols, prev_ref, next_ref, near, place, xa, out):
    steps = near.shape[0]
    quads = steps // (rows * cols)
    feats = out.shape[1]
    for b in range(rows * cols):
        r, c = b // cols, b % cols

        def pick(step):
            first = (step % quads) * QUAD
            if r == 0 or r == rows - 1:
                ref, slot = (prev_ref, 1) if r == 0 else (next_ref, 7)
                hot = window_hot(near[step], lines(place, b, first, QUAD), [slot])[0]
                out[step] = xa[step] + dot(ref[0, c, :feats], hot).astype(BF16)
            else:
                out[step] = xa[step]

        def body(i, _):
            pick(b * quads + 2 * i)
            pick(b * quads + 2 * i + 1)
            return 0

        lax.fori_loop(0, quads // 2, body, 0)


def finish_kernel(
    rows, front_ref, force, ahead, vel, pos, fresh_pos, fresh_vel, new_pos, new_vel
):
    front = front_ref[0] == 1
    for r in range(rows):
        total = force[r + 2]
        if r >= rows - 2:
            total = total + ahead[r - rows + 2]
        old_vel = vel[r + 1] if r < rows - 1 else ahead[2]
        old_pos = pos[r + 1] if r < rows - 1 else ahead[3]
        v = old_vel + KICK_FACTOR * total
        p = old_pos + MOVE_FACTOR * v
        if r == rows - 1:
            v = jnp.where(front, fresh_vel[...], v)
            p = jnp.where(front, fresh_pos[...], p)
        new_vel[r] = v
        new_pos[r] = p


def local_kernel(
    rows,
    cols,
    left_ref,
    right_ref,
    own_ref,
    near,
    place,
    xa,
    out,
    win,
    hot_even,
    hot_odd,
):
    blocks = rows * cols
    steps = near.shape[0]
    quads = steps // blocks
    feats = out.shape[1]

    def columns(r, c):
        found = []
        for k in range(3):
            row = r - 1 + k
            for col in (c - 1, c, c + 1):
                slot = 3 * k + col - c + 1
                if 0 <= row < rows and col != c:
                    if col < 0:
                        found.append((slot, left_ref[row, 0, :feats]))
                    elif col >= cols:
                        found.append((slot, right_ref[row, 0, :feats]))
                    else:
                        found.append((slot, own_ref[row, col, :feats]))
        return found

    for b in range(blocks):
        found = columns(b // cols, b % cols)
        count = len(found)
        for k, (_, block) in enumerate(found):
            win[b, :, k * LANES : (k + 1) * LANES] = block

        def pick(hot, step):
            first = (step % quads) * QUAD
            parts = window_hot(near[step], lines(place, b, first, QUAD), [x for x, _ in found])
            for k in range(count):
                hot[k * LANES : (k + 1) * LANES, :] = parts[k]
            picked = dot(win[b, :, : count * LANES], hot[: count * LANES, :])
            out[step] = xa[step] + picked.astype(BF16)

        def body(i, _):
            pick(hot_even, b * quads + 2 * i)
            pick(hot_odd, b * quads + 2 * i + 1)
            return 0

        lax.fori_loop(0, quads // 2, body, 0)


RING = 3


def energy_kernel(
    rows,
    cols,
    channels,
    slots,
    prev_ref,
    next_ref,
    prev_own_ref,
    next_own_ref,
    own_ref,
    left_ref,
    right_ref,
    codes_hbm,
    counts_hbm,
    near,
    w1s,
    w2s,
    wrs,
    wrt,
    woc,
    xl_hbm,
    en_ref,
    fleft_ref,
    fown_ref,
    fright_ref,
    force_ref,
    pos_ref,
    codes_ref,
    counts_ref,
    geo,
    har,
    win,
    xl,
    xg_even,
    xg_odd,
    w_even,
    w_odd,
    d_even,
    d_odd,
    held_even,
    held_odd,
    acc,
    inv,
    dys,
    lhs,
    sems,
    xsem,
    *,
    stream,
):
    blocks = rows * cols
    quads = slots // QUAD
    steps = blocks * quads
    wide = QUAD * LANES
    group = 8
    feats = 9 * channels
    root3, root5, root15 = math.sqrt(3.0), math.sqrt(5.0), math.sqrt(15.0)
    even, odd = (xg_even, w_even, d_even, held_even), (xg_odd, w_odd, d_odd, held_odd)

    def x_copy(step):
        at = step % RING
        return pltpu.make_async_copy(xl_hbm.at[step], xl.at[at], xsem.at[at])

    copies = copied([codes_hbm, counts_hbm], [codes_ref, counts_ref], sems)
    if stream:
        for i in range(RING):
            x_copy(i).start()

    for side, middle, r in ((prev_ref, prev_own_ref, 0), (next_ref, next_own_ref, rows + 1)):
        pos_ref[r, 0] = place_of(side[:, :LANES], feats)
        pos_ref[r, cols + 1] = place_of(side[:, LANES:], feats)
        for c in range(cols):
            pos_ref[r, c + 1] = place_of(middle[0, c], feats)
    for r in range(rows):
        pos_ref[r + 1, 0] = place_of(left_ref[r, 0], feats)
        pos_ref[r + 1, cols + 1] = place_of(right_ref[r, 0], feats)
        for c in range(cols):
            pos_ref[r + 1, c + 1] = place_of(own_ref[r, c], feats)
            none = jnp.zeros((feats, LANES), BF16)
            ref = prev_ref if r == 0 else next_ref
            ends = r == 0 or r == rows - 1
            b = r * cols + c
            win[b, :, :LANES] = ref[:feats, :LANES] if ends and c == 0 else none
            win[b, :, LANES:] = ref[:feats, LANES:] if ends and c == cols - 1 else none
    acc[...] = jnp.zeros(acc.shape, F32)
    for copy in copies:
        copy.wait()

    def geometry(b, _):
        r, c = b // cols, b % cols
        zq, near_block, atom = decoded(codes_ref[r, c])
        row3 = (near_block >= 3).astype(jnp.int32) + (near_block >= 6).astype(jnp.int32)
        shift_x = (row3 - 1).astype(F32) * BLOCK_LENGTH
        shift_y = (near_block - 3 * row3 - 1).astype(F32) * BLOCK_LENGTH
        shift_z = (zq - 1).astype(F32) * BLOCK_LENGTH
        centre = pos_ref[r + 1, c + 1]
        found = [jnp.zeros((slots, LANES), F32) for _ in range(3)]
        for k in range(9):
            place = pos_ref[r + k // 3, c + k % 3]
            here = near_block == k
            for i in range(3):
                line = jnp.broadcast_to(place[i : i + 1], (slots, LANES))
                value = jnp.take_along_axis(line, atom, axis=1, mode="promise_in_bounds")
                found[i] = jnp.where(here, value, found[i])
        rx = found[0] + shift_x - centre[0:1]
        ry = found[1] + shift_y - centre[1:2]
        rz = found[2] + shift_z - centre[2:3]
        dist = jnp.sqrt(rx * rx + ry * ry + rz * rz)
        recip = 1.0 / dist
        ux, uy, uz = rx * recip, ry * recip, rz * recip
        x = dist * (1.0 / CUTOFF_RADIUS)
        x2 = x * x
        x5 = x2 * x2 * x
        live = lax.broadcasted_iota(jnp.int32, (slots, LANES), 0) < counts_ref[r, c]
        scale = jnp.where(live, 1.0 / slots, 0.0)
        env = (1.0 - x5 * x * (28.0 - x * (48.0 - 21.0 * x))) * scale
        denv = (-168.0 / CUTOFF_RADIUS) * x5 * (1.0 - x * (2.0 - x)) * scale
        geo[b, 0] = dist
        geo[b, 1] = recip
        geo[b, 2] = env
        geo[b, 3] = denv
        geo[b, 4] = ux
        geo[b, 5] = uy
        geo[b, 6] = uz
        geo[b, 7] = near_block.astype(F32)
        har[b, 0] = root3 * ux
        har[b, 1] = root3 * uy
        har[b, 2] = root3 * uz
        har[b, 3] = root15 * ux * uy
        har[b, 4] = root15 * uy * uz
        har[b, 5] = 0.5 * root5 * (3.0 * uz * uz - 1.0)
        har[b, 6] = root15 * ux * uz
        har[b, 7] = 0.5 * root15 * (ux * ux - uy * uy)
        return 0

    lax.fori_loop(0, blocks, geometry, 0, unroll=blocks == 2)

    def hidden_rows(buffers, step):
        held = buffers[3]
        b, first = step // quads, (step % quads) * QUAD
        dist, recip, env, denv = [joined(geo, b, k, first, QUAD) for k in range(4)]
        order = (lax.broadcasted_iota(jnp.int32, (8, wide), 0) + 1).astype(F32)
        sin, cos = sin_cos_half_turns(order * (dist * (1.0 / CUTOFF_RADIUS)))
        norm = math.sqrt(2.0 / CUTOFF_RADIUS)
        basis = norm * sin * recip
        slope = ((norm * math.pi / CUTOFF_RADIUS) * order * cos - basis) * recip
        split = []
        for x in (basis, slope):
            hi = x.astype(BF16).astype(F32)
            split += [hi, x - hi] * 2
        pre2 = dot(w1s[...], jnp.concatenate(split, axis=0).astype(BF16))
        pre, dpre = pre2[: pre2.shape[0] // 2], pre2[pre2.shape[0] // 2 :]
        gate = 1.0 / (1.0 + jnp.exp(-pre))
        h = pre * gate
        dh = gate + h * (1.0 - gate)
        held[0] = value_rows(h * env)
        held[1] = value_rows(dh * dpre * env + h * denv)

    def radial_rows(buffers, step):
        _, wsc, dsc, held = buffers
        wsc[step // 2] = dot(w2s[...], held[0])
        dsc[step // 2] = dot(w2s[...], held[1])

    def gather(buffers, step):
        b, first = step // quads, (step % quads) * QUAD
        r = b // cols
        k0 = jnp.where(r == 0, 0, jnp.where(r == rows - 1, 6, 9))
        parts = window_hot(near[step], joined(geo, b, 7, first, QUAD), [k0, k0 + 2])
        if stream:
            x_copy(step).wait()
            held = xl[step % RING]
        else:
            held = xl_hbm[step]
        buffers[0][step // 2] = held.astype(F32) + dot(win[b], jnp.concatenate(parts, axis=0))

    def collect(buffers, step):
        xg, wsc = buffers[:2]
        b, first = step // quads, (step % quads) * QUAD
        for g in range(channels // group):
            at = g * group
            total = [acc[b, m, at : at + group, :] for m in range(9)]
            for s in range(QUAD):
                ln = slice(s * LANES, (s + 1) * LANES)
                xs = [
                    xg[step // 2, m * channels + at : m * channels + at + group, ln]
                    for m in range(9)
                ]
                w0, w1, w2 = [
                    wsc[step // 2, k * channels + at : k * channels + at + group, ln]
                    for k in range(3)
                ]
                ys = [har[b, m, pl.ds(first + s, 1), :] for m in range(8)]
                t0 = w0 * xs[0]
                vec = xs[1] * ys[0] + xs[2] * ys[1] + xs[3] * ys[2]
                total[0] = total[0] + (t0 + w1 * xs[0]) + w2 * vec
                for m in range(1, 9):
                    total[m] = total[m] + (t0 * ys[m - 1] + w1 * xs[m])
            for m in range(9):
                acc[b, m, at : at + group, :] = total[m]

    def advance(new, old, step, last=False):
        collect(old, step - 1)
        if not last:
            hidden_rows(old, step + 1)
        gather(new, step)
        radial_rows(new, step)
        if stream:

            @pl.when(step + RING - 1 < steps)
            def _():
                x_copy(step + RING - 1).start()

    def forward(i, _):
        advance(even, odd, 2 * i)
        advance(odd, even, 2 * i + 1)
        return 0

    hidden_rows(even, 0)
    hidden_rows(odd, 1)
    radial_rows(even, 0)
    gather(even, 0)
    advance(odd, even, 1)
    lax.fori_loop(1, steps // 2 - 1, forward, 0)
    advance(even, odd, steps - 2)
    advance(odd, even, steps - 1, last=True)
    collect(odd, steps - 1)

    for b in range(blocks):
        ln = slice(b * LANES, (b + 1) * LANES)
        a = [acc[b, m] for m in range(9)]
        inv[0:channels, ln] = a[0] * a[0]
        inv[channels : 2 * channels, ln] = a[1] * a[1] + a[2] * a[2] + a[3] * a[3]
        inv[2 * channels :, ln] = (
            a[4] * a[4] + a[5] * a[5] + a[6] * a[6] + a[7] * a[7] + a[8] * a[8]
        )
    z = dot(wrs[...], value_rows(inv[...]))
    gate = 1.0 / (1.0 + jnp.exp(-z))
    out = z * gate
    wo = woc[...]
    energy = jnp.sum(out * wo, axis=0, keepdims=True)
    dinv = dot(wrt[...], value_rows(wo * (gate + out * (1.0 - gate))))
    for b in range(blocks):
        ln = slice(b * LANES, (b + 1) * LANES)
        en_ref[b // cols, b % cols] = energy[:, ln]
        for m in range(9):
            part = 0 if m == 0 else (1 if m < 4 else 2)
            d = dinv[part * channels : (part + 1) * channels, ln]
            acc[b, m] = 2.0 * acc[b, m] * d

    def edge_terms(buffers, step):
        xg, wsc, dsc = buffers[:3]
        b, first = step // quads, (step % quads) * QUAD
        for s in range(QUAD):
            ln = slice(s * LANES, (s + 1) * LANES)
            ys = [har[b, m, pl.ds(first + s, 1), :] for m in range(8)]
            dy = [jnp.zeros((group, LANES), F32) for _ in range(9)]
            for g in range(channels // group):
                at = g * group
                xs = [
                    xg[step // 2, m * channels + at : m * channels + at + group, ln]
                    for m in range(9)
                ]
                gs = [acc[b, m, at : at + group, :] for m in range(9)]
                w0 = wsc[step // 2, at : at + group, ln]
                w2 = wsc[step // 2, 2 * channels + at : 2 * channels + at + group, ln]
                d0, d1, d2 = [
                    dsc[step // 2, k * channels + at : k * channels + at + group, ln]
                    for k in range(3)
                ]
                t0 = w0 * xs[0]
                t2 = w2 * gs[0]
                vec = xs[1] * ys[0] + xs[2] * ys[1] + xs[3] * ys[2]
                along = gs[0]
                direct = gs[0] * xs[0]
                for m in range(1, 9):
                    along = along + gs[m] * ys[m - 1]
                    direct = direct + gs[m] * xs[m]
                    dy[m - 1] = dy[m - 1] + t0 * gs[m]
                    if m < 4:
                        dy[m - 1] = dy[m - 1] + t2 * xs[m]
                dy[8] = dy[8] + (d0 * xs[0] * along + d1 * direct + d2 * gs[0] * vec)
            for m in range(9):
                dys[b, m, pl.ds(first + s, 1), :] = jnp.sum(dy[m], axis=0, keepdims=True)

    def backward(i, _):
        edge_terms(even, 2 * i)
        edge_terms(odd, 2 * i + 1)
        return 0

    lax.fori_loop(0, steps // 2, backward, 0)
    force_ref[...] = jnp.zeros(force_ref.shape, F32)

    def pull(b, _):
        r, c = b // cols, b % cols
        ux, uy, uz, recip = geo[b, 4], geo[b, 5], geo[b, 6], geo[b, 1]
        d1, d2, d3, d4, d5, d6, d7, d8 = [dys[b, m] for m in range(8)]
        gx = root3 * d1 + root15 * (uy * d4 + uz * d7 + ux * d8)
        gy = root3 * d2 + root15 * (ux * d4 + uz * d5 - uy * d8)
        gz = root3 * d3 + root15 * (uy * d5 + ux * d7) + (3.0 * root5) * uz * d6
        radial = dys[b, 8] - (ux * gx + uy * gy + uz * gz) * recip
        grads = [gx * recip + ux * radial, gy * recip + uy * radial, gz * recip + uz * radial]
        for i in range(3):
            here = jnp.sum(grads[i], axis=0, keepdims=True)
            force_ref[r + 1, c + 1, i : i + 1, :] += here
        split = [halves(g) for g in grads]
        which = lax.broadcasted_iota(jnp.int32, (16, LANES), 0).astype(F32)
        place = geo[b, 7]
        for n in range(slots):
            ln = slice(n * LANES, (n + 1) * LANES)
            hit = which == place[n : n + 1]
            for i in range(3):
                for v in range(2):
                    line = split[i][v][n : n + 1].astype(F32)
                    at = (3 * v + i) * 16
                    lhs[at : at + 16, ln] = jnp.where(hit, line, 0.0).astype(BF16)
        total = jnp.zeros((96, LANES), F32)
        for p in range(quads):
            total = total + lax.dot_general(
                lhs[:, p * wide : (p + 1) * wide],
                near[b * quads + p],
                (((1,), (1,)), ((), ())),
                preferred_element_type=F32,
            )
        for i in range(3):
            for k in range(9):
                at = i * 16 + k
                value = total[at : at + 1] + total[48 + at : 49 + at]
                force_ref[r + k // 3, c + k % 3, i : i + 1, :] -= value
        return 0

    lax.fori_loop(0, blocks, pull, 0, unroll=blocks == 2)
    for r in range(rows + 2):
        for i in range(3):
            fleft_ref[r, i] = force_ref[r, 0:1, i, :]
            fright_ref[r, i] = force_ref[r, cols + 1 :, i, :]
            fown_ref[r, i] = force_ref[r, 1 : cols + 1, i, :]


def vmem_call(body, name, ins, out_shape, scratch, limit, flops):
    vmem = pl.BlockSpec(memory_space=pltpu.VMEM)
    return pl.pallas_call(
        body,
        out_shape=out_shape,
        in_specs=ins,
        out_specs=[vmem] * len(out_shape),
        scratch_shapes=scratch,
        compiler_params=pltpu.CompilerParams(vmem_limit_bytes=limit * 1024 * 1024),
        cost_estimate=pl.CostEstimate(flops=flops, bytes_accessed=1024 * 1024, transcendentals=0),
        name=name,
    )


def pinned(*args):
    return [pltpu.with_memory_space_constraint(x, pltpu.HBM) for x in args]


def prepare_part(own, feats, neighbours, w_first, w_second, w_read, w_out):
    rows, cols, slots = neighbours.shape[0], neighbours.shape[1], neighbours.shape[2]
    hidden, basis = w_first.shape
    units, reads = w_read.shape
    weights = w_second.shape[0]
    blocks, steps, wide = rows * cols, rows * cols * slots // QUAD, QUAD * LANES
    spans = min(rows, 3)
    vmem = pl.BlockSpec(memory_space=pltpu.VMEM)
    hbm = pl.BlockSpec(memory_space=pltpu.HBM)
    sds = jax.ShapeDtypeStruct
    call = vmem_call(
        functools.partial(prepare_kernel, rows, cols, slots),
        "prepare",
        [vmem] + [hbm] * 5,
        [
            sds((steps, LANES, wide), BF16),
            sds((blocks, slots, LANES), F32),
            sds((2 * hidden, 8 * basis), BF16),
            sds((weights, 3 * hidden), BF16),
            sds((units, 3 * reads), BF16),
            sds((reads, 3 * units), BF16),
            sds((units, 1), F32),
            sds((steps, feats, wide), BF16),
        ],
        [
            pltpu.VMEM(neighbours.shape, jnp.int32),
            pltpu.VMEM((basis, hidden), F32),
            pltpu.VMEM((hidden, weights), F32),
            pltpu.VMEM((reads, units), F32),
            pltpu.VMEM((1, units), F32),
            pltpu.VMEM((blocks, slots, LANES), F32),
            pltpu.VMEM((blocks, feats, spans * LANES), BF16),
            pltpu.VMEM((spans * LANES, wide), BF16),
            pltpu.VMEM((spans * LANES, wide), BF16),
            pltpu.SemaphoreType.DMA((5,)),
        ],
        16,
        2 * feats * spans * LANES * steps * wide,
    )
    return call(
        own, *pinned(neighbours, w_first.T, w_second.T, w_read.T, w_out.reshape(1, units))
    )


def pack_part(features, pos):
    rows, cols, feats, _ = features.shape
    vmem = pl.BlockSpec(memory_space=pltpu.VMEM)
    hbm = pl.BlockSpec(memory_space=pltpu.HBM)
    call = vmem_call(
        functools.partial(pack_kernel, rows, cols),
        "pack",
        [hbm] * 2,
        [jax.ShapeDtypeStruct((rows, cols, feats + 16, LANES), BF16)],
        [pltpu.VMEM(pos.shape, F32), pltpu.SemaphoreType.DMA((1 + rows * cols,))],
        2,
        1000000,
    )
    return call(*pinned(features, pos))[0]


def ends_part(left, right):
    vmem = pl.BlockSpec(memory_space=pltpu.VMEM)
    message = jax.ShapeDtypeStruct((left.shape[2], 2 * LANES), BF16)
    call = vmem_call(
        functools.partial(ends_kernel, left.shape[0]),
        "ends",
        [vmem] * 2,
        [message] * 2,
        [],
        2,
        1000000,
    )
    return call(left, right)


def ghost_part(before, after, near, place, xa, rows, cols):
    vmem = pl.BlockSpec(memory_space=pltpu.VMEM)
    steps, feats, wide = xa.shape
    call = vmem_call(
        functools.partial(ghost_kernel, rows, cols),
        "ghost",
        [vmem] * 5,
        [jax.ShapeDtypeStruct(xa.shape, BF16)],
        [],
        8,
        2 * feats * LANES * steps * wide,
    )
    return call(before, after, near, place, xa)[0]


def finish_part(front, force, ahead, vel, pos, fresh_pos, fresh_vel):
    vmem = pl.BlockSpec(memory_space=pltpu.VMEM)
    smem = pl.BlockSpec(memory_space=pltpu.SMEM)
    call = vmem_call(
        functools.partial(finish_kernel, vel.shape[0]),
        "finish",
        [smem] + [vmem] * 6,
        [jax.ShapeDtypeStruct(vel.shape, F32)] * 2,
        [],
        2,
        100000,
    )
    return call(front, force, ahead, vel, pos, fresh_pos, fresh_vel)


def local_part(left, right, own, near, place, xa):
    rows, cols, feats = own.shape[0], own.shape[1], xa.shape[1]
    steps, _, wide = near.shape
    most = 2 * min(rows, 3)
    vmem = pl.BlockSpec(memory_space=pltpu.VMEM)
    call = vmem_call(
        functools.partial(local_kernel, rows, cols),
        "local",
        [vmem] * 6,
        [jax.ShapeDtypeStruct((steps, feats, wide), BF16)],
        [
            pltpu.VMEM((rows * cols, feats, most * LANES), BF16),
            pltpu.VMEM((most * LANES, wide), BF16),
            pltpu.VMEM((most * LANES, wide), BF16),
        ],
        16,
        2 * feats * most * LANES * steps * wide,
    )
    return call(left, right, own, near, place, xa)[0]


def energy_part(ghosts, own, left, right, neighbours, counts, prepared, gathered):
    near, place, w1s, w2s, wrs, wrt, woc = prepared[:7]
    rows, cols, slots = neighbours.shape[0], neighbours.shape[1], neighbours.shape[2]
    steps, _, wide = near.shape
    weights = w2s.shape[0]
    channels, blocks, feats = weights // 3, rows * cols, gathered.shape[1]
    vmem = pl.BlockSpec(memory_space=pltpu.VMEM)
    hbm = pl.BlockSpec(memory_space=pltpu.HBM)
    sds = jax.ShapeDtypeStruct
    side = sds((rows + 2, 3, 1, LANES), F32)
    stream = blocks > 2
    half = steps // 2
    call = vmem_call(
        functools.partial(energy_kernel, rows, cols, channels, slots, stream=stream),
        "energy",
        [vmem] * 7 + [hbm] * 2 + [vmem] * 6 + [hbm if stream else vmem],
        [sds((rows, cols, 1, LANES), F32), side, sds((rows + 2, 3, cols, LANES), F32), side],
        [
            pltpu.VMEM((rows + 2, cols + 2, 3, LANES), F32),
            pltpu.VMEM((rows + 2, cols + 2, 3, LANES), F32),
            pltpu.VMEM((rows, cols, slots, LANES), jnp.int32),
            pltpu.VMEM((rows, cols, 1, LANES), jnp.int32),
            pltpu.VMEM((blocks, 8, slots, LANES), F32),
            pltpu.VMEM((blocks, 8, slots, LANES), F32),
            pltpu.VMEM((blocks, feats, 2 * LANES), BF16),
            pltpu.VMEM((RING, feats, wide) if stream else (1, 16, LANES), BF16),
            pltpu.VMEM((half, feats, wide), F32),
            pltpu.VMEM((half, feats, wide), F32),
            pltpu.VMEM((half, weights, wide), F32),
            pltpu.VMEM((half, weights, wide), F32),
            pltpu.VMEM((half, weights, wide), F32),
            pltpu.VMEM((half, weights, wide), F32),
            pltpu.VMEM((2, 3 * (w1s.shape[0] // 2), wide), BF16),
            pltpu.VMEM((2, 3 * (w1s.shape[0] // 2), wide), BF16),
            pltpu.VMEM((blocks, 9, channels, LANES), F32),
            pltpu.VMEM((weights, blocks * LANES), F32),
            pltpu.VMEM((blocks, 9, slots, LANES), F32),
            pltpu.VMEM((96, slots * LANES), BF16),
            pltpu.SemaphoreType.DMA((2,)),
            pltpu.SemaphoreType.DMA((RING,)),
        ],
        56 if stream else 32,
        2 * feats * 9 * LANES * steps * wide,
    )
    energies, f_left, f_own, f_right = call(
        *ghosts,
        own,
        left,
        right,
        *pinned(neighbours, counts.reshape(rows, cols, 1, LANES)),
        near,
        w1s,
        w2s,
        wrs,
        wrt,
        woc,
        gathered,
    )
    return f_left, f_own, f_right, energies.reshape(rows, cols, LANES)


def local(
    positions,
    velocities,
    features,
    neighbours,
    counts,
    w_first,
    w_second,
    w_read,
    w_out,
    fresh_positions,
    fresh_velocities,
):
    nrows, ncols = (positions.shape[0], positions.shape[1])
    shock_place = lax.axis_index("shock")
    front = lax.axis_size("shock") - 1
    assert nrows >= 2 and neighbours.shape[2] % (2 * QUAD) == 0

    def sides(x, axis):
        last = lax.slice_in_dim(x, ncols - 1, ncols, axis=axis)
        first = lax.slice_in_dim(x, 0, 1, axis=axis)
        return shifted(last, "trans", 1), shifted(first, "trans", -1)

    pos = positions.transpose(0, 2, 1, 3)
    vel = velocities.transpose(0, 2, 1, 3)
    own = pack_part(features, pos)
    left, right = sides(own, 1)
    before = passed_along(own[nrows - 1 :], "shock", 1)
    after = passed_along(own[:1], "shock", -1)
    feats = features.shape[2]
    prepared = prepare_part(own, feats, neighbours, w_first, w_second, w_read, w_out)
    near, place, xa = prepared[0], prepared[1], prepared[7]
    xa = ghost_part(before, after, near, place, xa, nrows, ncols)
    left, right, xa = lax.optimization_barrier((left, right, xa))
    last, first = ends_part(left, right)
    ghosts = (
        passed_along(last, "shock", 1),
        passed_along(first, "shock", -1),
        before,
        after,
    )
    gathered = local_part(left, right, own, near, place, xa)
    f_left, f_own, f_right, energies = energy_part(
        ghosts, own, left, right, neighbours, counts, prepared, gathered
    )
    from_right = shifted(f_left, "trans", -1)
    from_left = shifted(f_right, "trans", 1)
    folded = f_own.at[:, :, ncols - 1].add(from_right[:, :, 0])
    folded = folded.at[:, :, 0].add(from_left[:, :, 0])
    packed = jnp.concatenate([folded[:2], vel[:1], pos[:1]], axis=0)
    ahead = passed_along(packed, "shock", -1)
    at_front = (shock_place == front).astype(jnp.int32).reshape(1)
    new_positions, new_velocities = finish_part(
        at_front,
        folded,
        ahead,
        vel,
        pos,
        fresh_positions.transpose(1, 0, 2),
        fresh_velocities.transpose(1, 0, 2),
    )
    return (energies, new_positions.transpose(0, 2, 1, 3), new_velocities.transpose(0, 2, 1, 3))


def solution(mesh):
    return jax.shard_map(
        local,
        mesh=mesh,
        in_specs=(
            P("shock", "trans", None, None),
            P("shock", "trans", None, None),
            P("shock", "trans", None, None),
            P("shock", "trans", None, None),
            P("shock", "trans", None),
            P(),
            P(),
            P(),
            P(),
            P("trans", None, None),
            P("trans", None, None),
        ),
        out_specs=(
            P("shock", "trans", None),
            P("shock", "trans", None, None),
            P("shock", "trans", None, None),
        ),
        check_vma=False,
    )
```

```python
import functools
import math

import jax
import jax.numpy as jnp
from jax import lax
from jax.experimental import pallas as pl
from jax.experimental.pallas import tpu as pltpu
from jax.sharding import PartitionSpec as P

CUTOFF_RADIUS = 9.5
BLOCK_LENGTH = 13.2
KICK_FACTOR = 4.0
MOVE_FACTOR = 0.5
F32 = jnp.float32
BF16 = jnp.bfloat16
LANES = 128
QUAD = 4


def shifted(x, axis, by):
    count = lax.axis_size(axis)
    return lax.ppermute(x, axis, [(i, (i + by) % count) for i in range(count)])


def passed_along(block, axis, distance):
    devices = range(lax.axis_size(axis))
    route = [(i - distance, i) for i in devices if i - distance in devices]
    return lax.ppermute(block, axis, route)


def halves(x):
    hi = x.astype(BF16)
    lo = (x - hi.astype(F32)).astype(BF16)
    return hi, lo


def value_rows(x):
    hi, lo = halves(x)
    return jnp.concatenate([hi, lo, hi], axis=0)


def dot(a, b):
    return jnp.dot(a, b, preferred_element_type=F32)


def sin_cos_half_turns(t):
    n = jnp.floor(t + 0.5)
    r = t - n
    odd = n - 2.0 * jnp.floor(0.5 * n)
    sign = 1.0 - 2.0 * odd
    x = math.pi * r
    y = x * x
    s = 1.0 + y * (
        -1.0 / 6
        + y
        * (
            1.0 / 120
            + y * (-1.0 / 5040 + y * (1.0 / 362880 + y * (-1.0 / 39916800 + y * (1.0 / 6227020800.0))))
        )
    )
    c = 1.0 + y * (
        -0.5
        + y
        * (
            1.0 / 24
            + y
            * (-1.0 / 720 + y * (1.0 / 40320 + y * (-1.0 / 3628800 + y * (1.0 / 479001600.0))))
        )
    )
    return sign * x * s, sign * c


def weight_halves(w):
    hi = w.astype(BF16).astype(F32)
    return hi, w - hi


def weight_rows(w):
    hi, lo = weight_halves(w)
    return jnp.concatenate([hi, hi, lo], axis=1).astype(BF16)


def joined(ref, b, k, first, count):
    lines = [ref[b, k, pl.ds(first + s, 1), :] for s in range(count)]
    return jnp.concatenate(lines, axis=1)


def lines(ref, b, first, count):
    return jnp.concatenate([ref[b, pl.ds(first + s, 1), :] for s in range(count)], axis=1)


def first_row(rows, r):
    return 1 if (rows == 2 and r == 0) else 0


def window_hot(near, place, wanted):
    lanes = near.shape[1]
    near3 = near.reshape(LANES // 16, 16, lanes)
    parts = []
    for k in wanted:
        mask = jnp.where(place == jnp.asarray(k).astype(F32), 1.0, 0.0)
        mask = jnp.broadcast_to(mask, (16, lanes)).astype(BF16)
        parts.append((near3 * mask[None]).reshape(LANES, lanes))
    return parts


def decoded(codes):
    zq = (codes >= 1152).astype(jnp.int32) + (codes >= 2304).astype(jnp.int32)
    slot = codes - 1152 * zq
    return zq, lax.shift_right_logical(slot, 7), slot & 127


def copied(sources, places, sems):
    copies = [
        pltpu.make_async_copy(x, y, sems.at[i]) for i, (x, y) in enumerate(zip(sources, places))
    ]
    for copy in copies:
        copy.start()
    return copies


def prepare_kernel(
    rows,
    cols,
    slots,
    own_ref,
    codes_hbm,
    w1_hbm,
    w2_hbm,
    wr_hbm,
    wo_hbm,
    near,
    place,
    w1s,
    w2s,
    wrs,
    wrt,
    woc,
    out,
    codes_ref,
    w1_ref,
    w2_ref,
    wr_ref,
    wo_ref,
    atoms,
    win,
    onehot_even,
    onehot_odd,
    sems,
):
    blocks = rows * cols
    quads = slots // QUAD
    wide = QUAD * LANES
    spans = win.shape[2] // LANES
    copies = copied(
        [codes_hbm, w1_hbm, w2_hbm, wr_hbm, wo_hbm],
        [codes_ref, w1_ref, w2_ref, wr_ref, wo_ref],
        sems,
    )
    copies[0].wait()
    for r in range(rows):
        for c in range(cols):
            _, block, atom = decoded(codes_ref[r, c])
            place[r * cols + c] = block.astype(F32)
            atoms[r * cols + c] = atom.astype(F32)
    feats = win.shape[1]
    for r in range(rows):
        first = first_row(rows, r)
        for c in range(cols):
            for k in range(spans):
                ln = slice(k * LANES, (k + 1) * LANES)
                if 0 <= r - 1 + first + k < rows:
                    win[r * cols + c, :, ln] = own_ref[r - 1 + first + k, c, :feats]
                else:
                    win[r * cols + c, :, ln] = jnp.zeros((feats, LANES), BF16)

    def pick(onehot, step):
        b, at = step // quads, (step % quads) * QUAD
        atom = lines(atoms, b, at, QUAD)
        sub = lax.broadcasted_iota(jnp.int32, (LANES, wide), 0).astype(F32)
        hot = jnp.where(sub == atom, 1.0, 0.0).astype(BF16)
        near[step] = hot
        first = jnp.where(b // cols == 0, first_row(rows, 0), 0)
        wanted = [3 * (first + k) + 1 for k in range(spans)]
        parts = window_hot(hot, lines(place, b, at, QUAD), wanted)
        for k in range(spans):
            onehot[k * LANES : (k + 1) * LANES, :] = parts[k]
        out[step] = dot(win[b], onehot[...]).astype(BF16)

    def body(i, _):
        pick(onehot_even, 2 * i)
        pick(onehot_odd, 2 * i + 1)
        return 0

    lax.fori_loop(0, blocks * quads // 2, body, 0)

    for copy in copies[1:]:
        copy.wait()
    hi, lo = weight_halves(w1_ref[...].T)
    line = jnp.concatenate([hi, hi, lo, lo], axis=1)
    none = jnp.zeros_like(line)
    w1s[...] = jnp.concatenate(
        [jnp.concatenate([line, none], axis=1), jnp.concatenate([none, line], axis=1)], axis=0
    ).astype(BF16)
    w2s[...] = weight_rows(w2_ref[...].T)
    wrs[...] = weight_rows(wr_ref[...].T)
    wrt[...] = weight_rows(wr_ref[...])
    units = wo_ref.shape[1]
    one = lax.broadcasted_iota(jnp.int32, (units, units), 0)
    two = lax.broadcasted_iota(jnp.int32, (units, units), 1)
    woc[...] = jnp.sum(jnp.where(one == two, wo_ref[...], 0.0), axis=1, keepdims=True)


def pack_kernel(rows, cols, feat_hbm, pos_hbm, out, pos_ref, sems):
    feats = feat_hbm.shape[2]
    copies = copied(
        [pos_hbm] + [feat_hbm.at[r, c] for r in range(rows) for c in range(cols)],
        [pos_ref] + [out.at[r, c, pl.ds(0, feats)] for r in range(rows) for c in range(cols)],
        sems,
    )
    copies[0].wait()
    for r in range(rows):
        for c in range(cols):
            rest = jnp.concatenate([pos_ref[r, i, c : c + 1, :] for i in range(3)], axis=0)
            parts = []
            for _ in range(3):
                part = rest.astype(BF16).astype(F32)
                parts.append(part)
                rest = rest - part
            parts.append(jnp.zeros((7, LANES), F32))
            out[r, c, feats:] = jnp.concatenate(parts, axis=0).astype(BF16)
    for copy in copies[1:]:
        copy.wait()


def place_of(block, feats):
    rest = block[feats : feats + 16].astype(F32)
    return rest[0:3] + rest[3:6] + rest[6:9]


def ends_kernel(rows, left_ref, right_ref, up, down):
    for out, r in ((up, rows - 1), (down, 0)):
        out[:, :LANES] = left_ref[r, 0]
        out[:, LANES:] = right_ref[r, 0]


def ghost_kernel(rows, cols, prev_ref, next_ref, near, place, xa, out):
    steps = near.shape[0]
    quads = steps // (rows * cols)
    feats = out.shape[1]
    for b in range(rows * cols):
        r, c = b // cols, b % cols

        def pick(step):
            first = (step % quads) * QUAD
            if r == 0 or r == rows - 1:
                ref, slot = (prev_ref, 1) if r == 0 else (next_ref, 7)
                hot = window_hot(near[step], lines(place, b, first, QUAD), [slot])[0]
                out[step] = xa[step] + dot(ref[0, c, :feats], hot).astype(BF16)
            else:
                out[step] = xa[step]

        def body(i, _):
            pick(b * quads + 2 * i)
            pick(b * quads + 2 * i + 1)
            return 0

        lax.fori_loop(0, quads // 2, body, 0)


def finish_kernel(
    rows, front_ref, force, ahead, vel, pos, fresh_pos, fresh_vel, new_pos, new_vel
):
    front = front_ref[0] == 1
    for r in range(rows):
        total = force[r + 2]
        if r >= rows - 2:
            total = total + ahead[r - rows + 2]
        old_vel = vel[r + 1] if r < rows - 1 else ahead[2]
        old_pos = pos[r + 1] if r < rows - 1 else ahead[3]
        v = old_vel + KICK_FACTOR * total
        p = old_pos + MOVE_FACTOR * v
        if r == rows - 1:
            v = jnp.where(front, fresh_vel[...], v)
            p = jnp.where(front, fresh_pos[...], p)
        new_vel[r] = v
        new_pos[r] = p


def local_kernel(
    rows,
    cols,
    left_ref,
    right_ref,
    own_ref,
    near,
    place,
    xa,
    out,
    win,
    hot_even,
    hot_odd,
):
    blocks = rows * cols
    steps = near.shape[0]
    quads = steps // blocks
    feats = out.shape[1]

    def columns(r, c):
        found = []
        for k in range(3):
            row = r - 1 + k
            for col in (c - 1, c, c + 1):
                slot = 3 * k + col - c + 1
                if 0 <= row < rows and col != c:
                    if col < 0:
                        found.append((slot, left_ref[row, 0, :feats]))
                    elif col >= cols:
                        found.append((slot, right_ref[row, 0, :feats]))
                    else:
                        found.append((slot, own_ref[row, col, :feats]))
        return found

    for b in range(blocks):
        found = columns(b // cols, b % cols)
        count = len(found)
        for k, (_, block) in enumerate(found):
            win[b, :, k * LANES : (k + 1) * LANES] = block

        def pick(hot, step):
            first = (step % quads) * QUAD
            parts = window_hot(near[step], lines(place, b, first, QUAD), [x for x, _ in found])
            for k in range(count):
                hot[k * LANES : (k + 1) * LANES, :] = parts[k]
            picked = dot(win[b, :, : count * LANES], hot[: count * LANES, :])
            out[step] = xa[step] + picked.astype(BF16)

        def body(i, _):
            pick(hot_even, b * quads + 2 * i)
            pick(hot_odd, b * quads + 2 * i + 1)
            return 0

        lax.fori_loop(0, quads // 2, body, 0)


RING = 3


def energy_kernel(
    rows,
    cols,
    channels,
    slots,
    prev_ref,
    next_ref,
    prev_own_ref,
    next_own_ref,
    own_ref,
    left_ref,
    right_ref,
    codes_hbm,
    counts_hbm,
    near,
    w1s,
    w2s,
    wrs,
    wrt,
    woc,
    xl_hbm,
    en_ref,
    fleft_ref,
    fown_ref,
    fright_ref,
    force_ref,
    pos_ref,
    codes_ref,
    counts_ref,
    geo,
    har,
    win,
    xl,
    xg_even,
    xg_odd,
    w_even,
    w_odd,
    d_even,
    d_odd,
    held_even,
    held_odd,
    acc,
    inv,
    dys,
    lhs,
    sems,
    xsem,
    *,
    stream,
):
    blocks = rows * cols
    quads = slots // QUAD
    steps = blocks * quads
    wide = QUAD * LANES
    group = 8
    feats = 9 * channels
    root3, root5, root15 = math.sqrt(3.0), math.sqrt(5.0), math.sqrt(15.0)
    even, odd = (xg_even, w_even, d_even, held_even), (xg_odd, w_odd, d_odd, held_odd)

    def x_copy(step):
        at = step % RING
        return pltpu.make_async_copy(xl_hbm.at[step], xl.at[at], xsem.at[at])

    copies = copied([codes_hbm, counts_hbm], [codes_ref, counts_ref], sems)
    if stream:
        for i in range(RING):
            x_copy(i).start()

    for side, middle, r in ((prev_ref, prev_own_ref, 0), (next_ref, next_own_ref, rows + 1)):
        pos_ref[r, 0] = place_of(side[:, :LANES], feats)
        pos_ref[r, cols + 1] = place_of(side[:, LANES:], feats)
        for c in range(cols):
            pos_ref[r, c + 1] = place_of(middle[0, c], feats)
    for r in range(rows):
        pos_ref[r + 1, 0] = place_of(left_ref[r, 0], feats)
        pos_ref[r + 1, cols + 1] = place_of(right_ref[r, 0], feats)
        for c in range(cols):
            pos_ref[r + 1, c + 1] = place_of(own_ref[r, c], feats)
            none = jnp.zeros((feats, LANES), BF16)
            ref = prev_ref if r == 0 else next_ref
            ends = r == 0 or r == rows - 1
            b = r * cols + c
            win[b, :, :LANES] = ref[:feats, :LANES] if ends and c == 0 else none
            win[b, :, LANES:] = ref[:feats, LANES:] if ends and c == cols - 1 else none
    acc[...] = jnp.zeros(acc.shape, F32)
    for copy in copies:
        copy.wait()

    def geometry(b, _):
        r, c = b // cols, b % cols
        zq, near_block, atom = decoded(codes_ref[r, c])
        row3 = (near_block >= 3).astype(jnp.int32) + (near_block >= 6).astype(jnp.int32)
        shift_x = (row3 - 1).astype(F32) * BLOCK_LENGTH
        shift_y = (near_block - 3 * row3 - 1).astype(F32) * BLOCK_LENGTH
        shift_z = (zq - 1).astype(F32) * BLOCK_LENGTH
        centre = pos_ref[r + 1, c + 1]
        found = [jnp.zeros((slots, LANES), F32) for _ in range(3)]
        for k in range(9):
            place = pos_ref[r + k // 3, c + k % 3]
            here = near_block == k
            for i in range(3):
                line = jnp.broadcast_to(place[i : i + 1], (slots, LANES))
                value = jnp.take_along_axis(line, atom, axis=1, mode="promise_in_bounds")
                found[i] = jnp.where(here, value, found[i])
        rx = found[0] + shift_x - centre[0:1]
        ry = found[1] + shift_y - centre[1:2]
        rz = found[2] + shift_z - centre[2:3]
        dist = jnp.sqrt(rx * rx + ry * ry + rz * rz)
        recip = 1.0 / dist
        ux, uy, uz = rx * recip, ry * recip, rz * recip
        x = dist * (1.0 / CUTOFF_RADIUS)
        x2 = x * x
        x5 = x2 * x2 * x
        live = lax.broadcasted_iota(jnp.int32, (slots, LANES), 0) < counts_ref[r, c]
        scale = jnp.where(live, 1.0 / slots, 0.0)
        env = (1.0 - x5 * x * (28.0 - x * (48.0 - 21.0 * x))) * scale
        denv = (-168.0 / CUTOFF_RADIUS) * x5 * (1.0 - x * (2.0 - x)) * scale
        geo[b, 0] = dist
        geo[b, 1] = recip
        geo[b, 2] = env
        geo[b, 3] = denv
        geo[b, 4] = ux
        geo[b, 5] = uy
        geo[b, 6] = uz
        geo[b, 7] = near_block.astype(F32)
        har[b, 0] = root3 * ux
        har[b, 1] = root3 * uy
        har[b, 2] = root3 * uz
        har[b, 3] = root15 * ux * uy
        har[b, 4] = root15 * uy * uz
        har[b, 5] = 0.5 * root5 * (3.0 * uz * uz - 1.0)
        har[b, 6] = root15 * ux * uz
        har[b, 7] = 0.5 * root15 * (ux * ux - uy * uy)
        return 0

    lax.fori_loop(0, blocks, geometry, 0, unroll=blocks == 2)

    def hidden_rows(buffers, step):
        held = buffers[3]
        b, first = step // quads, (step % quads) * QUAD
        dist, recip, env, denv = [joined(geo, b, k, first, QUAD) for k in range(4)]
        order = (lax.broadcasted_iota(jnp.int32, (8, wide), 0) + 1).astype(F32)
        sin, cos = sin_cos_half_turns(order * (dist * (1.0 / CUTOFF_RADIUS)))
        norm = math.sqrt(2.0 / CUTOFF_RADIUS)
        basis = norm * sin * recip
        slope = ((norm * math.pi / CUTOFF_RADIUS) * order * cos - basis) * recip
        split = []
        for x in (basis, slope):
            hi = x.astype(BF16).astype(F32)
            split += [hi, x - hi] * 2
        pre2 = dot(w1s[...], jnp.concatenate(split, axis=0).astype(BF16))
        pre, dpre = pre2[: pre2.shape[0] // 2], pre2[pre2.shape[0] // 2 :]
        gate = 1.0 / (1.0 + jnp.exp(-pre))
        h = pre * gate
        dh = gate + h * (1.0 - gate)
        held[0] = value_rows(h * env)
        held[1] = value_rows(dh * dpre * env + h * denv)

    def radial_rows(buffers, step):
        _, wsc, dsc, held = buffers
        wsc[step // 2] = dot(w2s[...], held[0])
        dsc[step // 2] = dot(w2s[...], held[1])

    def gather(buffers, step):
        b, first = step // quads, (step % quads) * QUAD
        r = b // cols
        k0 = jnp.where(r == 0, 0, jnp.where(r == rows - 1, 6, 9))
        parts = window_hot(near[step], joined(geo, b, 7, first, QUAD), [k0, k0 + 2])
        if stream:
            x_copy(step).wait()
            held = xl[step % RING]
        else:
            held = xl_hbm[step]
        buffers[0][step // 2] = held.astype(F32) + dot(win[b], jnp.concatenate(parts, axis=0))

    def collect(buffers, step):
        xg, wsc = buffers[:2]
        b, first = step // quads, (step % quads) * QUAD
        for g in range(channels // group):
            at = g * group
            total = [acc[b, m, at : at + group, :] for m in range(9)]
            for s in range(QUAD):
                ln = slice(s * LANES, (s + 1) * LANES)
                xs = [
                    xg[step // 2, m * channels + at : m * channels + at + group, ln]
                    for m in range(9)
                ]
                w0, w1, w2 = [
                    wsc[step // 2, k * channels + at : k * channels + at + group, ln]
                    for k in range(3)
                ]
                ys = [har[b, m, pl.ds(first + s, 1), :] for m in range(8)]
                t0 = w0 * xs[0]
                vec = xs[1] * ys[0] + xs[2] * ys[1] + xs[3] * ys[2]
                total[0] = total[0] + (t0 + w1 * xs[0]) + w2 * vec
                for m in range(1, 9):
                    total[m] = total[m] + (t0 * ys[m - 1] + w1 * xs[m])
            for m in range(9):
                acc[b, m, at : at + group, :] = total[m]

    def advance(new, old, step, last=False):
        collect(old, step - 1)
        if not last:
            hidden_rows(old, step + 1)
        gather(new, step)
        radial_rows(new, step)
        if stream:

            @pl.when(step + RING - 1 < steps)
            def _():
                x_copy(step + RING - 1).start()

    def forward(i, _):
        advance(even, odd, 2 * i)
        advance(odd, even, 2 * i + 1)
        return 0

    hidden_rows(even, 0)
    hidden_rows(odd, 1)
    radial_rows(even, 0)
    gather(even, 0)
    advance(odd, even, 1)
    lax.fori_loop(1, steps // 2 - 1, forward, 0)
    advance(even, odd, steps - 2)
    advance(odd, even, steps - 1, last=True)
    collect(odd, steps - 1)

    for b in range(blocks):
        ln = slice(b * LANES, (b + 1) * LANES)
        a = [acc[b, m] for m in range(9)]
        inv[0:channels, ln] = a[0] * a[0]
        inv[channels : 2 * channels, ln] = a[1] * a[1] + a[2] * a[2] + a[3] * a[3]
        inv[2 * channels :, ln] = (
            a[4] * a[4] + a[5] * a[5] + a[6] * a[6] + a[7] * a[7] + a[8] * a[8]
        )
    z = dot(wrs[...], value_rows(inv[...]))
    gate = 1.0 / (1.0 + jnp.exp(-z))
    out = z * gate
    wo = woc[...]
    energy = jnp.sum(out * wo, axis=0, keepdims=True)
    dinv = dot(wrt[...], value_rows(wo * (gate + out * (1.0 - gate))))
    for b in range(blocks):
        ln = slice(b * LANES, (b + 1) * LANES)
        en_ref[b // cols, b % cols] = energy[:, ln]
        for m in range(9):
            part = 0 if m == 0 else (1 if m < 4 else 2)
            d = dinv[part * channels : (part + 1) * channels, ln]
            acc[b, m] = 2.0 * acc[b, m] * d

    def edge_terms(buffers, step):
        xg, wsc, dsc = buffers[:3]
        group = 16
        b, first = step // quads, (step % quads) * QUAD
        for s in range(QUAD):
            ln = slice(s * LANES, (s + 1) * LANES)
            ys = [har[b, m, pl.ds(first + s, 1), :] for m in range(8)]
            dy = [jnp.zeros((group, LANES), F32) for _ in range(9)]
            for g in range(channels // group):
                at = g * group
                xs = [
                    xg[step // 2, m * channels + at : m * channels + at + group, ln]
                    for m in range(9)
                ]
                gs = [acc[b, m, at : at + group, :] for m in range(9)]
                w0 = wsc[step // 2, at : at + group, ln]
                w2 = wsc[step // 2, 2 * channels + at : 2 * channels + at + group, ln]
                d0, d1, d2 = [
                    dsc[step // 2, k * channels + at : k * channels + at + group, ln]
                    for k in range(3)
                ]
                t0 = w0 * xs[0]
                t2 = w2 * gs[0]
                vec = xs[1] * ys[0] + xs[2] * ys[1] + xs[3] * ys[2]
                along = gs[0]
                direct = gs[0] * xs[0]
                for m in range(1, 9):
                    along = along + gs[m] * ys[m - 1]
                    direct = direct + gs[m] * xs[m]
                    dy[m - 1] = dy[m - 1] + t0 * gs[m]
                    if m < 4:
                        dy[m - 1] = dy[m - 1] + t2 * xs[m]
                dy[8] = dy[8] + (d0 * xs[0] * along + d1 * direct + d2 * gs[0] * vec)
            for m in range(9):
                dys[b, m, pl.ds(first + s, 1), :] = jnp.sum(dy[m], axis=0, keepdims=True)

    def backward(i, _):
        edge_terms(even, 2 * i)
        edge_terms(odd, 2 * i + 1)
        return 0

    lax.fori_loop(0, steps // 2, backward, 0)
    force_ref[...] = jnp.zeros(force_ref.shape, F32)

    def pull(b, _):
        r, c = b // cols, b % cols
        ux, uy, uz, recip = geo[b, 4], geo[b, 5], geo[b, 6], geo[b, 1]
        d1, d2, d3, d4, d5, d6, d7, d8 = [dys[b, m] for m in range(8)]
        gx = root3 * d1 + root15 * (uy * d4 + uz * d7 + ux * d8)
        gy = root3 * d2 + root15 * (ux * d4 + uz * d5 - uy * d8)
        gz = root3 * d3 + root15 * (uy * d5 + ux * d7) + (3.0 * root5) * uz * d6
        radial = dys[b, 8] - (ux * gx + uy * gy + uz * gz) * recip
        grads = [gx * recip + ux * radial, gy * recip + uy * radial, gz * recip + uz * radial]
        for i in range(3):
            here = jnp.sum(grads[i], axis=0, keepdims=True)
            force_ref[r + 1, c + 1, i : i + 1, :] += here
        split = [halves(g) for g in grads]
        which = lax.broadcasted_iota(jnp.int32, (16, LANES), 0).astype(F32)
        place = geo[b, 7]
        for n in range(slots):
            ln = slice(n * LANES, (n + 1) * LANES)
            hit = which == place[n : n + 1]
            for i in range(3):
                for v in range(2):
                    line = split[i][v][n : n + 1].astype(F32)
                    at = (3 * v + i) * 16
                    lhs[at : at + 16, ln] = jnp.where(hit, line, 0.0).astype(BF16)
        total = jnp.zeros((96, LANES), F32)
        for p in range(quads):
            total = total + lax.dot_general(
                lhs[:, p * wide : (p + 1) * wide],
                near[b * quads + p],
                (((1,), (1,)), ((), ())),
                preferred_element_type=F32,
            )
        for i in range(3):
            for k in range(9):
                at = i * 16 + k
                value = total[at : at + 1] + total[48 + at : 49 + at]
                force_ref[r + k // 3, c + k % 3, i : i + 1, :] -= value
        return 0

    lax.fori_loop(0, blocks, pull, 0, unroll=blocks == 2)
    for r in range(rows + 2):
        for i in range(3):
            fleft_ref[r, i] = force_ref[r, 0:1, i, :]
            fright_ref[r, i] = force_ref[r, cols + 1 :, i, :]
            fown_ref[r, i] = force_ref[r, 1 : cols + 1, i, :]


def vmem_call(body, name, ins, out_shape, scratch, limit, flops):
    vmem = pl.BlockSpec(memory_space=pltpu.VMEM)
    return pl.pallas_call(
        body,
        out_shape=out_shape,
        in_specs=ins,
        out_specs=[vmem] * len(out_shape),
        scratch_shapes=scratch,
        compiler_params=pltpu.CompilerParams(vmem_limit_bytes=limit * 1024 * 1024),
        cost_estimate=pl.CostEstimate(flops=flops, bytes_accessed=1024 * 1024, transcendentals=0),
        name=name,
    )


def pinned(*args):
    return [pltpu.with_memory_space_constraint(x, pltpu.HBM) for x in args]


def prepare_part(own, feats, neighbours, w_first, w_second, w_read, w_out):
    rows, cols, slots = neighbours.shape[0], neighbours.shape[1], neighbours.shape[2]
    hidden, basis = w_first.shape
    units, reads = w_read.shape
    weights = w_second.shape[0]
    blocks, steps, wide = rows * cols, rows * cols * slots // QUAD, QUAD * LANES
    spans = min(rows, 3)
    vmem = pl.BlockSpec(memory_space=pltpu.VMEM)
    hbm = pl.BlockSpec(memory_space=pltpu.HBM)
    sds = jax.ShapeDtypeStruct
    call = vmem_call(
        functools.partial(prepare_kernel, rows, cols, slots),
        "prepare",
        [vmem] + [hbm] * 5,
        [
            sds((steps, LANES, wide), BF16),
            sds((blocks, slots, LANES), F32),
            sds((2 * hidden, 8 * basis), BF16),
            sds((weights, 3 * hidden), BF16),
            sds((units, 3 * reads), BF16),
            sds((reads, 3 * units), BF16),
            sds((units, 1), F32),
            sds((steps, feats, wide), BF16),
        ],
        [
            pltpu.VMEM(neighbours.shape, jnp.int32),
            pltpu.VMEM((basis, hidden), F32),
            pltpu.VMEM((hidden, weights), F32),
            pltpu.VMEM((reads, units), F32),
            pltpu.VMEM((1, units), F32),
            pltpu.VMEM((blocks, slots, LANES), F32),
            pltpu.VMEM((blocks, feats, spans * LANES), BF16),
            pltpu.VMEM((spans * LANES, wide), BF16),
            pltpu.VMEM((spans * LANES, wide), BF16),
            pltpu.SemaphoreType.DMA((5,)),
        ],
        16,
        2 * feats * spans * LANES * steps * wide,
    )
    return call(
        own, *pinned(neighbours, w_first.T, w_second.T, w_read.T, w_out.reshape(1, units))
    )


def pack_part(features, pos):
    rows, cols, feats, _ = features.shape
    vmem = pl.BlockSpec(memory_space=pltpu.VMEM)
    hbm = pl.BlockSpec(memory_space=pltpu.HBM)
    call = vmem_call(
        functools.partial(pack_kernel, rows, cols),
        "pack",
        [hbm] * 2,
        [jax.ShapeDtypeStruct((rows, cols, feats + 16, LANES), BF16)],
        [pltpu.VMEM(pos.shape, F32), pltpu.SemaphoreType.DMA((1 + rows * cols,))],
        2,
        1000000,
    )
    return call(*pinned(features, pos))[0]


def ends_part(left, right):
    vmem = pl.BlockSpec(memory_space=pltpu.VMEM)
    message = jax.ShapeDtypeStruct((left.shape[2], 2 * LANES), BF16)
    call = vmem_call(
        functools.partial(ends_kernel, left.shape[0]),
        "ends",
        [vmem] * 2,
        [message] * 2,
        [],
        2,
        1000000,
    )
    return call(left, right)


def ghost_part(before, after, near, place, xa, rows, cols):
    vmem = pl.BlockSpec(memory_space=pltpu.VMEM)
    steps, feats, wide = xa.shape
    call = vmem_call(
        functools.partial(ghost_kernel, rows, cols),
        "ghost",
        [vmem] * 5,
        [jax.ShapeDtypeStruct(xa.shape, BF16)],
        [],
        8,
        2 * feats * LANES * steps * wide,
    )
    return call(before, after, near, place, xa)[0]


def finish_part(front, force, ahead, vel, pos, fresh_pos, fresh_vel):
    vmem = pl.BlockSpec(memory_space=pltpu.VMEM)
    smem = pl.BlockSpec(memory_space=pltpu.SMEM)
    call = vmem_call(
        functools.partial(finish_kernel, vel.shape[0]),
        "finish",
        [smem] + [vmem] * 6,
        [jax.ShapeDtypeStruct(vel.shape, F32)] * 2,
        [],
        2,
        100000,
    )
    return call(front, force, ahead, vel, pos, fresh_pos, fresh_vel)


def local_part(left, right, own, near, place, xa):
    rows, cols, feats = own.shape[0], own.shape[1], xa.shape[1]
    steps, _, wide = near.shape
    most = 2 * min(rows, 3)
    vmem = pl.BlockSpec(memory_space=pltpu.VMEM)
    call = vmem_call(
        functools.partial(local_kernel, rows, cols),
        "local",
        [vmem] * 6,
        [jax.ShapeDtypeStruct((steps, feats, wide), BF16)],
        [
            pltpu.VMEM((rows * cols, feats, most * LANES), BF16),
            pltpu.VMEM((most * LANES, wide), BF16),
            pltpu.VMEM((most * LANES, wide), BF16),
        ],
        16,
        2 * feats * most * LANES * steps * wide,
    )
    return call(left, right, own, near, place, xa)[0]


def energy_part(ghosts, own, left, right, neighbours, counts, prepared, gathered):
    near, place, w1s, w2s, wrs, wrt, woc = prepared[:7]
    rows, cols, slots = neighbours.shape[0], neighbours.shape[1], neighbours.shape[2]
    steps, _, wide = near.shape
    weights = w2s.shape[0]
    channels, blocks, feats = weights // 3, rows * cols, gathered.shape[1]
    vmem = pl.BlockSpec(memory_space=pltpu.VMEM)
    hbm = pl.BlockSpec(memory_space=pltpu.HBM)
    sds = jax.ShapeDtypeStruct
    side = sds((rows + 2, 3, 1, LANES), F32)
    stream = blocks > 2
    half = steps // 2
    call = vmem_call(
        functools.partial(energy_kernel, rows, cols, channels, slots, stream=stream),
        "energy",
        [vmem] * 7 + [hbm] * 2 + [vmem] * 6 + [hbm if stream else vmem],
        [sds((rows, cols, 1, LANES), F32), side, sds((rows + 2, 3, cols, LANES), F32), side],
        [
            pltpu.VMEM((rows + 2, cols + 2, 3, LANES), F32),
            pltpu.VMEM((rows + 2, cols + 2, 3, LANES), F32),
            pltpu.VMEM((rows, cols, slots, LANES), jnp.int32),
            pltpu.VMEM((rows, cols, 1, LANES), jnp.int32),
            pltpu.VMEM((blocks, 8, slots, LANES), F32),
            pltpu.VMEM((blocks, 8, slots, LANES), F32),
            pltpu.VMEM((blocks, feats, 2 * LANES), BF16),
            pltpu.VMEM((RING, feats, wide) if stream else (1, 16, LANES), BF16),
            pltpu.VMEM((half, feats, wide), F32),
            pltpu.VMEM((half, feats, wide), F32),
            pltpu.VMEM((half, weights, wide), F32),
            pltpu.VMEM((half, weights, wide), F32),
            pltpu.VMEM((half, weights, wide), F32),
            pltpu.VMEM((half, weights, wide), F32),
            pltpu.VMEM((2, 3 * (w1s.shape[0] // 2), wide), BF16),
            pltpu.VMEM((2, 3 * (w1s.shape[0] // 2), wide), BF16),
            pltpu.VMEM((blocks, 9, channels, LANES), F32),
            pltpu.VMEM((weights, blocks * LANES), F32),
            pltpu.VMEM((blocks, 9, slots, LANES), F32),
            pltpu.VMEM((96, slots * LANES), BF16),
            pltpu.SemaphoreType.DMA((2,)),
            pltpu.SemaphoreType.DMA((RING,)),
        ],
        56 if stream else 32,
        2 * feats * 9 * LANES * steps * wide,
    )
    energies, f_left, f_own, f_right = call(
        *ghosts,
        own,
        left,
        right,
        *pinned(neighbours, counts.reshape(rows, cols, 1, LANES)),
        near,
        w1s,
        w2s,
        wrs,
        wrt,
        woc,
        gathered,
    )
    return f_left, f_own, f_right, energies.reshape(rows, cols, LANES)


def local(
    positions,
    velocities,
    features,
    neighbours,
    counts,
    w_first,
    w_second,
    w_read,
    w_out,
    fresh_positions,
    fresh_velocities,
):
    nrows, ncols = (positions.shape[0], positions.shape[1])
    shock_place = lax.axis_index("shock")
    front = lax.axis_size("shock") - 1
    assert nrows >= 2 and neighbours.shape[2] % (2 * QUAD) == 0

    def sides(x, axis):
        last = lax.slice_in_dim(x, ncols - 1, ncols, axis=axis)
        first = lax.slice_in_dim(x, 0, 1, axis=axis)
        return shifted(last, "trans", 1), shifted(first, "trans", -1)

    pos = positions.transpose(0, 2, 1, 3)
    vel = velocities.transpose(0, 2, 1, 3)
    own = pack_part(features, pos)
    left, right = sides(own, 1)
    before = passed_along(own[nrows - 1 :], "shock", 1)
    after = passed_along(own[:1], "shock", -1)
    feats = features.shape[2]
    prepared = prepare_part(own, feats, neighbours, w_first, w_second, w_read, w_out)
    near, place, xa = prepared[0], prepared[1], prepared[7]
    xa = ghost_part(before, after, near, place, xa, nrows, ncols)
    left, right, xa = lax.optimization_barrier((left, right, xa))
    last, first = ends_part(left, right)
    ghosts = (
        passed_along(last, "shock", 1),
        passed_along(first, "shock", -1),
        before,
        after,
    )
    gathered = local_part(left, right, own, near, place, xa)
    f_left, f_own, f_right, energies = energy_part(
        ghosts, own, left, right, neighbours, counts, prepared, gathered
    )
    from_right = shifted(f_left, "trans", -1)
    from_left = shifted(f_right, "trans", 1)
    folded = f_own.at[:, :, ncols - 1].add(from_right[:, :, 0])
    folded = folded.at[:, :, 0].add(from_left[:, :, 0])
    packed = jnp.concatenate([folded[:2], vel[:1], pos[:1]], axis=0)
    ahead = passed_along(packed, "shock", -1)
    at_front = (shock_place == front).astype(jnp.int32).reshape(1)
    new_positions, new_velocities = finish_part(
        at_front,
        folded,
        ahead,
        vel,
        pos,
        fresh_positions.transpose(1, 0, 2),
        fresh_velocities.transpose(1, 0, 2),
    )
    return (energies, new_positions.transpose(0, 2, 1, 3), new_velocities.transpose(0, 2, 1, 3))


def solution(mesh):
    return jax.shard_map(
        local,
        mesh=mesh,
        in_specs=(
            P("shock", "trans", None, None),
            P("shock", "trans", None, None),
            P("shock", "trans", None, None),
            P("shock", "trans", None, None),
            P("shock", "trans", None),
            P(),
            P(),
            P(),
            P(),
            P("trans", None, None),
            P("trans", None, None),
        ),
        out_specs=(
            P("shock", "trans", None),
            P("shock", "trans", None, None),
            P("shock", "trans", None, None),
        ),
        check_vma=False,
    )
```
